32 devices in a mesh: crops: 2 (over x), dap: 16 (over z, y, core).
Axes of the slice: x: 2, y: 2, z: 4, core: 2. Of those that a mesh axis runs over, the one named last changes fastest.
Arguments:
- homolog_embedding: bfloat16 [64, 128, 256], P(('crops', 'dap')), parts along dimension 0, may hold values from -6 to 6
- coverage_indicator: int32 [64, 128], P(('crops', 'dap')), parts along dimension 0, may hold values from 0 to 1, as said below
- genuine_amino_flag: int32 [256], P('crops'), parts along dimension 0, may hold values 0 or 1
- couple_embedding: bfloat16 [256, 128, 128], P(('crops', 'dap')), parts along dimension 0, may hold values from -6 to 6
- pairing_entry_matrices: bfloat16 [256, 2, 32], replicated, may hold values from -0.375 to 0.375
- pairing_exit_matrix: bfloat16 [1024, 128], replicated, may hold values from -0.75 to 0.75
- trilateral_entry_matrices: bfloat16 [2, 128, 5, 128], replicated, may hold values from -0.5 to 0.5
- trilateral_exit_matrices: bfloat16 [2, 128, 128], replicated, may hold values from -0.5 to 0.5
Outputs:
- pair_out: bfloat16 [256, 128, 128], P(('crops', 'dap')), parts along dimension 0
The draws below stay inside these ranges and needn't reach their ends.
There are 2 independent parts, one for each index of `crops`. The reference program is written for one: setup_inputs(seed, part) draws one part's arguments, and reference() takes and returns one part's arrays. A program takes and returns all parts, laid end to end along the dimension named above; an argument that names none is the same for every part. Nothing has to cross between parts.
Inputs may be any that keep to these rules, and one draw needn't show every extreme that they name: `coverage_indicator`: row 0 is all ones (the query sequence); every other row is one run of ones over consecutive residues, zeros elsewhere.
All inputs are finite; a program needn't handle non-finite values.
Results may differ from the reference program's by a relative error of at most 0.0085.
Values may be sent and summed in bfloat16 or wider, within the bound.
No kernel may reach another device: no remote copies, remote signals or barrier semaphores. Data moves between devices by JAX's collectives and lax.ppermute only.
A program may use at most 128 MiB of HBM per device.

```python
import jax
import jax.numpy as jnp
from jax import lax

ALIGNED_FEATURES = 256
C = 128
HIDDEN_FEATURES = 32
LOCAL_PAIR_LINES = 8
AMINO_TOTAL = 128
HOMOLOG_NUMBER = 32
N_DAP = 16


def draw_coverage_indicator(key, part):
    key = jax.random.fold_in(key, 11)
    start_key, span_key = jax.random.split(key)
    run_starts = jax.random.randint(start_key, (HOMOLOG_NUMBER, 1), 0, AMINO_TOTAL)
    run_lengths = jax.random.randint(span_key, (HOMOLOG_NUMBER, 1), AMINO_TOTAL // 8 + 1, AMINO_TOTAL + 1)
    position = jnp.arange(AMINO_TOTAL, dtype=jnp.int32)[None, :]
    covered = (position >= run_starts) & (position < run_starts + run_lengths)
    covered = covered | (jnp.arange(HOMOLOG_NUMBER, dtype=jnp.int32)[:, None] == 0)
    return covered.astype(jnp.int32)


def place_ends(array, stream_key, least, top_value):
    dims = array.shape
    spot = [jax.random.randint(jax.random.fold_in(stream_key, axis), (), 0, dims[axis]) for axis in range(len(dims))]
    array = array.at[tuple(spot)].set(least)
    longest = dims.index(max(dims))
    spot[longest] = (spot[longest] + 1) % dims[longest]
    return array.at[tuple(spot)].set(top_value)


def shard_levels(own_key, extent, cuts, low, largest):
    level, own = 1.0, jax.random.fold_in(own_key, 6)
    for dim, shards_of in cuts:
        heights = jnp.exp(jax.random.uniform(jax.random.fold_in(own, dim), (shards_of,), jnp.float32, low / len(cuts), largest / len(cuts)))
        level = level * jnp.repeat(heights, extent[dim] // shards_of).reshape([-1 if axis == dim else 1 for axis in range(len(extent))])
    return level


def gaussian(own_key, dims, deviation, bound, shards=(), kind=jnp.bfloat16):
    gain = shard_levels(own_key, dims, shards, -0.22, 0.18) if shards else 1.0
    values = jax.random.normal(own_key, dims, jnp.float32) * deviation * gain
    return jnp.minimum(jnp.maximum(values, -bound), bound).astype(kind)


def setup_inputs(seed: int = 0, part: int = 0) -> dict:
    key_list = jax.random.split(jax.random.key(seed), 9)
    part_keys = jax.random.split(jax.random.fold_in(key_list[8], part), 9)
    return {
        "homolog_embedding": gaussian(part_keys[0], (HOMOLOG_NUMBER, AMINO_TOTAL, ALIGNED_FEATURES), 1.0, 6.0, ((0, 16),)),
        "coverage_indicator": draw_coverage_indicator(jax.random.fold_in(jax.random.fold_in(key_list[8], part), 71), part),
        "genuine_amino_flag": place_ends((jax.random.randint(part_keys[2], (AMINO_TOTAL,), 0, 4) < 3).astype(jnp.int32), jax.random.fold_in(part_keys[2], 1), 0, 1),
        "couple_embedding": gaussian(part_keys[3], (AMINO_TOTAL, AMINO_TOTAL, C), 1.0, 6.0, ((0, 16),)),
        "pairing_entry_matrices": gaussian(key_list[4], (ALIGNED_FEATURES, 2, HIDDEN_FEATURES), ALIGNED_FEATURES ** -0.5, 0.375),
        "pairing_exit_matrix": gaussian(key_list[5], (HIDDEN_FEATURES * HIDDEN_FEATURES, C), (4.0 / HIDDEN_FEATURES), 0.75),
        "trilateral_entry_matrices": gaussian(key_list[6], (2, C, 5, C), C ** -0.5, 0.5),
        "trilateral_exit_matrices": gaussian(key_list[7], (2, C, C), C ** -0.5, 0.5),
    }


def standardize_features(values, axis):
    average = lax.optimization_barrier(jnp.mean(values, axis=axis, keepdims=True))
    centered = values - average
    variance = lax.optimization_barrier(jnp.mean(centered * centered, axis=axis, keepdims=True))
    return centered * lax.rsqrt(variance + 1e-05)

def truncated_entries(values):
    return lax.optimization_barrier(values.astype(jnp.bfloat16)).astype(jnp.float32)

def triangle(pair_now, pair_mask, weights, out_weight, incoming):
    normalized = truncated_entries(standardize_features(pair_now.astype(jnp.float32), -1))
    weights = weights.astype(jnp.float32)
    projections = jnp.einsum('ijc,ckh->khij', normalized, weights[:, :4])
    left_proj = truncated_entries(jax.nn.sigmoid(projections[0]) * projections[1] * pair_mask)
    right_proj = truncated_entries(jax.nn.sigmoid(projections[2]) * projections[3] * pair_mask)
    gate_val = jax.nn.sigmoid(jnp.einsum('ijc,ch->ijh', normalized, weights[:, 4]))
    if incoming:
        products = jnp.einsum('hki,hkj->hij', left_proj, right_proj)
    else:
        products = jnp.einsum('hik,hjk->hij', left_proj, right_proj)
    products = truncated_entries(products)
    normed_products = truncated_entries(standardize_features(products, 0))
    pair_update = jnp.einsum('hij,hc->ijc', normed_products, out_weight.astype(jnp.float32))
    return (pair_now.astype(jnp.float32) + gate_val * pair_update).astype(jnp.bfloat16)

def reference(homolog_embedding, coverage_indicator, genuine_amino_flag, couple_embedding, pairing_entry_matrices, pairing_exit_matrix, trilateral_entry_matrices, trilateral_exit_matrices):
    sequence_mask = coverage_indicator.astype(jnp.float32)
    coverage_norm_factor = truncated_entries(standardize_features(homolog_embedding.astype(jnp.float32), -1))
    mapped_entries = jnp.einsum('rgl,loe->roeg', coverage_norm_factor, pairing_entry_matrices.astype(jnp.float32))
    mapped_entries = truncated_entries(mapped_entries * sequence_mask[:, None, None, :])
    first_homolog_embedding = mapped_entries[:, 0]
    second_homolog_embedding = mapped_entries[:, 1]
    out_weight = pairing_exit_matrix.astype(jnp.float32)

    def outer_rows(block_index):
        initial_line_index = block_index * LOCAL_PAIR_LINES
        first_factor_slab = lax.dynamic_slice_in_dim(first_homolog_embedding, initial_line_index, LOCAL_PAIR_LINES, 2)
        mask_block = lax.dynamic_slice_in_dim(sequence_mask, initial_line_index, LOCAL_PAIR_LINES, 1)
        tensor_accumulant = truncated_entries(jnp.einsum('rzp,rej->pjze', first_factor_slab, second_homolog_embedding))
        tensor_accumulant = tensor_accumulant.reshape(LOCAL_PAIR_LINES, AMINO_TOTAL, HIDDEN_FEATURES * HIDDEN_FEATURES)
        pair_update = jnp.einsum('ijf,fc->ijc', tensor_accumulant, out_weight)
        pair_count = jnp.einsum('si,sj->ij', mask_block, sequence_mask)
        pair_block = lax.dynamic_slice_in_dim(couple_embedding, initial_line_index, LOCAL_PAIR_LINES, 0).astype(jnp.float32)
        return (pair_block + pair_update / pair_count[:, :, None]).astype(jnp.bfloat16)
    pair_one = lax.map(outer_rows, jnp.arange(N_DAP, dtype=jnp.int32)).reshape(AMINO_TOTAL, AMINO_TOTAL, C)
    residues = genuine_amino_flag.astype(jnp.float32)
    pair_mask = residues[:, None] * residues[None, :]
    pair_two = triangle(pair_one, pair_mask, trilateral_entry_matrices[0], trilateral_exit_matrices[0], False)
    return triangle(pair_two, pair_mask, trilateral_entry_matrices[1], trilateral_exit_matrices[1], True)
```

```python
import jax
import jax.numpy as jnp
from jax import lax
from jax.sharding import PartitionSpec as P


def standardize_features(values, axis):
    average = jnp.mean(values, axis=axis, keepdims=True)
    centered = values - average
    variance = jnp.mean(centered * centered, axis=axis, keepdims=True)
    return centered * lax.rsqrt(variance + 1e-05)


def exchange(blocks):
    return lax.all_to_all(blocks, "dap", split_axis=0, concat_axis=0, tiled=True)


def outer_update(left_local, mask_local, right_cols, mask_cols, couple_embedding, pairing_exit_matrix):
    proj_width = left_local.shape[1]
    local_rows = left_local.shape[2]
    col_total = right_cols.shape[2]
    outer = jnp.einsum("rzp,rej->pjze", left_local, right_cols, preferred_element_type=jnp.float32)
    outer = outer.astype(jnp.bfloat16).reshape(local_rows, col_total, proj_width * proj_width)
    pair_update = jnp.einsum("ijf,fc->ijc", outer, pairing_exit_matrix, preferred_element_type=jnp.float32)
    pair_count = jnp.einsum("si,sj->ij", mask_local, mask_cols, preferred_element_type=jnp.float32)
    return (couple_embedding.astype(jnp.float32) + pair_update / pair_count[:, :, None]).astype(jnp.bfloat16)


def triangle(pair_now, row_mask, weights, out_weight, incoming, devices):
    rows, cols, channels = pair_now.shape
    part = channels // devices
    normalized = standardize_features(pair_now.astype(jnp.float32), -1).astype(jnp.bfloat16)
    projections = jnp.einsum("ijc,ckh->khij", normalized, weights[:, :4], preferred_element_type=jnp.float32)
    left_proj = (jax.nn.sigmoid(projections[0]) * projections[1] * row_mask).astype(jnp.bfloat16)
    right_proj = (jax.nn.sigmoid(projections[2]) * projections[3] * row_mask).astype(jnp.bfloat16)
    gate_val = jax.nn.sigmoid(
        jnp.einsum("ijc,ch->ijh", normalized, weights[:, 4], preferred_element_type=jnp.float32)
    )
    both = jnp.stack(
        [left_proj.reshape(devices, part, rows, cols), right_proj.reshape(devices, part, rows, cols)], axis=1
    )
    both = exchange(both)
    both = jnp.transpose(both, (1, 2, 0, 3, 4)).reshape(2, part, devices * rows, cols)
    einsum_form = "hki,hkj->hij" if incoming else "hik,hjk->hij"
    products = jnp.einsum(einsum_form, both[0], both[1], preferred_element_type=jnp.float32).astype(jnp.bfloat16)
    products = jnp.transpose(products.reshape(part, devices, rows, cols), (1, 0, 2, 3))
    returned = exchange(products).reshape(channels, rows, cols)
    normed_products = standardize_features(returned.astype(jnp.float32), 0).astype(jnp.bfloat16)
    pair_update = jnp.einsum("hij,hc->ijc", normed_products, out_weight, preferred_element_type=jnp.float32)
    return (pair_now.astype(jnp.float32) + gate_val * pair_update).astype(jnp.bfloat16)


def local(
    devices,
    homolog_embedding,
    coverage_indicator,
    genuine_amino_flag,
    couple_embedding,
    pairing_entry_matrices,
    pairing_exit_matrix,
    trilateral_entry_matrices,
    trilateral_exit_matrices,
):
    rows, cols, _ = couple_embedding.shape
    held = homolog_embedding.shape[0]
    width = pairing_entry_matrices.shape[2]
    sequence_mask = coverage_indicator.astype(jnp.float32)
    msa_norm = standardize_features(homolog_embedding.astype(jnp.float32), -1).astype(jnp.bfloat16)
    entries = jnp.einsum("rgl,loe->roeg", msa_norm, pairing_entry_matrices, preferred_element_type=jnp.float32)
    entries = (entries * sequence_mask[:, None, None, :]).astype(jnp.bfloat16)
    own = jnp.transpose(entries[:, 0].reshape(held, width, devices, rows), (2, 0, 1, 3))
    shared = jnp.concatenate([entries[:, 1].reshape(held, width * cols), sequence_mask.astype(jnp.bfloat16)], axis=1)
    packed = jnp.concatenate(
        [jnp.broadcast_to(shared[None], (devices,) + shared.shape), own.reshape(devices, held, width * rows)], axis=2
    )
    packed = exchange(packed).reshape(devices * held, -1)
    right_cols = packed[:, : width * cols].reshape(-1, width, cols)
    mask_cols = packed[:, width * cols : (width + 1) * cols]
    left_local = packed[:, (width + 1) * cols :].reshape(-1, width, rows)
    first_row = lax.axis_index("dap") * rows
    mask_local = lax.dynamic_slice_in_dim(mask_cols, first_row, rows, 1)
    pair_one = outer_update(left_local, mask_local, right_cols, mask_cols, couple_embedding, pairing_exit_matrix)
    residues = genuine_amino_flag.astype(jnp.float32)
    row_mask = lax.dynamic_slice_in_dim(residues, first_row, rows, 0)[:, None] * residues[None, :]
    pair_two = triangle(
        pair_one, row_mask, trilateral_entry_matrices[0], trilateral_exit_matrices[0], False, devices
    )
    return triangle(pair_two, row_mask, trilateral_entry_matrices[1], trilateral_exit_matrices[1], True, devices)


def solution(mesh):
    devices = mesh.shape["dap"]
    return jax.shard_map(
        lambda *arrays: local(devices, *arrays),
        mesh=mesh,
        in_specs=(
            P(("crops", "dap"), None, None),
            P(("crops", "dap"), None),
            P("crops"),
            P(("crops", "dap"), None, None),
            P(),
            P(),
            P(),
            P(),
        ),
        out_specs=P(("crops", "dap"), None, None),
        check_vma=False,
    )
```

```python
import functools

import jax
import jax.numpy as jnp
from jax import lax
from jax.experimental import pallas as pl
from jax.experimental.pallas import tpu as pltpu
from jax.sharding import PartitionSpec as P

F32 = jnp.float32
BF16 = jnp.bfloat16
EPS = 1e-05
LANES = 128
VMEM = pl.BlockSpec(memory_space=pltpu.VMEM)
SMEM = pl.BlockSpec(memory_space=pltpu.SMEM)
PARAMS = pltpu.CompilerParams(vmem_limit_bytes=40 * 1024 * 1024)


def dot(a, b, left=1, right=0):
    return lax.dot_general(a, b, (((left,), (right,)), ((), ())), preferred_element_type=F32)


def sigmoid(values):
    return 0.5 * jnp.tanh(0.5 * values) + 0.5


def norm(values, axis):
    size = values.shape[axis]
    average = jnp.sum(values, axis=axis, keepdims=True) * (1.0 / size)
    centered = values - average
    variance = jnp.sum(centered * centered, axis=axis, keepdims=True) * (1.0 / size)
    return (centered * lax.rsqrt(variance + EPS)).astype(BF16)


def standardize_features(values, axis):
    average = jnp.mean(values, axis=axis, keepdims=True)
    centered = values - average
    variance = jnp.mean(centered * centered, axis=axis, keepdims=True)
    return centered * lax.rsqrt(variance + 1e-05)


def exchange(blocks):
    return lax.all_to_all(blocks, "dap", split_axis=0, concat_axis=0, tiled=True)


def outer_update(left_local, mask_local, right_cols, mask_cols, couple_embedding, pairing_exit_matrix):
    proj_width = left_local.shape[1]
    local_rows = left_local.shape[2]
    col_total = right_cols.shape[2]
    outer = jnp.einsum("rzp,rej->pjze", left_local, right_cols, preferred_element_type=jnp.float32)
    outer = outer.astype(jnp.bfloat16).reshape(local_rows, col_total, proj_width * proj_width)
    pair_update = jnp.einsum("ijf,fc->ijc", outer, pairing_exit_matrix, preferred_element_type=jnp.float32)
    pair_count = jnp.einsum("si,sj->ij", mask_local, mask_cols, preferred_element_type=jnp.float32)
    return (couple_embedding.astype(jnp.float32) + pair_update / pair_count[:, :, None]).astype(jnp.bfloat16)


def triangle(pair_now, row_mask, weights, out_weight, incoming, devices):
    rows, cols, channels = pair_now.shape
    part = channels // devices
    normalized = standardize_features(pair_now.astype(jnp.float32), -1).astype(jnp.bfloat16)
    projections = jnp.einsum("ijc,ckh->khij", normalized, weights[:, :4], preferred_element_type=jnp.float32)
    left_proj = (jax.nn.sigmoid(projections[0]) * projections[1] * row_mask).astype(jnp.bfloat16)
    right_proj = (jax.nn.sigmoid(projections[2]) * projections[3] * row_mask).astype(jnp.bfloat16)
    gate_val = jax.nn.sigmoid(
        jnp.einsum("ijc,ch->ijh", normalized, weights[:, 4], preferred_element_type=jnp.float32)
    )
    both = jnp.stack(
        [left_proj.reshape(devices, part, rows, cols), right_proj.reshape(devices, part, rows, cols)], axis=1
    )
    both = exchange(both)
    both = jnp.transpose(both, (1, 2, 0, 3, 4)).reshape(2, part, devices * rows, cols)
    einsum_form = "hki,hkj->hij" if incoming else "hik,hjk->hij"
    products = jnp.einsum(einsum_form, both[0], both[1], preferred_element_type=jnp.float32).astype(jnp.bfloat16)
    products = jnp.transpose(products.reshape(part, devices, rows, cols), (1, 0, 2, 3))
    returned = exchange(products).reshape(channels, rows, cols)
    normed_products = standardize_features(returned.astype(jnp.float32), 0).astype(jnp.bfloat16)
    pair_update = jnp.einsum("hij,hc->ijc", normed_products, out_weight, preferred_element_type=jnp.float32)
    return (pair_now.astype(jnp.float32) + gate_val * pair_update).astype(jnp.bfloat16)


def local(
    devices,
    homolog_embedding,
    coverage_indicator,
    genuine_amino_flag,
    couple_embedding,
    pairing_entry_matrices,
    pairing_exit_matrix,
    trilateral_entry_matrices,
    trilateral_exit_matrices,
):
    rows, cols, _ = couple_embedding.shape
    held = homolog_embedding.shape[0]
    width = pairing_entry_matrices.shape[2]
    sequence_mask = coverage_indicator.astype(jnp.float32)
    msa_norm = standardize_features(homolog_embedding.astype(jnp.float32), -1).astype(jnp.bfloat16)
    entries = jnp.einsum("rgl,loe->roeg", msa_norm, pairing_entry_matrices, preferred_element_type=jnp.float32)
    entries = (entries * sequence_mask[:, None, None, :]).astype(jnp.bfloat16)
    own = jnp.transpose(entries[:, 0].reshape(held, width, devices, rows), (2, 0, 1, 3))
    shared = jnp.concatenate([entries[:, 1].reshape(held, width * cols), sequence_mask.astype(jnp.bfloat16)], axis=1)
    packed = jnp.concatenate(
        [jnp.broadcast_to(shared[None], (devices,) + shared.shape), own.reshape(devices, held, width * rows)], axis=2
    )
    packed = exchange(packed).reshape(devices * held, -1)
    right_cols = packed[:, : width * cols].reshape(-1, width, cols)
    mask_cols = packed[:, width * cols : (width + 1) * cols]
    left_local = packed[:, (width + 1) * cols :].reshape(-1, width, rows)
    first_row = lax.axis_index("dap") * rows
    mask_local = lax.dynamic_slice_in_dim(mask_cols, first_row, rows, 1)
    pair_one = outer_update(left_local, mask_local, right_cols, mask_cols, couple_embedding, pairing_exit_matrix)
    residues = genuine_amino_flag.astype(jnp.float32)
    row_mask = lax.dynamic_slice_in_dim(residues, first_row, rows, 0)[:, None] * residues[None, :]
    pair_two = triangle(
        pair_one, row_mask, trilateral_entry_matrices[0], trilateral_exit_matrices[0], False, devices
    )
    return triangle(pair_two, row_mask, trilateral_entry_matrices[1], trilateral_exit_matrices[1], True, devices)


def entry_kernel(x_ref, cover_ref, own_weight_ref, shared_weight_ref, out_ref):
    held, cols, _ = x_ref.shape
    width = shared_weight_ref.shape[0]
    devices = out_ref.shape[0]
    cover = cover_ref[...].astype(F32)
    columns = jnp.transpose(jnp.concatenate([cover, jnp.zeros((8 - held, cols), F32)], axis=0))
    own = jnp.zeros((cols, LANES), F32)
    marks = []
    for s in range(held):
        normalized = norm(x_ref[s].astype(F32), -1)
        shared = (dot(shared_weight_ref[...], normalized, 1, 1) * cover[s : s + 1]).astype(BF16)
        for peer in range(devices):
            out_ref[peer, s * width : (s + 1) * width, :] = shared
        own = own + dot(normalized, own_weight_ref[s]) * columns[:, s : s + 1]
        marks += [pltpu.roll(cover[s : s + 1], LANES // 2, 1), cover[s : s + 1]]
    marks = jnp.concatenate(marks + [jnp.zeros((8 - 2 * held, cols), F32)], axis=0)
    lane = lax.broadcasted_iota(jnp.int32, (8, LANES), 1)
    for peer in range(devices):
        block = jnp.where(lane < held * width, own[peer * 8 : peer * 8 + 8], marks)
        out_ref[peer, held * width :, :] = block.astype(BF16)


def project(pair_tile, weight_ref, mask_ref, out_ref, gate_ref, first, devices):
    cols = pair_tile.shape[1] // 2
    both = 2 * pair_tile.shape[0]
    normalized = norm(pair_tile, 0)
    mask = jnp.concatenate([mask_ref[first : first + 1], mask_ref[first + 1 : first + 2]], axis=1)
    gates = sigmoid(dot(weight_ref[0:both], normalized))
    values = dot(weight_ref[both : 2 * both], normalized)
    sides = (gates * values * mask).astype(BF16)
    gate_ref[:, first * cols : (first + 2) * cols] = sigmoid(dot(weight_ref[2 * both :], normalized))
    share = both // devices
    for peer in range(devices):
        for row in range(2):
            at = (first + row) * share
            out_ref[peer, at : at + share, :] = sides[peer * share : (peer + 1) * share, row * cols : (row + 1) * cols]


def outer_kernel(
    place_ref, got_ref, couple_ref, exit_ref, weight_ref, mask_ref,
    out_ref, pair_ref, gate_ref, shared_ref, aux_ref, outer_ref,
):
    devices, _, cols = got_ref.shape
    channels = couple_ref.shape[0]
    rows = mask_ref.shape[0]
    held, width = 2, 32
    shared_ref[...] = got_ref[:, : held * width, :].astype(F32).reshape(devices * held * width, cols)
    aux_ref[...] = got_ref[:, held * width :, :].astype(F32).reshape(devices * 8, cols)
    lane = lax.broadcasted_iota(jnp.int32, (devices, LANES), 1)
    cover = []
    for s in range(held):
        low = aux_ref[pl.ds(2 * s, devices, stride=8), :]
        high = aux_ref[pl.ds(2 * s + 1, devices, stride=8), :]
        cover.append(jnp.where(lane < LANES // 2, pltpu.roll(low, LANES // 2, 1), high))
    cover = jnp.concatenate(cover, axis=0).astype(BF16)
    chosen = lax.broadcasted_iota(jnp.int32, (rows, LANES), 1) == (
        lax.broadcasted_iota(jnp.int32, (rows, LANES), 0) + place_ref[0] * rows
    )
    cover_rows = dot(chosen.astype(BF16), cover, 1, 1).astype(BF16)
    scale = 1.0 / dot(cover_rows, cover)
    per_tile = LANES // width
    tiles = []
    for tile in range(rows // per_tile):
        sides = [jnp.zeros((devices, LANES), F32) for _ in range(held)]
        for place in range(per_tile):
            values = aux_ref[pl.ds(tile * per_tile + place, devices, stride=8), :]
            here = (lane >= place * width) & (lane < (place + 1) * width)
            for s in range(held):
                turn = ((place - s) * width) % LANES
                turned = pltpu.roll(values, turn, 1) if turn else values
                sides[s] = jnp.where(here, turned, sides[s])
        tiles.append(jnp.concatenate(sides, axis=0))
    own = jnp.transpose(jnp.concatenate(tiles, axis=1)).astype(BF16)
    for e in range(0, width, 2):
        parts = []
        for step in range(2):
            parts.append(
                jnp.concatenate(
                    [
                        shared_ref[pl.ds(s * width + e + step, devices, stride=held * width), :]
                        for s in range(held)
                    ],
                    axis=0,
                )
            )
        result = dot(own, jnp.concatenate(parts, axis=1).astype(BF16)).astype(BF16)
        for step in range(2):
            for i in range(rows):
                outer_ref[(e + step) * width : (e + step + 1) * width, i * cols : (i + 1) * cols] = result[
                    i * width : (i + 1) * width, step * cols : (step + 1) * cols
                ]
    for first in range(0, rows, 2):
        at = slice(first * cols, (first + 2) * cols)
        update = dot(exit_ref[...], outer_ref[:, at])
        per_pair = jnp.concatenate([scale[first : first + 1], scale[first + 1 : first + 2]], axis=1)
        pair = (couple_ref[:, at].astype(F32) + update * per_pair).astype(BF16)
        pair_ref[:, at] = pair
        project(pair.astype(F32), weight_ref, mask_ref, out_ref, gate_ref, first, devices)


def product_kernel(incoming, got_ref, out_ref, sides_ref, products_ref):
    devices, _, cols = got_ref.shape
    part = 8
    total = sides_ref.shape[0] // (2 * part)
    sides_ref[...] = got_ref[...].astype(F32).reshape(total * 2 * part, cols)
    for h in range(part):
        left = sides_ref[pl.ds(h, total, stride=2 * part), :].astype(BF16)
        right = sides_ref[pl.ds(part + h, total, stride=2 * part), :].astype(BF16)
        result = dot(left, right, 0, 0) if incoming else dot(left, right, 1, 1)
        products_ref[pl.ds(h, total, stride=part), :] = result
    out_ref[...] = products_ref[...].astype(BF16).reshape(out_ref.shape)


def updated(got_ref, pair_ref, gate_ref, exit_ref, first):
    devices, _, cols = got_ref.shape
    part = 8
    channels = devices * part
    got = got_ref[:, first * part : (first + 2) * part, :].astype(F32)
    products = jnp.concatenate(
        [got[:, :part].reshape(channels, cols), got[:, part:].reshape(channels, cols)], axis=1
    )
    at = slice(first * cols, (first + 2) * cols)
    update = dot(exit_ref[...], norm(products, 0))
    return pair_ref[:, at].astype(F32) + gate_ref[:, at] * update


def middle_kernel(got_ref, pair_ref, gate_ref, exit_ref, weight_ref, mask_ref, out_ref, next_ref, next_gate_ref):
    devices, _, cols = got_ref.shape
    for first in range(0, mask_ref.shape[0], 2):
        pair = updated(got_ref, pair_ref, gate_ref, exit_ref, first).astype(BF16)
        next_ref[:, first * cols : (first + 2) * cols] = pair
        project(pair.astype(F32), weight_ref, mask_ref, out_ref, next_gate_ref, first, devices)


def last_kernel(got_ref, pair_ref, gate_ref, exit_ref, out_ref):
    rows, cols, _ = out_ref.shape
    for first in range(0, rows, 2):
        pair = updated(got_ref, pair_ref, gate_ref, exit_ref, first)
        for row in range(2):
            out_ref[first + row] = jnp.transpose(pair[:, row * cols : (row + 1) * cols]).astype(BF16)


def call(kernel, inputs, outputs, scratch=(), in_specs=None):
    return pl.pallas_call(
        kernel,
        out_shape=outputs,
        in_specs=in_specs or [VMEM] * len(inputs),
        out_specs=[VMEM] * len(outputs),
        scratch_shapes=list(scratch),
        compiler_params=PARAMS,
    )(*inputs)


def shape(dims, kind=BF16):
    return jax.ShapeDtypeStruct(dims, kind)


def fast(
    devices,
    homolog_embedding,
    coverage_indicator,
    genuine_amino_flag,
    couple_embedding,
    pairing_entry_matrices,
    pairing_exit_matrix,
    trilateral_entry_matrices,
    trilateral_exit_matrices,
):
    rows, cols, channels = couple_embedding.shape
    held = homolog_embedding.shape[0]
    width = pairing_entry_matrices.shape[2]
    part = channels // devices
    blank = jnp.zeros_like(pairing_entry_matrices[:, 0])
    own_weight = jnp.stack(
        [
            jnp.concatenate([pairing_entry_matrices[:, 0] if at == s else blank for at in range(LANES // width)], axis=1)
            for s in range(held)
        ]
    )
    shared_weight = jnp.transpose(pairing_entry_matrices[:, 1])
    (packed,) = call(
        entry_kernel,
        (homolog_embedding, coverage_indicator, own_weight, shared_weight),
        [shape((devices, held * width + 8, cols))],
    )
    packed, entry, leave, exit_weight, couple, residues = lax.optimization_barrier(
        (
            packed,
            trilateral_entry_matrices,
            trilateral_exit_matrices,
            pairing_exit_matrix,
            couple_embedding,
            genuine_amino_flag,
        )
    )
    got = exchange(packed)
    place = lax.axis_index("dap")
    residues = residues.astype(F32)
    row_mask = lax.dynamic_slice_in_dim(residues, place * rows, rows, 0)[:, None] * residues[None, :]
    sides = entry[:, :, :4].reshape(2, channels, 2, 2, devices, part)
    sides = jnp.transpose(sides, (0, 3, 4, 2, 5, 1)).reshape(2, 4 * channels, channels)
    entry = jnp.concatenate([sides, jnp.transpose(entry[:, :, 4], (0, 2, 1))], axis=1)
    leave = jnp.transpose(leave, (0, 2, 1))
    exit_weight = jnp.transpose(exit_weight.reshape(width, width, channels), (2, 1, 0)).reshape(channels, width * width)
    couple = jnp.transpose(couple, (2, 0, 1)).reshape(channels, rows * cols)

    projected = [
        shape((devices, rows * 2 * part, cols)),
        shape((channels, rows * cols)),
        shape((channels, rows * cols), F32),
    ]
    both, pair, gate = call(
        outer_kernel,
        (place.astype(jnp.int32).reshape(1), got, couple, exit_weight, entry[0], row_mask),
        projected,
        [
            pltpu.VMEM((devices * held * width, cols), F32),
            pltpu.VMEM((devices * 8, cols), F32),
            pltpu.VMEM((width * width, rows * cols), BF16),
        ],
        [SMEM] + [VMEM] * 5,
    )

    def multiply(both, incoming):
        (products,) = call(
            functools.partial(product_kernel, incoming),
            (exchange(both),),
            [shape((devices, rows * part, cols))],
            [pltpu.VMEM((devices * rows * 2 * part, cols), F32), pltpu.VMEM((devices * rows * part, cols), F32)],
        )
        return exchange(products)

    got = multiply(both, False)
    both, pair, gate = call(middle_kernel, (got, pair, gate, leave[0], entry[1], row_mask), projected)
    got = multiply(both, True)
    (pair_out,) = call(last_kernel, (got, pair, gate, leave[1]), [shape((rows, cols, channels))])
    return pair_out


def fits(devices, homolog_embedding, couple_embedding, pairing_entry_matrices):
    rows, cols, channels = couple_embedding.shape
    return (
        homolog_embedding.shape[0] == 2
        and rows == 8
        and cols == LANES
        and channels == 8 * devices
        and channels == LANES
        and pairing_entry_matrices.shape[2] == 32
    )


def solution(mesh):
    devices = mesh.shape["dap"]

    def one_device(*arrays):
        chosen = fast if fits(devices, arrays[0], arrays[3], arrays[4]) else local
        return chosen(devices, *arrays)

    return jax.shard_map(
        one_device,
        mesh=mesh,
        in_specs=(
            P(("crops", "dap"), None, None),
            P(("crops", "dap"), None),
            P("crops"),
            P(("crops", "dap"), None, None),
            P(),
            P(),
            P(),
            P(),
        ),
        out_specs=P(("crops", "dap"), None, None),
        check_vma=False,
    )
```

```python
import functools

import jax
import jax.numpy as jnp
from jax import lax
from jax.experimental import pallas as pl
from jax.experimental.pallas import tpu as pltpu
from jax.sharding import PartitionSpec as P

F32 = jnp.float32
BF16 = jnp.bfloat16
EPS = 1e-05
LANES = 128
VMEM = pl.BlockSpec(memory_space=pltpu.VMEM)
SMEM = pl.BlockSpec(memory_space=pltpu.SMEM)
PARAMS = pltpu.CompilerParams(vmem_limit_bytes=40 * 1024 * 1024)


def dot(a, b, left=1, right=0):
    return lax.dot_general(a, b, (((left,), (right,)), ((), ())), preferred_element_type=F32)


def sigmoid(values):
    return 0.5 * jnp.tanh(0.5 * values) + 0.5


def norm(values, axis):
    size = values.shape[axis]
    average = jnp.sum(values, axis=axis, keepdims=True) * (1.0 / size)
    centered = values - average
    variance = jnp.sum(centered * centered, axis=axis, keepdims=True) * (1.0 / size)
    return (centered * lax.rsqrt(variance + EPS)).astype(BF16)


def standardize_features(values, axis):
    average = jnp.mean(values, axis=axis, keepdims=True)
    centered = values - average
    variance = jnp.mean(centered * centered, axis=axis, keepdims=True)
    return centered * lax.rsqrt(variance + 1e-05)


def exchange(blocks):
    return lax.all_to_all(blocks, "dap", split_axis=0, concat_axis=0, tiled=True)


def outer_update(left_local, mask_local, right_cols, mask_cols, couple_embedding, pairing_exit_matrix):
    proj_width = left_local.shape[1]
    local_rows = left_local.shape[2]
    col_total = right_cols.shape[2]
    outer = jnp.einsum("rzp,rej->pjze", left_local, right_cols, preferred_element_type=jnp.float32)
    outer = outer.astype(jnp.bfloat16).reshape(local_rows, col_total, proj_width * proj_width)
    pair_update = jnp.einsum("ijf,fc->ijc", outer, pairing_exit_matrix, preferred_element_type=jnp.float32)
    pair_count = jnp.einsum("si,sj->ij", mask_local, mask_cols, preferred_element_type=jnp.float32)
    return (couple_embedding.astype(jnp.float32) + pair_update / pair_count[:, :, None]).astype(jnp.bfloat16)


def triangle(pair_now, row_mask, weights, out_weight, incoming, devices):
    rows, cols, channels = pair_now.shape
    part = channels // devices
    normalized = standardize_features(pair_now.astype(jnp.float32), -1).astype(jnp.bfloat16)
    projections = jnp.einsum("ijc,ckh->khij", normalized, weights[:, :4], preferred_element_type=jnp.float32)
    left_proj = (jax.nn.sigmoid(projections[0]) * projections[1] * row_mask).astype(jnp.bfloat16)
    right_proj = (jax.nn.sigmoid(projections[2]) * projections[3] * row_mask).astype(jnp.bfloat16)
    gate_val = jax.nn.sigmoid(
        jnp.einsum("ijc,ch->ijh", normalized, weights[:, 4], preferred_element_type=jnp.float32)
    )
    both = jnp.stack(
        [left_proj.reshape(devices, part, rows, cols), right_proj.reshape(devices, part, rows, cols)], axis=1
    )
    both = exchange(both)
    both = jnp.transpose(both, (1, 2, 0, 3, 4)).reshape(2, part, devices * rows, cols)
    einsum_form = "hki,hkj->hij" if incoming else "hik,hjk->hij"
    products = jnp.einsum(einsum_form, both[0], both[1], preferred_element_type=jnp.float32).astype(jnp.bfloat16)
    products = jnp.transpose(products.reshape(part, devices, rows, cols), (1, 0, 2, 3))
    returned = exchange(products).reshape(channels, rows, cols)
    normed_products = standardize_features(returned.astype(jnp.float32), 0).astype(jnp.bfloat16)
    pair_update = jnp.einsum("hij,hc->ijc", normed_products, out_weight, preferred_element_type=jnp.float32)
    return (pair_now.astype(jnp.float32) + gate_val * pair_update).astype(jnp.bfloat16)


def local(
    devices,
    homolog_embedding,
    coverage_indicator,
    genuine_amino_flag,
    couple_embedding,
    pairing_entry_matrices,
    pairing_exit_matrix,
    trilateral_entry_matrices,
    trilateral_exit_matrices,
):
    rows, cols, _ = couple_embedding.shape
    held = homolog_embedding.shape[0]
    width = pairing_entry_matrices.shape[2]
    sequence_mask = coverage_indicator.astype(jnp.float32)
    msa_norm = standardize_features(homolog_embedding.astype(jnp.float32), -1).astype(jnp.bfloat16)
    entries = jnp.einsum("rgl,loe->roeg", msa_norm, pairing_entry_matrices, preferred_element_type=jnp.float32)
    entries = (entries * sequence_mask[:, None, None, :]).astype(jnp.bfloat16)
    own = jnp.transpose(entries[:, 0].reshape(held, width, devices, rows), (2, 0, 1, 3))
    shared = jnp.concatenate([entries[:, 1].reshape(held, width * cols), sequence_mask.astype(jnp.bfloat16)], axis=1)
    packed = jnp.concatenate(
        [jnp.broadcast_to(shared[None], (devices,) + shared.shape), own.reshape(devices, held, width * rows)], axis=2
    )
    packed = exchange(packed).reshape(devices * held, -1)
    right_cols = packed[:, : width * cols].reshape(-1, width, cols)
    mask_cols = packed[:, width * cols : (width + 1) * cols]
    left_local = packed[:, (width + 1) * cols :].reshape(-1, width, rows)
    first_row = lax.axis_index("dap") * rows
    mask_local = lax.dynamic_slice_in_dim(mask_cols, first_row, rows, 1)
    pair_one = outer_update(left_local, mask_local, right_cols, mask_cols, couple_embedding, pairing_exit_matrix)
    residues = genuine_amino_flag.astype(jnp.float32)
    row_mask = lax.dynamic_slice_in_dim(residues, first_row, rows, 0)[:, None] * residues[None, :]
    pair_two = triangle(
        pair_one, row_mask, trilateral_entry_matrices[0], trilateral_exit_matrices[0], False, devices
    )
    return triangle(pair_two, row_mask, trilateral_entry_matrices[1], trilateral_exit_matrices[1], True, devices)


def entry_kernel(x_ref, cover_ref, weight_ref, out_ref):
    held, cols, _ = x_ref.shape
    width = weight_ref.shape[1]
    devices = out_ref.shape[0]
    cover = cover_ref[...].astype(F32)
    columns = jnp.transpose(jnp.concatenate([cover, jnp.zeros((8 - held, cols), F32)], axis=0))
    blank = jnp.zeros_like(weight_ref[0])
    own = jnp.zeros((cols, LANES), F32)
    marks = []
    for s in range(held):
        normalized = norm(x_ref[s].astype(F32), -1)
        shared = (dot(weight_ref[1], normalized, 1, 1) * cover[s : s + 1]).astype(BF16)
        for peer in range(devices):
            out_ref[peer, s * width : (s + 1) * width, :] = shared
        weight = jnp.concatenate([weight_ref[0] if at == s else blank for at in range(LANES // width)], axis=0)
        own = own + dot(normalized, weight, 1, 1) * columns[:, s : s + 1]
        marks += [pltpu.roll(cover[s : s + 1], LANES // 2, 1), cover[s : s + 1]]
    marks = jnp.concatenate(marks + [jnp.zeros((8 - 2 * held, cols), F32)], axis=0)
    lane = lax.broadcasted_iota(jnp.int32, (8, LANES), 1)
    for peer in range(devices):
        block = jnp.where(lane < held * width, own[peer * 8 : peer * 8 + 8], marks)
        out_ref[peer, held * width :, :] = block.astype(BF16)


def project(pair_tile, weights, mask_ref, out_ref, gate_ref, first, devices):
    cols = pair_tile.shape[1] // 2
    share = pair_tile.shape[0] // devices
    normalized = norm(pair_tile, 0)
    mask = jnp.concatenate([mask_ref[first : first + 1], mask_ref[first + 1 : first + 2]], axis=1)
    left, right = (
        sigmoid(dot(weights[k], normalized)) * dot(weights[k + 1], normalized) * mask for k in (0, 2)
    )
    gate_ref[:, first * cols : (first + 2) * cols] = sigmoid(dot(weights[4], normalized))
    for peer in range(devices):
        for row in range(2):
            block = [
                side[peer * share : (peer + 1) * share, row * cols : (row + 1) * cols] for side in (left, right)
            ]
            at = (first + row) * 2 * share
            out_ref[peer, at : at + 2 * share, :] = jnp.concatenate(block, axis=0).astype(BF16)


def turned(weight_ref, t):
    return [jnp.transpose(weight_ref[t, k]) for k in range(weight_ref.shape[1])]


def outer_kernel(
    place_ref, got_ref, couple_ref, exit_ref, weight_ref, flag_ref,
    out_ref, pair_ref, gate_ref, mask_ref, shared_ref, aux_ref, outer_ref,
):
    devices, _, cols = got_ref.shape
    rows, _, channels = couple_ref.shape
    held, width = 2, 32
    shared_ref[...] = got_ref[:, : held * width, :].astype(F32).reshape(devices * held * width, cols)
    aux_ref[...] = got_ref[:, held * width :, :].astype(F32).reshape(devices * 8, cols)
    lane = lax.broadcasted_iota(jnp.int32, (devices, LANES), 1)
    cover = []
    for s in range(held):
        low = aux_ref[pl.ds(2 * s, devices, stride=8), :]
        high = aux_ref[pl.ds(2 * s + 1, devices, stride=8), :]
        cover.append(jnp.where(lane < LANES // 2, pltpu.roll(low, LANES // 2, 1), high))
    cover = jnp.concatenate(cover, axis=0).astype(BF16)
    chosen = lax.broadcasted_iota(jnp.int32, (rows, LANES), 1) == (
        lax.broadcasted_iota(jnp.int32, (rows, LANES), 0) + place_ref[0] * rows
    )
    cover_rows = dot(chosen.astype(BF16), cover, 1, 1).astype(BF16)
    scale = 1.0 / dot(cover_rows, cover)
    flags = flag_ref[...].astype(F32)
    mask_ref[...] = jnp.sum(jnp.where(chosen, flags, 0.0), axis=1, keepdims=True) * flags
    per_tile = LANES // width
    tiles = []
    for tile in range(rows // per_tile):
        sides = [jnp.zeros((devices, LANES), F32) for _ in range(held)]
        for place in range(per_tile):
            values = aux_ref[pl.ds(tile * per_tile + place, devices, stride=8), :]
            here = (lane >= place * width) & (lane < (place + 1) * width)
            for s in range(held):
                turn = ((place - s) * width) % LANES
                moved = pltpu.roll(values, turn, 1) if turn else values
                sides[s] = jnp.where(here, moved, sides[s])
        tiles.append(jnp.concatenate(sides, axis=0))
    own = jnp.transpose(jnp.concatenate(tiles, axis=1)).astype(BF16)
    for e in range(0, width, 2):
        parts = []
        for step in range(2):
            parts.append(
                jnp.concatenate(
                    [
                        shared_ref[pl.ds(s * width + e + step, devices, stride=held * width), :]
                        for s in range(held)
                    ],
                    axis=0,
                )
            )
        result = dot(own, jnp.concatenate(parts, axis=1).astype(BF16)).astype(BF16)
        for step in range(2):
            for i in range(rows):
                outer_ref[(e + step) * width : (e + step + 1) * width, i * cols : (i + 1) * cols] = result[
                    i * width : (i + 1) * width, step * cols : (step + 1) * cols
                ]
    shared_ref[...] = exit_ref[...].astype(F32)
    leave = jnp.concatenate([shared_ref[pl.ds(e, width, stride=width), :] for e in range(width)], axis=0)
    leave = jnp.transpose(leave.astype(BF16))
    weights = turned(weight_ref, 0)
    for first in range(0, rows, 2):
        at = slice(first * cols, (first + 2) * cols)
        update = dot(leave, outer_ref[:, at])
        per_pair = jnp.concatenate([scale[first : first + 1], scale[first + 1 : first + 2]], axis=1)
        couple = jnp.concatenate([jnp.transpose(couple_ref[first + row].astype(F32)) for row in range(2)], axis=1)
        pair = (couple + update * per_pair).astype(BF16)
        pair_ref[:, at] = pair
        project(pair.astype(F32), weights, mask_ref, out_ref, gate_ref, first, devices)


def product_kernel(incoming, got_ref, out_ref, sides_ref, products_ref):
    devices, _, cols = got_ref.shape
    part = 8
    total = sides_ref.shape[0] // (2 * part)
    sides_ref[...] = got_ref[...].astype(F32).reshape(total * 2 * part, cols)
    for h in range(part):
        left = sides_ref[pl.ds(h, total, stride=2 * part), :].astype(BF16)
        right = sides_ref[pl.ds(part + h, total, stride=2 * part), :].astype(BF16)
        result = dot(left, right, 0, 0) if incoming else dot(left, right, 1, 1)
        products_ref[pl.ds(h, total, stride=part), :] = result
    out_ref[...] = products_ref[...].astype(BF16).reshape(out_ref.shape)


def updated(got_ref, pair_ref, gate_ref, leave, first):
    devices, _, cols = got_ref.shape
    part = 8
    channels = devices * part
    got = got_ref[:, first * part : (first + 2) * part, :].astype(F32)
    products = jnp.concatenate(
        [got[:, :part].reshape(channels, cols), got[:, part:].reshape(channels, cols)], axis=1
    )
    at = slice(first * cols, (first + 2) * cols)
    update = dot(leave, norm(products, 0))
    return pair_ref[:, at].astype(F32) + gate_ref[:, at] * update


def middle_kernel(got_ref, pair_ref, gate_ref, leave_ref, weight_ref, mask_ref, out_ref, next_ref, next_gate_ref):
    devices, _, cols = got_ref.shape
    leave = jnp.transpose(leave_ref[0])
    weights = turned(weight_ref, 1)
    for first in range(0, mask_ref.shape[0], 2):
        pair = updated(got_ref, pair_ref, gate_ref, leave, first).astype(BF16)
        next_ref[:, first * cols : (first + 2) * cols] = pair
        project(pair.astype(F32), weights, mask_ref, out_ref, next_gate_ref, first, devices)


def last_kernel(got_ref, pair_ref, gate_ref, leave_ref, out_ref):
    rows, cols, _ = out_ref.shape
    leave = jnp.transpose(leave_ref[1])
    for first in range(0, rows, 2):
        pair = updated(got_ref, pair_ref, gate_ref, leave, first)
        for row in range(2):
            out_ref[first + row] = jnp.transpose(pair[:, row * cols : (row + 1) * cols]).astype(BF16)


def call(kernel, inputs, outputs, scratch=(), in_specs=None):
    return pl.pallas_call(
        kernel,
        out_shape=outputs,
        in_specs=in_specs or [VMEM] * len(inputs),
        out_specs=[VMEM] * len(outputs),
        scratch_shapes=list(scratch),
        compiler_params=PARAMS,
    )(*inputs)


def shape(dims, kind=BF16):
    return jax.ShapeDtypeStruct(dims, kind)


def fast(
    devices,
    homolog_embedding,
    coverage_indicator,
    genuine_amino_flag,
    couple_embedding,
    pairing_entry_matrices,
    pairing_exit_matrix,
    trilateral_entry_matrices,
    trilateral_exit_matrices,
):
    rows, cols, channels = couple_embedding.shape
    held = homolog_embedding.shape[0]
    width = pairing_entry_matrices.shape[2]
    part = channels // devices
    (packed,) = call(
        entry_kernel,
        (homolog_embedding, coverage_indicator, jnp.transpose(pairing_entry_matrices, (1, 2, 0))),
        [shape((devices, held * width + 8, cols))],
    )
    entry = jnp.transpose(trilateral_entry_matrices, (0, 2, 1, 3))
    leave = trilateral_exit_matrices
    projected = [
        shape((devices, rows * 2 * part, cols)),
        shape((channels, rows * cols)),
        shape((channels, rows * cols), F32),
    ]
    both, pair, gate, row_mask = call(
        outer_kernel,
        (
            lax.axis_index("dap").astype(jnp.int32).reshape(1),
            exchange(packed),
            couple_embedding,
            pairing_exit_matrix,
            entry,
            genuine_amino_flag.reshape(1, cols),
        ),
        projected + [shape((rows, cols), F32)],
        [
            pltpu.VMEM((devices * held * width, cols), F32),
            pltpu.VMEM((devices * 8, cols), F32),
            pltpu.VMEM((width * width, rows * cols), BF16),
        ],
        [SMEM] + [VMEM] * 5,
    )

    def multiply(both, incoming):
        (products,) = call(
            functools.partial(product_kernel, incoming),
            (exchange(both),),
            [shape((devices, rows * part, cols))],
            [pltpu.VMEM((devices * rows * 2 * part, cols), F32), pltpu.VMEM((devices * rows * part, cols), F32)],
        )
        return exchange(products)

    got = multiply(both, False)
    both, pair, gate = call(middle_kernel, (got, pair, gate, leave, entry, row_mask), projected)
    got = multiply(both, True)
    (pair_out,) = call(last_kernel, (got, pair, gate, leave), [shape((rows, cols, channels))])
    return pair_out


def fits(devices, homolog_embedding, couple_embedding, pairing_entry_matrices):
    rows, cols, channels = couple_embedding.shape
    return (
        homolog_embedding.shape[0] == 2
        and rows == 8
        and cols == LANES
        and channels == 8 * devices
        and channels == LANES
        and pairing_entry_matrices.shape[2] == 32
    )


def solution(mesh):
    devices = mesh.shape["dap"]

    def one_device(*arrays):
        chosen = fast if fits(devices, arrays[0], arrays[3], arrays[4]) else local
        return chosen(devices, *arrays)

    return jax.shard_map(
        one_device,
        mesh=mesh,
        in_specs=(
            P(("crops", "dap"), None, None),
            P(("crops", "dap"), None),
            P("crops"),
            P(("crops", "dap"), None, None),
            P(),
            P(),
            P(),
            P(),
        ),
        out_specs=P(("crops", "dap"), None, None),
        check_vma=False,
    )
```

```python
import functools

import jax
import jax.numpy as jnp
from jax import lax
from jax.experimental import pallas as pl
from jax.experimental.pallas import tpu as pltpu
from jax.sharding import PartitionSpec as P

F32 = jnp.float32
BF16 = jnp.bfloat16
EPS = 1e-05
LANES = 128
VMEM = pl.BlockSpec(memory_space=pltpu.VMEM)
HBM = pl.BlockSpec(memory_space=pltpu.HBM)


def dot(a, b, left=1, right=0):
    return lax.dot_general(a, b, (((left,), (right,)), ((), ())), preferred_element_type=F32)


def sigmoid(values):
    return 0.5 * jnp.tanh(0.5 * values) + 0.5


def norm(values, axis):
    size = values.shape[axis]
    average = jnp.sum(values, axis=axis, keepdims=True) * (1.0 / size)
    centered = values - average
    variance = jnp.sum(centered * centered, axis=axis, keepdims=True) * (1.0 / size)
    return (centered * lax.rsqrt(variance + EPS)).astype(BF16)


def standardize_features(values, axis):
    average = jnp.mean(values, axis=axis, keepdims=True)
    centered = values - average
    variance = jnp.mean(centered * centered, axis=axis, keepdims=True)
    return centered * lax.rsqrt(variance + 1e-05)


def exchange(blocks):
    return lax.all_to_all(blocks, "dap", split_axis=0, concat_axis=0, tiled=True)


def outer_update(left_local, mask_local, right_cols, mask_cols, couple_embedding, pairing_exit_matrix):
    proj_width = left_local.shape[1]
    local_rows = left_local.shape[2]
    col_total = right_cols.shape[2]
    outer = jnp.einsum("rzp,rej->pjze", left_local, right_cols, preferred_element_type=jnp.float32)
    outer = outer.astype(jnp.bfloat16).reshape(local_rows, col_total, proj_width * proj_width)
    pair_update = jnp.einsum("ijf,fc->ijc", outer, pairing_exit_matrix, preferred_element_type=jnp.float32)
    pair_count = jnp.einsum("si,sj->ij", mask_local, mask_cols, preferred_element_type=jnp.float32)
    return (couple_embedding.astype(jnp.float32) + pair_update / pair_count[:, :, None]).astype(jnp.bfloat16)


def triangle(pair_now, row_mask, weights, out_weight, incoming, devices):
    rows, cols, channels = pair_now.shape
    part = channels // devices
    normalized = standardize_features(pair_now.astype(jnp.float32), -1).astype(jnp.bfloat16)
    projections = jnp.einsum("ijc,ckh->khij", normalized, weights[:, :4], preferred_element_type=jnp.float32)
    left_proj = (jax.nn.sigmoid(projections[0]) * projections[1] * row_mask).astype(jnp.bfloat16)
    right_proj = (jax.nn.sigmoid(projections[2]) * projections[3] * row_mask).astype(jnp.bfloat16)
    gate_val = jax.nn.sigmoid(
        jnp.einsum("ijc,ch->ijh", normalized, weights[:, 4], preferred_element_type=jnp.float32)
    )
    both = jnp.stack(
        [left_proj.reshape(devices, part, rows, cols), right_proj.reshape(devices, part, rows, cols)], axis=1
    )
    both = exchange(both)
    both = jnp.transpose(both, (1, 2, 0, 3, 4)).reshape(2, part, devices * rows, cols)
    einsum_form = "hki,hkj->hij" if incoming else "hik,hjk->hij"
    products = jnp.einsum(einsum_form, both[0], both[1], preferred_element_type=jnp.float32).astype(jnp.bfloat16)
    products = jnp.transpose(products.reshape(part, devices, rows, cols), (1, 0, 2, 3))
    returned = exchange(products).reshape(channels, rows, cols)
    normed_products = standardize_features(returned.astype(jnp.float32), 0).astype(jnp.bfloat16)
    pair_update = jnp.einsum("hij,hc->ijc", normed_products, out_weight, preferred_element_type=jnp.float32)
    return (pair_now.astype(jnp.float32) + gate_val * pair_update).astype(jnp.bfloat16)


def local(
    devices,
    homolog_embedding,
    coverage_indicator,
    genuine_amino_flag,
    couple_embedding,
    pairing_entry_matrices,
    pairing_exit_matrix,
    trilateral_entry_matrices,
    trilateral_exit_matrices,
):
    rows, cols, _ = couple_embedding.shape
    held = homolog_embedding.shape[0]
    width = pairing_entry_matrices.shape[2]
    sequence_mask = coverage_indicator.astype(jnp.float32)
    msa_norm = standardize_features(homolog_embedding.astype(jnp.float32), -1).astype(jnp.bfloat16)
    entries = jnp.einsum("rgl,loe->roeg", msa_norm, pairing_entry_matrices, preferred_element_type=jnp.float32)
    entries = (entries * sequence_mask[:, None, None, :]).astype(jnp.bfloat16)
    own = jnp.transpose(entries[:, 0].reshape(held, width, devices, rows), (2, 0, 1, 3))
    shared = jnp.concatenate([entries[:, 1].reshape(held, width * cols), sequence_mask.astype(jnp.bfloat16)], axis=1)
    packed = jnp.concatenate(
        [jnp.broadcast_to(shared[None], (devices,) + shared.shape), own.reshape(devices, held, width * rows)], axis=2
    )
    packed = exchange(packed).reshape(devices * held, -1)
    right_cols = packed[:, : width * cols].reshape(-1, width, cols)
    mask_cols = packed[:, width * cols : (width + 1) * cols]
    left_local = packed[:, (width + 1) * cols :].reshape(-1, width, rows)
    first_row = lax.axis_index("dap") * rows
    mask_local = lax.dynamic_slice_in_dim(mask_cols, first_row, rows, 1)
    pair_one = outer_update(left_local, mask_local, right_cols, mask_cols, couple_embedding, pairing_exit_matrix)
    residues = genuine_amino_flag.astype(jnp.float32)
    row_mask = lax.dynamic_slice_in_dim(residues, first_row, rows, 0)[:, None] * residues[None, :]
    pair_two = triangle(
        pair_one, row_mask, trilateral_entry_matrices[0], trilateral_exit_matrices[0], False, devices
    )
    return triangle(pair_two, row_mask, trilateral_entry_matrices[1], trilateral_exit_matrices[1], True, devices)


def start_copies(pairs, sems):
    copies = [pltpu.make_async_copy(source, target, sems.at[at]) for at, (source, target) in enumerate(pairs)]
    for copy in copies:
        copy.start()
    return copies


def halves(row):
    return [pltpu.roll(row, LANES // 2, 1), row]


def entry_kernel(x_hbm, cover_hbm, flag_hbm, weight_hbm, out_ref, x_ref, cover_ref, flag_ref, weight_ref, sems):
    copies = start_copies(
        [(x_hbm, x_ref), (weight_hbm, weight_ref), (cover_hbm, cover_ref), (flag_hbm, flag_ref)], sems
    )
    for copy in copies:
        copy.wait()
    held, cols, _ = x_ref.shape
    width = weight_ref.shape[1]
    devices = out_ref.shape[0]
    cover = cover_ref[...].astype(F32)
    columns = jnp.transpose(jnp.concatenate([cover, jnp.zeros((8 - held, cols), F32)], axis=0))
    blank = jnp.zeros_like(weight_ref[0])
    own = jnp.zeros((cols, LANES), F32)
    marks = []
    for s in range(held):
        marks += halves(cover[s : s + 1])
    marks += halves(flag_ref[...].astype(F32))
    marks = jnp.concatenate(marks + [jnp.zeros((8 - len(marks), cols), F32)], axis=0)
    for s in range(held):
        normalized = norm(x_ref[s].astype(F32), -1)
        shared = (dot(weight_ref[1], normalized, 1, 1) * cover[s : s + 1]).astype(BF16)
        for peer in range(devices):
            out_ref[peer, s * width : (s + 1) * width, :] = shared
        weight = jnp.concatenate([weight_ref[0] if at == s else blank for at in range(LANES // width)], axis=0)
        own = own + dot(normalized, weight, 1, 1) * columns[:, s : s + 1]
    lane = lax.broadcasted_iota(jnp.int32, (8, LANES), 1)
    for peer in range(devices):
        block = jnp.where(lane < held * width, own[peer * 8 : peer * 8 + 8], marks)
        out_ref[peer, held * width :, :] = block.astype(BF16)


def project(pair_tile, weights, mask_ref, out_ref, gate_ref, first, devices):
    cols = pair_tile.shape[1] // 2
    share = pair_tile.shape[0] // devices
    normalized = norm(pair_tile, 0)
    mask = jnp.concatenate([mask_ref[first : first + 1], mask_ref[first + 1 : first + 2]], axis=1)
    left, right = (
        sigmoid(dot(weights[k], normalized)) * dot(weights[k + 1], normalized) * mask for k in (0, 2)
    )
    gate_ref[:, first * cols : (first + 2) * cols] = sigmoid(dot(weights[4], normalized))
    for peer in range(devices):
        for row in range(2):
            block = [
                side[peer * share : (peer + 1) * share, row * cols : (row + 1) * cols] for side in (left, right)
            ]
            at = (first + row) * 2 * share
            out_ref[peer, at : at + 2 * share, :] = jnp.concatenate(block, axis=0).astype(BF16)


def turned(weight_ref):
    return [jnp.transpose(weight_ref[k]) for k in range(weight_ref.shape[0])]


def outer_kernel(
    got_ref, couple_ref, exit_ref, weight_ref,
    out_ref, pair_ref, gate_ref, mask_ref,
    shared_ref, aux_ref, outer_ref,
):
    devices, _, cols = got_ref.shape
    rows, _, channels = couple_ref.shape
    held, width = 2, 32
    shared_ref[...] = got_ref[:, : held * width, :].astype(F32).reshape(devices * held * width, cols)
    aux_ref[...] = got_ref[:, held * width :, :].astype(F32).reshape(devices * 8, cols)
    lane = lax.broadcasted_iota(jnp.int32, (devices, LANES), 1)
    marks = []
    for row in range(0, 2 * held + 2, 2):
        low = aux_ref[pl.ds(row, devices, stride=8), :]
        high = aux_ref[pl.ds(row + 1, devices, stride=8), :]
        marks.append(jnp.where(lane < LANES // 2, pltpu.roll(low, LANES // 2, 1), high))
    cover = jnp.concatenate(marks[:held], axis=0).astype(BF16)
    flags = marks[held][0:1]
    chosen = lax.broadcasted_iota(jnp.int32, (rows, LANES), 1) == (
        lax.broadcasted_iota(jnp.int32, (rows, LANES), 0) + lax.axis_index("dap") * rows
    )
    cover_rows = dot(chosen.astype(BF16), cover, 1, 1).astype(BF16)
    scale = 1.0 / dot(cover_rows, cover)
    mask_ref[...] = jnp.sum(jnp.where(chosen, flags, 0.0), axis=1, keepdims=True) * flags
    per_tile = LANES // width
    tiles = []
    for tile in range(rows // per_tile):
        sides = [jnp.zeros((devices, LANES), F32) for _ in range(held)]
        for place in range(per_tile):
            values = aux_ref[pl.ds(tile * per_tile + place, devices, stride=8), :]
            here = (lane >= place * width) & (lane < (place + 1) * width)
            for s in range(held):
                turn = ((place - s) * width) % LANES
                moved = pltpu.roll(values, turn, 1) if turn else values
                sides[s] = jnp.where(here, moved, sides[s])
        tiles.append(jnp.concatenate(sides, axis=0))
    own = jnp.transpose(jnp.concatenate(tiles, axis=1)).astype(BF16)
    for e in range(0, width, 2):
        parts = []
        for step in range(2):
            parts.append(
                jnp.concatenate(
                    [
                        shared_ref[pl.ds(s * width + e + step, devices, stride=held * width), :]
                        for s in range(held)
                    ],
                    axis=0,
                )
            )
        result = dot(own, jnp.concatenate(parts, axis=1).astype(BF16)).astype(BF16)
        for step in range(2):
            for i in range(rows):
                outer_ref[(e + step) * width : (e + step + 1) * width, i * cols : (i + 1) * cols] = result[
                    i * width : (i + 1) * width, step * cols : (step + 1) * cols
                ]
    shared_ref[...] = exit_ref[...].astype(F32)
    leave = jnp.concatenate([shared_ref[pl.ds(e, width, stride=width), :] for e in range(width)], axis=0)
    leave = jnp.transpose(leave.astype(BF16))
    weights = turned(weight_ref.at[0])
    for first in range(0, rows, 2):
        at = slice(first * cols, (first + 2) * cols)
        update = dot(leave, outer_ref[:, at])
        per_pair = jnp.concatenate([scale[first : first + 1], scale[first + 1 : first + 2]], axis=1)
        couple = jnp.concatenate([jnp.transpose(couple_ref[first + row].astype(F32)) for row in range(2)], axis=1)
        pair = (couple + update * per_pair).astype(BF16)
        pair_ref[:, at] = pair
        project(pair.astype(F32), weights, mask_ref, out_ref, gate_ref, first, devices)


def product_kernel(incoming, got_ref, out_ref, sides_ref, products_ref):
    devices, _, cols = got_ref.shape
    part = 8
    total = sides_ref.shape[0] // (2 * part)
    sides_ref[...] = got_ref[...].astype(F32).reshape(total * 2 * part, cols)
    for h in range(part):
        left = sides_ref[pl.ds(h, total, stride=2 * part), :].astype(BF16)
        right = sides_ref[pl.ds(part + h, total, stride=2 * part), :].astype(BF16)
        result = dot(left, right, 0, 0) if incoming else dot(left, right, 1, 1)
        products_ref[pl.ds(h, total, stride=part), :] = result
    out_ref[...] = products_ref[...].astype(BF16).reshape(out_ref.shape)


def updated(got_ref, pair_ref, gate_ref, leave, first):
    devices, _, cols = got_ref.shape
    part = 8
    channels = devices * part
    got = got_ref[:, first * part : (first + 2) * part, :].astype(F32)
    products = jnp.concatenate(
        [got[:, :part].reshape(channels, cols), got[:, part:].reshape(channels, cols)], axis=1
    )
    at = slice(first * cols, (first + 2) * cols)
    update = dot(leave, norm(products, 0))
    return pair_ref[:, at].astype(F32) + gate_ref[:, at] * update


def middle_kernel(got_ref, pair_ref, gate_ref, leave_ref, weight_ref, mask_ref, out_ref, next_ref, next_gate_ref):
    devices, _, cols = got_ref.shape
    leave = jnp.transpose(leave_ref[0])
    weights = turned(weight_ref.at[1])
    for first in range(0, mask_ref.shape[0], 2):
        pair = updated(got_ref, pair_ref, gate_ref, leave, first).astype(BF16)
        next_ref[:, first * cols : (first + 2) * cols] = pair
        project(pair.astype(F32), weights, mask_ref, out_ref, next_gate_ref, first, devices)


def last_kernel(got_ref, pair_ref, gate_ref, leave_ref, out_hbm, out_ref, sems):
    rows, cols, _ = out_ref.shape
    leave = jnp.transpose(leave_ref[1])
    copies = []
    for first in range(0, rows, 2):
        pair = updated(got_ref, pair_ref, gate_ref, leave, first)
        for row in range(2):
            out_ref[first + row] = jnp.transpose(pair[:, row * cols : (row + 1) * cols]).astype(BF16)
        part = pl.ds(first, 2)
        copies.append(pltpu.make_async_copy(out_ref.at[part], out_hbm.at[part], sems.at[first // 2]))
        copies[-1].start()
    for copy in copies:
        copy.wait()


def call(kernel, inputs, outputs, scratch=(), in_specs=None, out_specs=None, limit=40):
    return pl.pallas_call(
        kernel,
        out_shape=outputs,
        in_specs=in_specs or [VMEM] * len(inputs),
        out_specs=out_specs or [VMEM] * len(outputs),
        scratch_shapes=list(scratch),
        compiler_params=pltpu.CompilerParams(vmem_limit_bytes=limit * 1024 * 1024),
    )(*inputs)


def shape(dims, kind=BF16):
    return jax.ShapeDtypeStruct(dims, kind)


def fast(
    devices,
    homolog_embedding,
    coverage_indicator,
    genuine_amino_flag,
    couple_embedding,
    pairing_entry_matrices,
    pairing_exit_matrix,
    trilateral_entry_matrices,
    trilateral_exit_matrices,
):
    rows, cols, channels = couple_embedding.shape
    held = homolog_embedding.shape[0]
    width = pairing_entry_matrices.shape[2]
    part = channels // devices
    (packed,) = call(
        entry_kernel,
        (
            homolog_embedding,
            coverage_indicator,
            genuine_amino_flag.reshape(1, cols),
            jnp.transpose(pairing_entry_matrices, (1, 2, 0)),
        ),
        [shape((devices, held * width + 8, cols))],
        [
            pltpu.VMEM(homolog_embedding.shape, BF16),
            pltpu.VMEM(coverage_indicator.shape, jnp.int32),
            pltpu.VMEM((1, cols), jnp.int32),
            pltpu.VMEM((2, width, homolog_embedding.shape[2]), BF16),
            pltpu.SemaphoreType.DMA((4,)),
        ],
        [HBM] * 4,
        limit=60,
    )
    entry = jnp.transpose(trilateral_entry_matrices, (0, 2, 1, 3))
    leave = trilateral_exit_matrices
    projected = [
        shape((devices, rows * 2 * part, cols)),
        shape((channels, rows * cols)),
        shape((channels, rows * cols), F32),
    ]
    both, pair, gate, row_mask = call(
        outer_kernel,
        (exchange(packed), couple_embedding, pairing_exit_matrix, entry),
        projected + [shape((rows, cols), F32)],
        [
            pltpu.VMEM((devices * held * width, cols), F32),
            pltpu.VMEM((devices * 8, cols), F32),
            pltpu.VMEM((width * width, rows * cols), BF16),
        ],
    )

    def multiply(both, incoming):
        (products,) = call(
            functools.partial(product_kernel, incoming),
            (exchange(both),),
            [shape((devices, rows * part, cols))],
            [pltpu.VMEM((devices * rows * 2 * part, cols), F32), pltpu.VMEM((devices * rows * part, cols), F32)],
        )
        return exchange(products)

    got = multiply(both, False)
    both, pair, gate = call(middle_kernel, (got, pair, gate, leave, entry, row_mask), projected)
    got = multiply(both, True)
    (pair_out,) = call(
        last_kernel,
        (got, pair, gate, leave),
        [shape((rows, cols, channels))],
        [pltpu.VMEM((rows, cols, channels), BF16), pltpu.SemaphoreType.DMA((rows // 2,))],
        out_specs=[HBM],
    )
    return pair_out


def fits(devices, homolog_embedding, couple_embedding, pairing_entry_matrices):
    rows, cols, channels = couple_embedding.shape
    return (
        homolog_embedding.shape[0] == 2
        and rows == 8
        and cols == LANES
        and channels == 8 * devices
        and channels == LANES
        and pairing_entry_matrices.shape[2] == 32
    )


def solution(mesh):
    devices = mesh.shape["dap"]

    def one_device(*arrays):
        chosen = fast if fits(devices, arrays[0], arrays[3], arrays[4]) else local
        return chosen(devices, *arrays)

    return jax.shard_map(
        one_device,
        mesh=mesh,
        in_specs=(
            P(("crops", "dap"), None, None),
            P(("crops", "dap"), None),
            P("crops"),
            P(("crops", "dap"), None, None),
            P(),
            P(),
            P(),
            P(),
        ),
        out_specs=P(("crops", "dap"), None, None),
        check_vma=False,
    )
```

```python
import functools

import jax
import jax.numpy as jnp
from jax import lax
from jax.experimental import pallas as pl
from jax.experimental.pallas import tpu as pltpu
from jax.sharding import PartitionSpec as P

F32 = jnp.float32
BF16 = jnp.bfloat16
EPS = 1e-05
LANES = 128
VMEM = pl.BlockSpec(memory_space=pltpu.VMEM)
HBM = pl.BlockSpec(memory_space=pltpu.HBM)


def dot(a, b, left=1, right=0):
    return lax.dot_general(a, b, (((left,), (right,)), ((), ())), preferred_element_type=F32)


def sigmoid(values):
    return 0.5 * jnp.tanh(0.5 * values) + 0.5


def norm(values, axis):
    size = values.shape[axis]
    average = jnp.sum(values, axis=axis, keepdims=True) * (1.0 / size)
    centered = values - average
    variance = jnp.sum(centered * centered, axis=axis, keepdims=True) * (1.0 / size)
    return (centered * lax.rsqrt(variance + EPS)).astype(BF16)


def standardize_features(values, axis):
    average = jnp.mean(values, axis=axis, keepdims=True)
    centered = values - average
    variance = jnp.mean(centered * centered, axis=axis, keepdims=True)
    return centered * lax.rsqrt(variance + 1e-05)


def exchange(blocks):
    return lax.all_to_all(blocks, "dap", split_axis=0, concat_axis=0, tiled=True)


def outer_update(left_local, mask_local, right_cols, mask_cols, couple_embedding, pairing_exit_matrix):
    proj_width = left_local.shape[1]
    local_rows = left_local.shape[2]
    col_total = right_cols.shape[2]
    outer = jnp.einsum("rzp,rej->pjze", left_local, right_cols, preferred_element_type=jnp.float32)
    outer = outer.astype(jnp.bfloat16).reshape(local_rows, col_total, proj_width * proj_width)
    pair_update = jnp.einsum("ijf,fc->ijc", outer, pairing_exit_matrix, preferred_element_type=jnp.float32)
    pair_count = jnp.einsum("si,sj->ij", mask_local, mask_cols, preferred_element_type=jnp.float32)
    return (couple_embedding.astype(jnp.float32) + pair_update / pair_count[:, :, None]).astype(jnp.bfloat16)


def triangle(pair_now, row_mask, weights, out_weight, incoming, devices):
    rows, cols, channels = pair_now.shape
    part = channels // devices
    normalized = standardize_features(pair_now.astype(jnp.float32), -1).astype(jnp.bfloat16)
    projections = jnp.einsum("ijc,ckh->khij", normalized, weights[:, :4], preferred_element_type=jnp.float32)
    left_proj = (jax.nn.sigmoid(projections[0]) * projections[1] * row_mask).astype(jnp.bfloat16)
    right_proj = (jax.nn.sigmoid(projections[2]) * projections[3] * row_mask).astype(jnp.bfloat16)
    gate_val = jax.nn.sigmoid(
        jnp.einsum("ijc,ch->ijh", normalized, weights[:, 4], preferred_element_type=jnp.float32)
    )
    both = jnp.stack(
        [left_proj.reshape(devices, part, rows, cols), right_proj.reshape(devices, part, rows, cols)], axis=1
    )
    both = exchange(both)
    both = jnp.transpose(both, (1, 2, 0, 3, 4)).reshape(2, part, devices * rows, cols)
    einsum_form = "hki,hkj->hij" if incoming else "hik,hjk->hij"
    products = jnp.einsum(einsum_form, both[0], both[1], preferred_element_type=jnp.float32).astype(jnp.bfloat16)
    products = jnp.transpose(products.reshape(part, devices, rows, cols), (1, 0, 2, 3))
    returned = exchange(products).reshape(channels, rows, cols)
    normed_products = standardize_features(returned.astype(jnp.float32), 0).astype(jnp.bfloat16)
    pair_update = jnp.einsum("hij,hc->ijc", normed_products, out_weight, preferred_element_type=jnp.float32)
    return (pair_now.astype(jnp.float32) + gate_val * pair_update).astype(jnp.bfloat16)


def local(
    devices,
    homolog_embedding,
    coverage_indicator,
    genuine_amino_flag,
    couple_embedding,
    pairing_entry_matrices,
    pairing_exit_matrix,
    trilateral_entry_matrices,
    trilateral_exit_matrices,
):
    rows, cols, _ = couple_embedding.shape
    held = homolog_embedding.shape[0]
    width = pairing_entry_matrices.shape[2]
    sequence_mask = coverage_indicator.astype(jnp.float32)
    msa_norm = standardize_features(homolog_embedding.astype(jnp.float32), -1).astype(jnp.bfloat16)
    entries = jnp.einsum("rgl,loe->roeg", msa_norm, pairing_entry_matrices, preferred_element_type=jnp.float32)
    entries = (entries * sequence_mask[:, None, None, :]).astype(jnp.bfloat16)
    own = jnp.transpose(entries[:, 0].reshape(held, width, devices, rows), (2, 0, 1, 3))
    shared = jnp.concatenate([entries[:, 1].reshape(held, width * cols), sequence_mask.astype(jnp.bfloat16)], axis=1)
    packed = jnp.concatenate(
        [jnp.broadcast_to(shared[None], (devices,) + shared.shape), own.reshape(devices, held, width * rows)], axis=2
    )
    packed = exchange(packed).reshape(devices * held, -1)
    right_cols = packed[:, : width * cols].reshape(-1, width, cols)
    mask_cols = packed[:, width * cols : (width + 1) * cols]
    left_local = packed[:, (width + 1) * cols :].reshape(-1, width, rows)
    first_row = lax.axis_index("dap") * rows
    mask_local = lax.dynamic_slice_in_dim(mask_cols, first_row, rows, 1)
    pair_one = outer_update(left_local, mask_local, right_cols, mask_cols, couple_embedding, pairing_exit_matrix)
    residues = genuine_amino_flag.astype(jnp.float32)
    row_mask = lax.dynamic_slice_in_dim(residues, first_row, rows, 0)[:, None] * residues[None, :]
    pair_two = triangle(
        pair_one, row_mask, trilateral_entry_matrices[0], trilateral_exit_matrices[0], False, devices
    )
    return triangle(pair_two, row_mask, trilateral_entry_matrices[1], trilateral_exit_matrices[1], True, devices)


def start_copies(pairs, sems):
    copies = [pltpu.make_async_copy(source, target, sems.at[at]) for at, (source, target) in enumerate(pairs)]
    for copy in copies:
        copy.start()
    return copies


def two_level(blocks, devices):
    groups = [list(range(parity, devices, 2)) for parity in range(2)]
    got = lax.all_to_all(blocks, "dap", split_axis=0, concat_axis=0, tiled=True, axis_index_groups=groups)
    return got, lax.ppermute(got, "dap", [(at, at ^ 1) for at in range(devices)])


def halves(row):
    return [pltpu.roll(row, LANES // 2, 1), row]


def entry_kernel(x_hbm, cover_hbm, flag_hbm, weight_hbm, out_ref, x_ref, cover_ref, flag_ref, weight_ref, sems):
    copies = start_copies(
        [(x_hbm, x_ref), (weight_hbm, weight_ref), (cover_hbm, cover_ref), (flag_hbm, flag_ref)], sems
    )
    for copy in copies:
        copy.wait()
    held, cols, _ = x_ref.shape
    width = weight_ref.shape[1]
    pairs = out_ref.shape[0]
    cover = cover_ref[...].astype(F32)
    columns = jnp.transpose(jnp.concatenate([cover, jnp.zeros((8 - held, cols), F32)], axis=0))
    blank = jnp.zeros_like(weight_ref[0])
    own = jnp.zeros((cols, LANES), F32)
    marks = []
    for s in range(held):
        marks += halves(cover[s : s + 1])
    marks += halves(flag_ref[...].astype(F32))
    marks = jnp.concatenate(marks + [jnp.zeros((8 - len(marks), cols), F32)], axis=0)
    for s in range(held):
        normalized = norm(x_ref[s].astype(F32), -1)
        shared = (dot(weight_ref[1], normalized, 1, 1) * cover[s : s + 1]).astype(BF16)
        for pair in range(pairs):
            out_ref[pair, s * width : (s + 1) * width, :] = shared
        weight = jnp.concatenate([weight_ref[0] if at == s else blank for at in range(LANES // width)], axis=0)
        own = own + dot(normalized, weight, 1, 1) * columns[:, s : s + 1]
    lane = lax.broadcasted_iota(jnp.int32, (16, LANES), 1)
    marks = jnp.concatenate([marks, marks], axis=0)
    for pair in range(pairs):
        block = jnp.where(lane < held * width, own[pair * 16 : pair * 16 + 16], marks)
        out_ref[pair, held * width :, :] = block.astype(BF16)


def project(pair_tile, weights, mask_ref, out_ref, gate_ref, first, devices):
    cols = pair_tile.shape[1] // 2
    share = pair_tile.shape[0] // devices
    normalized = norm(pair_tile, 0)
    mask = jnp.concatenate([mask_ref[first : first + 1], mask_ref[first + 1 : first + 2]], axis=1)
    left, right = (
        sigmoid(dot(weights[k], normalized)) * dot(weights[k + 1], normalized) * mask for k in (0, 2)
    )
    gate_ref[:, first * cols : (first + 2) * cols] = sigmoid(dot(weights[4], normalized))
    for peer in range(devices):
        for row in range(2):
            block = [
                side[peer * share : (peer + 1) * share, row * cols : (row + 1) * cols] for side in (left, right)
            ]
            at = (first + row) * 2 * share
            out_ref[peer, at : at + 2 * share, :] = jnp.concatenate(block, axis=0).astype(BF16)


def weight_kernel(entry_ref, exit_ref, leave_ref, couple_ref, out_entry, out_exit, out_leave, out_couple, rows_ref):
    for t in range(entry_ref.shape[0]):
        for k in range(entry_ref.shape[1]):
            out_entry[t, k] = jnp.transpose(entry_ref[t, k])
        out_leave[t] = jnp.transpose(leave_ref[t])
    width = 32
    rows_ref[...] = exit_ref[...].astype(F32)
    leave = jnp.concatenate([rows_ref[pl.ds(e, width, stride=width), :] for e in range(width)], axis=0)
    out_exit[...] = jnp.transpose(leave).astype(BF16)
    for row in range(couple_ref.shape[0]):
        out_couple[:, row * LANES : (row + 1) * LANES] = jnp.transpose(couple_ref[row])


def outer_kernel(
    got_ref, other_ref, couple_ref, exit_ref, weight_ref,
    out_ref, pair_ref, gate_ref, mask_ref,
    shared_ref, aux_ref, outer_ref,
):
    pairs, _, cols = got_ref.shape
    devices = 2 * pairs
    rows = couple_ref.shape[1] // cols
    held, width = 2, 32
    core = lax.rem(lax.axis_index("dap"), 2)
    for side, ref in enumerate((got_ref, other_ref)):
        shared = ref[:, : held * width, :].astype(F32).reshape(pairs * held * width, cols)
        shared_ref[side * pairs * held * width : (side + 1) * pairs * held * width, :] = shared
        aux = ref[:, held * width :, :].astype(F32)
        aux = jnp.where(core == 0, aux[:, :8], aux[:, 8:])
        aux_ref[side * pairs * 8 : (side + 1) * pairs * 8, :] = aux.reshape(pairs * 8, cols)
    lane = lax.broadcasted_iota(jnp.int32, (devices, LANES), 1)
    marks = []
    for row in range(0, 2 * held + 2, 2):
        low = aux_ref[pl.ds(row, devices, stride=8), :]
        high = aux_ref[pl.ds(row + 1, devices, stride=8), :]
        marks.append(jnp.where(lane < LANES // 2, pltpu.roll(low, LANES // 2, 1), high))
    cover = jnp.concatenate(marks[:held], axis=0).astype(BF16)
    flags = marks[held][0:1]
    chosen = lax.broadcasted_iota(jnp.int32, (rows, LANES), 1) == (
        lax.broadcasted_iota(jnp.int32, (rows, LANES), 0) + lax.axis_index("dap") * rows
    )
    cover_rows = dot(chosen.astype(BF16), cover, 1, 1).astype(BF16)
    scale = 1.0 / dot(cover_rows, cover)
    mask_ref[...] = jnp.sum(jnp.where(chosen, flags, 0.0), axis=1, keepdims=True) * flags
    per_tile = LANES // width
    tiles = []
    for tile in range(rows // per_tile):
        sides = [jnp.zeros((devices, LANES), F32) for _ in range(held)]
        for place in range(per_tile):
            values = aux_ref[pl.ds(tile * per_tile + place, devices, stride=8), :]
            here = (lane >= place * width) & (lane < (place + 1) * width)
            for s in range(held):
                turn = ((place - s) * width) % LANES
                moved = pltpu.roll(values, turn, 1) if turn else values
                sides[s] = jnp.where(here, moved, sides[s])
        tiles.append(jnp.concatenate(sides, axis=0))
    own = jnp.transpose(jnp.concatenate(tiles, axis=1)).astype(BF16)
    for e in range(0, width, 2):
        parts = []
        for step in range(2):
            parts.append(
                jnp.concatenate(
                    [
                        shared_ref[pl.ds(s * width + e + step, devices, stride=held * width), :]
                        for s in range(held)
                    ],
                    axis=0,
                )
            )
        result = dot(own, jnp.concatenate(parts, axis=1).astype(BF16)).astype(BF16)
        for step in range(2):
            for i in range(rows):
                outer_ref[(e + step) * width : (e + step + 1) * width, i * cols : (i + 1) * cols] = result[
                    i * width : (i + 1) * width, step * cols : (step + 1) * cols
                ]
    weights = [weight_ref[0, k] for k in range(5)]
    for first in range(0, rows, 2):
        at = slice(first * cols, (first + 2) * cols)
        update = dot(exit_ref[...], outer_ref[:, at])
        per_pair = jnp.concatenate([scale[first : first + 1], scale[first + 1 : first + 2]], axis=1)
        pair = (couple_ref[:, at].astype(F32) + update * per_pair).astype(BF16)
        pair_ref[:, at] = pair
        project(pair.astype(F32), weights, mask_ref, out_ref, gate_ref, first, devices)


def product_kernel(incoming, got_ref, out_ref, sides_ref, products_ref):
    devices, _, cols = got_ref.shape
    part = 8
    total = sides_ref.shape[0] // (2 * part)
    sides_ref[...] = got_ref[...].astype(F32).reshape(total * 2 * part, cols)
    for h in range(part):
        left = sides_ref[pl.ds(h, total, stride=2 * part), :].astype(BF16)
        right = sides_ref[pl.ds(part + h, total, stride=2 * part), :].astype(BF16)
        result = dot(left, right, 0, 0) if incoming else dot(left, right, 1, 1)
        products_ref[pl.ds(h, total, stride=part), :] = result
    out_ref[...] = products_ref[...].astype(BF16).reshape(out_ref.shape)


def updated(got_ref, pair_ref, gate_ref, leave, first):
    devices, _, cols = got_ref.shape
    part = 8
    channels = devices * part
    got = got_ref[:, first * part : (first + 2) * part, :].astype(F32)
    products = jnp.concatenate(
        [got[:, :part].reshape(channels, cols), got[:, part:].reshape(channels, cols)], axis=1
    )
    at = slice(first * cols, (first + 2) * cols)
    update = dot(leave, norm(products, 0))
    return pair_ref[:, at].astype(F32) + gate_ref[:, at] * update


def middle_kernel(got_ref, pair_ref, gate_ref, leave_ref, weight_ref, mask_ref, out_ref, next_ref, next_gate_ref):
    devices, _, cols = got_ref.shape
    leave = leave_ref[0]
    weights = [weight_ref[1, k] for k in range(5)]
    for first in range(0, mask_ref.shape[0], 2):
        pair = updated(got_ref, pair_ref, gate_ref, leave, first).astype(BF16)
        next_ref[:, first * cols : (first + 2) * cols] = pair
        project(pair.astype(F32), weights, mask_ref, out_ref, next_gate_ref, first, devices)


def last_kernel(got_ref, pair_ref, gate_ref, leave_ref, out_hbm, out_ref, sems):
    rows, cols, _ = out_ref.shape
    leave = leave_ref[1]
    copies = []
    for first in range(0, rows, 2):
        pair = updated(got_ref, pair_ref, gate_ref, leave, first)
        for row in range(2):
            out_ref[first + row] = jnp.transpose(pair[:, row * cols : (row + 1) * cols]).astype(BF16)
        part = pl.ds(first, 2)
        copies.append(pltpu.make_async_copy(out_ref.at[part], out_hbm.at[part], sems.at[first // 2]))
        copies[-1].start()
    for copy in copies:
        copy.wait()


def call(kernel, inputs, outputs, scratch=(), in_specs=None, out_specs=None, limit=40):
    return pl.pallas_call(
        kernel,
        out_shape=outputs,
        in_specs=in_specs or [VMEM] * len(inputs),
        out_specs=out_specs or [VMEM] * len(outputs),
        scratch_shapes=list(scratch),
        compiler_params=pltpu.CompilerParams(vmem_limit_bytes=limit * 1024 * 1024),
    )(*inputs)


def shape(dims, kind=BF16):
    return jax.ShapeDtypeStruct(dims, kind)


def fast(
    devices,
    homolog_embedding,
    coverage_indicator,
    genuine_amino_flag,
    couple_embedding,
    pairing_entry_matrices,
    pairing_exit_matrix,
    trilateral_entry_matrices,
    trilateral_exit_matrices,
):
    rows, cols, channels = couple_embedding.shape
    held = homolog_embedding.shape[0]
    width = pairing_entry_matrices.shape[2]
    part = channels // devices
    (packed,) = call(
        entry_kernel,
        (
            homolog_embedding,
            coverage_indicator,
            genuine_amino_flag.reshape(1, cols),
            jnp.transpose(pairing_entry_matrices, (1, 2, 0)),
        ),
        [shape((devices // 2, held * width + 16, cols))],
        [
            pltpu.VMEM(homolog_embedding.shape, BF16),
            pltpu.VMEM(coverage_indicator.shape, jnp.int32),
            pltpu.VMEM((1, cols), jnp.int32),
            pltpu.VMEM((2, width, homolog_embedding.shape[2]), BF16),
            pltpu.SemaphoreType.DMA((4,)),
        ],
        [HBM] * 4,
        limit=60,
    )
    packed, entry, leave_rows, exit_rows, couple_rows = lax.optimization_barrier(
        (packed, trilateral_entry_matrices, trilateral_exit_matrices, pairing_exit_matrix, couple_embedding)
    )
    got = two_level(packed, devices)
    entry, exit_matrix, leave, couple = call(
        weight_kernel,
        (jnp.transpose(entry, (0, 2, 1, 3)), exit_rows, leave_rows, couple_rows),
        [
            shape((2, 5, channels, channels)),
            shape((channels, width * width)),
            shape((2, channels, channels)),
            shape((channels, rows * cols)),
        ],
        [pltpu.VMEM((width * width, channels), F32)],
    )
    projected = [
        shape((devices, rows * 2 * part, cols)),
        shape((channels, rows * cols)),
        shape((channels, rows * cols), F32),
    ]
    both, pair, gate, row_mask = call(
        outer_kernel,
        (*got, couple, exit_matrix, entry),
        projected + [shape((rows, cols), F32)],
        [
            pltpu.VMEM((devices * held * width, cols), F32),
            pltpu.VMEM((devices * 8, cols), F32),
            pltpu.VMEM((width * width, rows * cols), BF16),
        ],
    )

    def multiply(both, incoming):
        (products,) = call(
            functools.partial(product_kernel, incoming),
            (exchange(both),),
            [shape((devices, rows * part, cols))],
            [pltpu.VMEM((devices * rows * 2 * part, cols), F32), pltpu.VMEM((devices * rows * part, cols), F32)],
        )
        return exchange(products)

    got = multiply(both, False)
    both, pair, gate = call(middle_kernel, (got, pair, gate, leave, entry, row_mask), projected)
    got = multiply(both, True)
    (pair_out,) = call(
        last_kernel,
        (got, pair, gate, leave),
        [shape((rows, cols, channels))],
        [pltpu.VMEM((rows, cols, channels), BF16), pltpu.SemaphoreType.DMA((rows // 2,))],
        out_specs=[HBM],
    )
    return pair_out


def fits(devices, homolog_embedding, couple_embedding, pairing_entry_matrices):
    rows, cols, channels = couple_embedding.shape
    return (
        devices % 2 == 0
        and homolog_embedding.shape[0] == 2
        and rows == 8
        and cols == LANES
        and channels == 8 * devices
        and channels == LANES
        and pairing_entry_matrices.shape[2] == 32
    )


def solution(mesh):
    devices = mesh.shape["dap"]

    def one_device(*arrays):
        chosen = fast if fits(devices, arrays[0], arrays[3], arrays[4]) else local
        return chosen(devices, *arrays)

    return jax.shard_map(
        one_device,
        mesh=mesh,
        in_specs=(
            P(("crops", "dap"), None, None),
            P(("crops", "dap"), None),
            P("crops"),
            P(("crops", "dap"), None, None),
            P(),
            P(),
            P(),
            P(),
        ),
        out_specs=P(("crops", "dap"), None, None),
        check_vma=False,
    )
```

```python
import functools

import jax
import jax.numpy as jnp
from jax import lax
from jax.experimental import pallas as pl
from jax.experimental.pallas import tpu as pltpu
from jax.sharding import PartitionSpec as P

F32 = jnp.float32
BF16 = jnp.bfloat16
EPS = 1e-05
LANES = 128
VMEM = pl.BlockSpec(memory_space=pltpu.VMEM)
HBM = pl.BlockSpec(memory_space=pltpu.HBM)


def dot(a, b, left=1, right=0):
    return lax.dot_general(a, b, (((left,), (right,)), ((), ())), preferred_element_type=F32)


def sigmoid(values):
    return 0.5 * jnp.tanh(0.5 * values) + 0.5


def norm(values, axis):
    size = values.shape[axis]
    average = jnp.sum(values, axis=axis, keepdims=True) * (1.0 / size)
    centered = values - average
    variance = jnp.sum(centered * centered, axis=axis, keepdims=True) * (1.0 / size)
    return (centered * lax.rsqrt(variance + EPS)).astype(BF16)


def standardize_features(values, axis):
    average = jnp.mean(values, axis=axis, keepdims=True)
    centered = values - average
    variance = jnp.mean(centered * centered, axis=axis, keepdims=True)
    return centered * lax.rsqrt(variance + 1e-05)


def exchange(blocks):
    return lax.all_to_all(blocks, "dap", split_axis=0, concat_axis=0, tiled=True)


def outer_update(left_local, mask_local, right_cols, mask_cols, couple_embedding, pairing_exit_matrix):
    proj_width = left_local.shape[1]
    local_rows = left_local.shape[2]
    col_total = right_cols.shape[2]
    outer = jnp.einsum("rzp,rej->pjze", left_local, right_cols, preferred_element_type=jnp.float32)
    outer = outer.astype(jnp.bfloat16).reshape(local_rows, col_total, proj_width * proj_width)
    pair_update = jnp.einsum("ijf,fc->ijc", outer, pairing_exit_matrix, preferred_element_type=jnp.float32)
    pair_count = jnp.einsum("si,sj->ij", mask_local, mask_cols, preferred_element_type=jnp.float32)
    return (couple_embedding.astype(jnp.float32) + pair_update / pair_count[:, :, None]).astype(jnp.bfloat16)


def triangle(pair_now, row_mask, weights, out_weight, incoming, devices):
    rows, cols, channels = pair_now.shape
    part = channels // devices
    normalized = standardize_features(pair_now.astype(jnp.float32), -1).astype(jnp.bfloat16)
    projections = jnp.einsum("ijc,ckh->khij", normalized, weights[:, :4], preferred_element_type=jnp.float32)
    left_proj = (jax.nn.sigmoid(projections[0]) * projections[1] * row_mask).astype(jnp.bfloat16)
    right_proj = (jax.nn.sigmoid(projections[2]) * projections[3] * row_mask).astype(jnp.bfloat16)
    gate_val = jax.nn.sigmoid(
        jnp.einsum("ijc,ch->ijh", normalized, weights[:, 4], preferred_element_type=jnp.float32)
    )
    both = jnp.stack(
        [left_proj.reshape(devices, part, rows, cols), right_proj.reshape(devices, part, rows, cols)], axis=1
    )
    both = exchange(both)
    both = jnp.transpose(both, (1, 2, 0, 3, 4)).reshape(2, part, devices * rows, cols)
    einsum_form = "hki,hkj->hij" if incoming else "hik,hjk->hij"
    products = jnp.einsum(einsum_form, both[0], both[1], preferred_element_type=jnp.float32).astype(jnp.bfloat16)
    products = jnp.transpose(products.reshape(part, devices, rows, cols), (1, 0, 2, 3))
    returned = exchange(products).reshape(channels, rows, cols)
    normed_products = standardize_features(returned.astype(jnp.float32), 0).astype(jnp.bfloat16)
    pair_update = jnp.einsum("hij,hc->ijc", normed_products, out_weight, preferred_element_type=jnp.float32)
    return (pair_now.astype(jnp.float32) + gate_val * pair_update).astype(jnp.bfloat16)


def local(
    devices,
    homolog_embedding,
    coverage_indicator,
    genuine_amino_flag,
    couple_embedding,
    pairing_entry_matrices,
    pairing_exit_matrix,
    trilateral_entry_matrices,
    trilateral_exit_matrices,
):
    rows, cols, _ = couple_embedding.shape
    held = homolog_embedding.shape[0]
    width = pairing_entry_matrices.shape[2]
    sequence_mask = coverage_indicator.astype(jnp.float32)
    msa_norm = standardize_features(homolog_embedding.astype(jnp.float32), -1).astype(jnp.bfloat16)
    entries = jnp.einsum("rgl,loe->roeg", msa_norm, pairing_entry_matrices, preferred_element_type=jnp.float32)
    entries = (entries * sequence_mask[:, None, None, :]).astype(jnp.bfloat16)
    own = jnp.transpose(entries[:, 0].reshape(held, width, devices, rows), (2, 0, 1, 3))
    shared = jnp.concatenate([entries[:, 1].reshape(held, width * cols), sequence_mask.astype(jnp.bfloat16)], axis=1)
    packed = jnp.concatenate(
        [jnp.broadcast_to(shared[None], (devices,) + shared.shape), own.reshape(devices, held, width * rows)], axis=2
    )
    packed = exchange(packed).reshape(devices * held, -1)
    right_cols = packed[:, : width * cols].reshape(-1, width, cols)
    mask_cols = packed[:, width * cols : (width + 1) * cols]
    left_local = packed[:, (width + 1) * cols :].reshape(-1, width, rows)
    first_row = lax.axis_index("dap") * rows
    mask_local = lax.dynamic_slice_in_dim(mask_cols, first_row, rows, 1)
    pair_one = outer_update(left_local, mask_local, right_cols, mask_cols, couple_embedding, pairing_exit_matrix)
    residues = genuine_amino_flag.astype(jnp.float32)
    row_mask = lax.dynamic_slice_in_dim(residues, first_row, rows, 0)[:, None] * residues[None, :]
    pair_two = triangle(
        pair_one, row_mask, trilateral_entry_matrices[0], trilateral_exit_matrices[0], False, devices
    )
    return triangle(pair_two, row_mask, trilateral_entry_matrices[1], trilateral_exit_matrices[1], True, devices)


def start_copies(pairs, sems):
    copies = [pltpu.make_async_copy(source, target, sems.at[at]) for at, (source, target) in enumerate(pairs)]
    for copy in copies:
        copy.start()
    return copies


def two_level(blocks, devices):
    groups = [list(range(parity, devices, 2)) for parity in range(2)]
    got = lax.all_to_all(blocks, "dap", split_axis=0, concat_axis=0, tiled=True, axis_index_groups=groups)
    return got, lax.ppermute(got, "dap", [(at, at ^ 1) for at in range(devices)])


def halves(row):
    return [pltpu.roll(row, LANES // 2, 1), row]


def entry_kernel(x_hbm, cover_hbm, flag_hbm, weight_hbm, out_ref, x_ref, cover_ref, flag_ref, weight_ref, sems):
    copies = start_copies(
        [(x_hbm, x_ref), (weight_hbm, weight_ref), (cover_hbm, cover_ref), (flag_hbm, flag_ref)], sems
    )
    for copy in copies:
        copy.wait()
    held, cols, _ = x_ref.shape
    width = weight_ref.shape[1]
    pairs = out_ref.shape[0]
    cover = cover_ref[...].astype(F32)
    columns = jnp.transpose(jnp.concatenate([cover, jnp.zeros((8 - held, cols), F32)], axis=0))
    blank = jnp.zeros_like(weight_ref[0])
    own = jnp.zeros((cols, LANES), F32)
    marks = []
    for s in range(held):
        marks += halves(cover[s : s + 1])
    marks += halves(flag_ref[...].astype(F32))
    marks = jnp.concatenate(marks + [jnp.zeros((8 - len(marks), cols), F32)], axis=0)
    for s in range(held):
        normalized = norm(x_ref[s].astype(F32), -1)
        shared = (dot(weight_ref[1], normalized, 1, 1) * cover[s : s + 1]).astype(BF16)
        for pair in range(pairs):
            out_ref[pair, s * width : (s + 1) * width, :] = shared
        weight = jnp.concatenate([weight_ref[0] if at == s else blank for at in range(LANES // width)], axis=0)
        own = own + dot(normalized, weight, 1, 1) * columns[:, s : s + 1]
    lane = lax.broadcasted_iota(jnp.int32, (16, LANES), 1)
    marks = jnp.concatenate([marks, marks], axis=0)
    for pair in range(pairs):
        block = jnp.where(lane < held * width, own[pair * 16 : pair * 16 + 16], marks)
        out_ref[pair, held * width :, :] = block.astype(BF16)


def project(pair_tile, weights, mask_ref, out_ref, gate_ref, first, devices):
    cols = pair_tile.shape[1] // 2
    share = pair_tile.shape[0] // devices
    normalized = norm(pair_tile, 0)
    mask = jnp.concatenate([mask_ref[first : first + 1], mask_ref[first + 1 : first + 2]], axis=1)
    size = pair_tile.shape[0]
    entries = dot(weights, normalized)
    entries = [entries[k * size : (k + 1) * size] for k in range(5)]
    left, right = (sigmoid(entries[k]) * entries[k + 1] * mask for k in (0, 2))
    gate_ref[:, first * cols : (first + 2) * cols] = sigmoid(entries[4])
    for peer in range(devices):
        for row in range(2):
            block = [
                side[peer * share : (peer + 1) * share, row * cols : (row + 1) * cols] for side in (left, right)
            ]
            at = (first + row) * 2 * share
            out_ref[peer, at : at + 2 * share, :] = jnp.concatenate(block, axis=0).astype(BF16)


def weight_kernel(entry_ref, exit_ref, out_entry, out_exit, rows_ref):
    for t in range(entry_ref.shape[0]):
        for k in range(entry_ref.shape[1]):
            out_entry[t, k * LANES : (k + 1) * LANES, :] = jnp.transpose(entry_ref[t, k])
    width = 32
    rows_ref[...] = exit_ref[...].astype(F32)
    leave = jnp.concatenate([rows_ref[pl.ds(e, width, stride=width), :] for e in range(width)], axis=0)
    out_exit[...] = jnp.transpose(leave).astype(BF16)


def outer_kernel(
    got_ref, other_ref, couple_ref, exit_ref, weight_ref,
    out_ref, pair_ref, gate_ref, mask_ref,
    shared_ref, aux_ref, outer_ref,
):
    pairs, _, cols = got_ref.shape
    devices = 2 * pairs
    rows = couple_ref.shape[0]
    held, width = 2, 32
    core = lax.rem(lax.axis_index("dap"), 2)
    for side, ref in enumerate((got_ref, other_ref)):
        shared = ref[:, : held * width, :].astype(F32).reshape(pairs * held * width, cols)
        shared_ref[side * pairs * held * width : (side + 1) * pairs * held * width, :] = shared
        aux = ref[:, held * width :, :].astype(F32)
        aux = jnp.where(core == 0, aux[:, :8], aux[:, 8:])
        aux_ref[side * pairs * 8 : (side + 1) * pairs * 8, :] = aux.reshape(pairs * 8, cols)
    lane = lax.broadcasted_iota(jnp.int32, (devices, LANES), 1)
    marks = []
    for row in range(0, 2 * held + 2, 2):
        low = aux_ref[pl.ds(row, devices, stride=8), :]
        high = aux_ref[pl.ds(row + 1, devices, stride=8), :]
        marks.append(jnp.where(lane < LANES // 2, pltpu.roll(low, LANES // 2, 1), high))
    cover = jnp.concatenate(marks[:held], axis=0).astype(BF16)
    flags = marks[held][0:1]
    chosen = lax.broadcasted_iota(jnp.int32, (rows, LANES), 1) == (
        lax.broadcasted_iota(jnp.int32, (rows, LANES), 0) + lax.axis_index("dap") * rows
    )
    cover_rows = dot(chosen.astype(BF16), cover, 1, 1).astype(BF16)
    scale = 1.0 / dot(cover_rows, cover)
    mask_ref[...] = jnp.sum(jnp.where(chosen, flags, 0.0), axis=1, keepdims=True) * flags
    per_tile = LANES // width
    tiles = []
    for tile in range(rows // per_tile):
        sides = [jnp.zeros((devices, LANES), F32) for _ in range(held)]
        for place in range(per_tile):
            values = aux_ref[pl.ds(tile * per_tile + place, devices, stride=8), :]
            here = (lane >= place * width) & (lane < (place + 1) * width)
            for s in range(held):
                turn = ((place - s) * width) % LANES
                moved = pltpu.roll(values, turn, 1) if turn else values
                sides[s] = jnp.where(here, moved, sides[s])
        tiles.append(jnp.concatenate(sides, axis=0))
    own = jnp.transpose(jnp.concatenate(tiles, axis=1)).astype(BF16)
    for e in range(0, width, 2):
        parts = []
        for step in range(2):
            parts.append(
                jnp.concatenate(
                    [
                        shared_ref[pl.ds(s * width + e + step, devices, stride=held * width), :]
                        for s in range(held)
                    ],
                    axis=0,
                )
            )
        result = dot(own, jnp.concatenate(parts, axis=1).astype(BF16)).astype(BF16)
        for step in range(2):
            for i in range(rows):
                outer_ref[(e + step) * width : (e + step + 1) * width, i * cols : (i + 1) * cols] = result[
                    i * width : (i + 1) * width, step * cols : (step + 1) * cols
                ]
    weights = weight_ref[0]
    for first in range(0, rows, 2):
        at = slice(first * cols, (first + 2) * cols)
        update = dot(exit_ref[...], outer_ref[:, at])
        per_pair = jnp.concatenate([scale[first : first + 1], scale[first + 1 : first + 2]], axis=1)
        couple = jnp.concatenate([jnp.transpose(couple_ref[first + row]) for row in range(2)], axis=1)
        pair = (couple.astype(F32) + update * per_pair).astype(BF16)
        pair_ref[:, at] = pair
        project(pair.astype(F32), weights, mask_ref, out_ref, gate_ref, first, devices)


def product_kernel(incoming, got_ref, out_ref, sides_ref, products_ref):
    devices, _, cols = got_ref.shape
    part = 8
    total = sides_ref.shape[0] // (2 * part)
    sides_ref[...] = got_ref[...].astype(F32).reshape(total * 2 * part, cols)
    for h in range(part):
        left = sides_ref[pl.ds(h, total, stride=2 * part), :].astype(BF16)
        right = sides_ref[pl.ds(part + h, total, stride=2 * part), :].astype(BF16)
        result = dot(left, right, 0, 0) if incoming else dot(left, right, 1, 1)
        products_ref[pl.ds(h, total, stride=part), :] = result
    out_ref[...] = products_ref[...].astype(BF16).reshape(out_ref.shape)


def updated(got_ref, pair_ref, gate_ref, leave, first):
    devices, _, cols = got_ref.shape
    part = 8
    channels = devices * part
    got = got_ref[:, first * part : (first + 2) * part, :].astype(F32)
    products = jnp.concatenate(
        [got[:, :part].reshape(channels, cols), got[:, part:].reshape(channels, cols)], axis=1
    )
    at = slice(first * cols, (first + 2) * cols)
    update = dot(leave, norm(products, 0))
    return pair_ref[:, at].astype(F32) + gate_ref[:, at] * update


def middle_kernel(got_ref, pair_ref, gate_ref, leave_ref, weight_ref, mask_ref, out_ref, next_ref, next_gate_ref):
    devices, _, cols = got_ref.shape
    leave = jnp.transpose(leave_ref[0])
    weights = weight_ref[1]
    for first in range(0, mask_ref.shape[0], 2):
        pair = updated(got_ref, pair_ref, gate_ref, leave, first).astype(BF16)
        next_ref[:, first * cols : (first + 2) * cols] = pair
        project(pair.astype(F32), weights, mask_ref, out_ref, next_gate_ref, first, devices)


def last_kernel(got_ref, pair_ref, gate_ref, leave_ref, out_hbm, out_ref, sems):
    rows, cols, _ = out_ref.shape
    leave = jnp.transpose(leave_ref[1])
    copies = []
    for first in range(0, rows, 2):
        pair = updated(got_ref, pair_ref, gate_ref, leave, first)
        for row in range(2):
            out_ref[first + row] = jnp.transpose(pair[:, row * cols : (row + 1) * cols]).astype(BF16)
        part = pl.ds(first, 2)
        copies.append(pltpu.make_async_copy(out_ref.at[part], out_hbm.at[part], sems.at[first // 2]))
        copies[-1].start()
    for copy in copies:
        copy.wait()


def call(kernel, inputs, outputs, scratch=(), in_specs=None, out_specs=None, limit=40):
    return pl.pallas_call(
        kernel,
        out_shape=outputs,
        in_specs=in_specs or [VMEM] * len(inputs),
        out_specs=out_specs or [VMEM] * len(outputs),
        scratch_shapes=list(scratch),
        compiler_params=pltpu.CompilerParams(vmem_limit_bytes=limit * 1024 * 1024),
    )(*inputs)


def shape(dims, kind=BF16):
    return jax.ShapeDtypeStruct(dims, kind)


def fast(
    devices,
    homolog_embedding,
    coverage_indicator,
    genuine_amino_flag,
    couple_embedding,
    pairing_entry_matrices,
    pairing_exit_matrix,
    trilateral_entry_matrices,
    trilateral_exit_matrices,
):
    rows, cols, channels = couple_embedding.shape
    held = homolog_embedding.shape[0]
    width = pairing_entry_matrices.shape[2]
    part = channels // devices
    (packed,) = call(
        entry_kernel,
        (
            homolog_embedding,
            coverage_indicator,
            genuine_amino_flag.reshape(1, cols),
            jnp.transpose(pairing_entry_matrices, (1, 2, 0)),
        ),
        [shape((devices // 2, held * width + 16, cols))],
        [
            pltpu.VMEM(homolog_embedding.shape, BF16),
            pltpu.VMEM(coverage_indicator.shape, jnp.int32),
            pltpu.VMEM((1, cols), jnp.int32),
            pltpu.VMEM((2, width, homolog_embedding.shape[2]), BF16),
            pltpu.SemaphoreType.DMA((4,)),
        ],
        [HBM] * 4,
        limit=60,
    )
    packed, entry, exit_rows = lax.optimization_barrier((packed, trilateral_entry_matrices, pairing_exit_matrix))
    got = two_level(packed, devices)
    entry, exit_matrix = call(
        weight_kernel,
        (jnp.transpose(entry, (0, 2, 1, 3)), exit_rows),
        [
            shape((2, 5 * channels, channels)),
            shape((channels, width * width)),
        ],
        [pltpu.VMEM((width * width, channels), F32)],
    )
    projected = [
        shape((devices, rows * 2 * part, cols)),
        shape((channels, rows * cols)),
        shape((channels, rows * cols), F32),
    ]
    both, pair, gate, row_mask = call(
        outer_kernel,
        (*got, couple_embedding, exit_matrix, entry),
        projected + [shape((rows, cols), F32)],
        [
            pltpu.VMEM((devices * held * width, cols), F32),
            pltpu.VMEM((devices * 8, cols), F32),
            pltpu.VMEM((width * width, rows * cols), BF16),
        ],
    )

    def multiply(both, incoming):
        (products,) = call(
            functools.partial(product_kernel, incoming),
            (exchange(both),),
            [shape((devices, rows * part, cols))],
            [pltpu.VMEM((devices * rows * 2 * part, cols), F32), pltpu.VMEM((devices * rows * part, cols), F32)],
        )
        return exchange(products)

    got = multiply(both, False)
    both, pair, gate = call(middle_kernel, (got, pair, gate, trilateral_exit_matrices, entry, row_mask), projected)
    got = multiply(both, True)
    (pair_out,) = call(
        last_kernel,
        (got, pair, gate, trilateral_exit_matrices),
        [shape((rows, cols, channels))],
        [pltpu.VMEM((rows, cols, channels), BF16), pltpu.SemaphoreType.DMA((rows // 2,))],
        out_specs=[HBM],
    )
    return pair_out


def fits(devices, homolog_embedding, couple_embedding, pairing_entry_matrices):
    rows, cols, channels = couple_embedding.shape
    return (
        devices % 2 == 0
        and homolog_embedding.shape[0] == 2
        and rows == 8
        and cols == LANES
        and channels == 8 * devices
        and channels == LANES
        and pairing_entry_matrices.shape[2] == 32
    )


def solution(mesh):
    devices = mesh.shape["dap"]

    def one_device(*arrays):
        chosen = fast if fits(devices, arrays[0], arrays[3], arrays[4]) else local
        return chosen(devices, *arrays)

    return jax.shard_map(
        one_device,
        mesh=mesh,
        in_specs=(
            P(("crops", "dap"), None, None),
            P(("crops", "dap"), None),
            P("crops"),
            P(("crops", "dap"), None, None),
            P(),
            P(),
            P(),
            P(),
        ),
        out_specs=P(("crops", "dap"), None, None),
        check_vma=False,
    )
```

```python
import functools

import jax
import jax.numpy as jnp
from jax import lax
from jax.experimental import pallas as pl
from jax.experimental.pallas import tpu as pltpu
from jax.sharding import PartitionSpec as P

F32 = jnp.float32
BF16 = jnp.bfloat16
EPS = 1e-05
LANES = 128
VMEM = pl.BlockSpec(memory_space=pltpu.VMEM)
HBM = pl.BlockSpec(memory_space=pltpu.HBM)


def dot(a, b, left=1, right=0):
    return lax.dot_general(a, b, (((left,), (right,)), ((), ())), preferred_element_type=F32)


def sigmoid(values):
    return 0.5 * jnp.tanh(0.5 * values) + 0.5


def norm(values, axis):
    size = values.shape[axis]
    average = jnp.sum(values, axis=axis, keepdims=True) * (1.0 / size)
    centered = values - average
    variance = jnp.sum(centered * centered, axis=axis, keepdims=True) * (1.0 / size)
    return (centered * lax.rsqrt(variance + EPS)).astype(BF16)


def standardize_features(values, axis):
    average = jnp.mean(values, axis=axis, keepdims=True)
    centered = values - average
    variance = jnp.mean(centered * centered, axis=axis, keepdims=True)
    return centered * lax.rsqrt(variance + 1e-05)


def exchange(blocks):
    return lax.all_to_all(blocks, "dap", split_axis=0, concat_axis=0, tiled=True)


def outer_update(left_local, mask_local, right_cols, mask_cols, couple_embedding, pairing_exit_matrix):
    proj_width = left_local.shape[1]
    local_rows = left_local.shape[2]
    col_total = right_cols.shape[2]
    outer = jnp.einsum("rzp,rej->pjze", left_local, right_cols, preferred_element_type=jnp.float32)
    outer = outer.astype(jnp.bfloat16).reshape(local_rows, col_total, proj_width * proj_width)
    pair_update = jnp.einsum("ijf,fc->ijc", outer, pairing_exit_matrix, preferred_element_type=jnp.float32)
    pair_count = jnp.einsum("si,sj->ij", mask_local, mask_cols, preferred_element_type=jnp.float32)
    return (couple_embedding.astype(jnp.float32) + pair_update / pair_count[:, :, None]).astype(jnp.bfloat16)


def triangle(pair_now, row_mask, weights, out_weight, incoming, devices):
    rows, cols, channels = pair_now.shape
    part = channels // devices
    normalized = standardize_features(pair_now.astype(jnp.float32), -1).astype(jnp.bfloat16)
    projections = jnp.einsum("ijc,ckh->khij", normalized, weights[:, :4], preferred_element_type=jnp.float32)
    left_proj = (jax.nn.sigmoid(projections[0]) * projections[1] * row_mask).astype(jnp.bfloat16)
    right_proj = (jax.nn.sigmoid(projections[2]) * projections[3] * row_mask).astype(jnp.bfloat16)
    gate_val = jax.nn.sigmoid(
        jnp.einsum("ijc,ch->ijh", normalized, weights[:, 4], preferred_element_type=jnp.float32)
    )
    both = jnp.stack(
        [left_proj.reshape(devices, part, rows, cols), right_proj.reshape(devices, part, rows, cols)], axis=1
    )
    both = exchange(both)
    both = jnp.transpose(both, (1, 2, 0, 3, 4)).reshape(2, part, devices * rows, cols)
    einsum_form = "hki,hkj->hij" if incoming else "hik,hjk->hij"
    products = jnp.einsum(einsum_form, both[0], both[1], preferred_element_type=jnp.float32).astype(jnp.bfloat16)
    products = jnp.transpose(products.reshape(part, devices, rows, cols), (1, 0, 2, 3))
    returned = exchange(products).reshape(channels, rows, cols)
    normed_products = standardize_features(returned.astype(jnp.float32), 0).astype(jnp.bfloat16)
    pair_update = jnp.einsum("hij,hc->ijc", normed_products, out_weight, preferred_element_type=jnp.float32)
    return (pair_now.astype(jnp.float32) + gate_val * pair_update).astype(jnp.bfloat16)


def local(
    devices,
    homolog_embedding,
    coverage_indicator,
    genuine_amino_flag,
    couple_embedding,
    pairing_entry_matrices,
    pairing_exit_matrix,
    trilateral_entry_matrices,
    trilateral_exit_matrices,
):
    rows, cols, _ = couple_embedding.shape
    held = homolog_embedding.shape[0]
    width = pairing_entry_matrices.shape[2]
    sequence_mask = coverage_indicator.astype(jnp.float32)
    msa_norm = standardize_features(homolog_embedding.astype(jnp.float32), -1).astype(jnp.bfloat16)
    entries = jnp.einsum("rgl,loe->roeg", msa_norm, pairing_entry_matrices, preferred_element_type=jnp.float32)
    entries = (entries * sequence_mask[:, None, None, :]).astype(jnp.bfloat16)
    own = jnp.transpose(entries[:, 0].reshape(held, width, devices, rows), (2, 0, 1, 3))
    shared = jnp.concatenate([entries[:, 1].reshape(held, width * cols), sequence_mask.astype(jnp.bfloat16)], axis=1)
    packed = jnp.concatenate(
        [jnp.broadcast_to(shared[None], (devices,) + shared.shape), own.reshape(devices, held, width * rows)], axis=2
    )
    packed = exchange(packed).reshape(devices * held, -1)
    right_cols = packed[:, : width * cols].reshape(-1, width, cols)
    mask_cols = packed[:, width * cols : (width + 1) * cols]
    left_local = packed[:, (width + 1) * cols :].reshape(-1, width, rows)
    first_row = lax.axis_index("dap") * rows
    mask_local = lax.dynamic_slice_in_dim(mask_cols, first_row, rows, 1)
    pair_one = outer_update(left_local, mask_local, right_cols, mask_cols, couple_embedding, pairing_exit_matrix)
    residues = genuine_amino_flag.astype(jnp.float32)
    row_mask = lax.dynamic_slice_in_dim(residues, first_row, rows, 0)[:, None] * residues[None, :]
    pair_two = triangle(
        pair_one, row_mask, trilateral_entry_matrices[0], trilateral_exit_matrices[0], False, devices
    )
    return triangle(pair_two, row_mask, trilateral_entry_matrices[1], trilateral_exit_matrices[1], True, devices)


def start_copies(pairs, sems):
    copies = [pltpu.make_async_copy(source, target, sems.at[at]) for at, (source, target) in enumerate(pairs)]
    for copy in copies:
        copy.start()
    return copies


def two_level(blocks, devices):
    groups = [list(range(parity, devices, 2)) for parity in range(2)]
    got = lax.all_to_all(blocks, "dap", split_axis=0, concat_axis=0, tiled=True, axis_index_groups=groups)
    return got, lax.ppermute(got, "dap", [(at, at ^ 1) for at in range(devices)])


def halves(row):
    return [pltpu.roll(row, LANES // 2, 1), row]


def entry_kernel(x_hbm, cover_hbm, flag_hbm, weight_hbm, out_ref, x_ref, cover_ref, flag_ref, weight_ref, sems):
    copies = start_copies(
        [(x_hbm, x_ref), (weight_hbm, weight_ref), (cover_hbm, cover_ref), (flag_hbm, flag_ref)], sems
    )
    for copy in copies:
        copy.wait()
    held, cols, _ = x_ref.shape
    width = weight_ref.shape[1]
    pairs = out_ref.shape[0]
    cover = cover_ref[...].astype(F32)
    columns = jnp.transpose(jnp.concatenate([cover, jnp.zeros((8 - held, cols), F32)], axis=0))
    blank = jnp.zeros_like(weight_ref[0])
    own = jnp.zeros((cols, LANES), F32)
    marks = []
    for s in range(held):
        marks += halves(cover[s : s + 1])
    marks += halves(flag_ref[...].astype(F32))
    marks = jnp.concatenate(marks + [jnp.zeros((8 - len(marks), cols), F32)], axis=0)
    for s in range(held):
        normalized = norm(x_ref[s].astype(F32), -1)
        shared = (dot(weight_ref[1], normalized, 1, 1) * cover[s : s + 1]).astype(BF16)
        for pair in range(pairs):
            out_ref[pair, s * width : (s + 1) * width, :] = shared
        weight = jnp.concatenate([weight_ref[0] if at == s else blank for at in range(LANES // width)], axis=0)
        own = own + dot(normalized, weight, 1, 1) * columns[:, s : s + 1]
    lane = lax.broadcasted_iota(jnp.int32, (16, LANES), 1)
    marks = jnp.concatenate([marks, marks], axis=0)
    for pair in range(pairs):
        block = jnp.where(lane < held * width, own[pair * 16 : pair * 16 + 16], marks)
        out_ref[pair, held * width :, :] = block.astype(BF16)


def flat(rows):
    return jnp.concatenate([rows[row : row + 1] for row in range(rows.shape[0])], axis=1)


def project(pair, weights, mask_ref, out_ref, gate_ref):
    size = pair.shape[0]
    rows, cols = mask_ref.shape
    share = size // out_ref.shape[0]
    entries = dot(weights, norm(pair, 0))
    entries = [entries[k * size : (k + 1) * size] for k in range(5)]
    mask = flat(mask_ref[...])
    left, right = (sigmoid(entries[k]) * entries[k + 1] * mask for k in (0, 2))
    gate_ref[...] = sigmoid(entries[4])
    for peer in range(out_ref.shape[0]):
        for row in range(rows):
            block = [side[peer * share : (peer + 1) * share, row * cols : (row + 1) * cols] for side in (left, right)]
            at = row * 2 * share
            out_ref[peer, at : at + 2 * share, :] = jnp.concatenate(block, axis=0).astype(BF16)


def weight_kernel(entry_ref, exit_ref, out_entry, out_exit, rows_ref):
    for t in range(entry_ref.shape[0]):
        for k in range(entry_ref.shape[1]):
            out_entry[t, k * LANES : (k + 1) * LANES, :] = jnp.transpose(entry_ref[t, k])
    width = 32
    rows_ref[...] = exit_ref[...].astype(F32)
    leave = jnp.concatenate([rows_ref[pl.ds(e, width, stride=width), :] for e in range(width)], axis=0)
    out_exit[...] = jnp.transpose(leave).astype(BF16)


def outer_kernel(
    got_ref, other_ref, couple_ref, exit_ref, weight_ref,
    out_ref, pair_ref, gate_ref, mask_ref,
    shared_ref, aux_ref, outer_ref,
):
    pairs, _, cols = got_ref.shape
    devices = 2 * pairs
    rows = couple_ref.shape[0]
    held, width = 2, 32
    core = lax.rem(lax.axis_index("dap"), 2)
    for side, ref in enumerate((got_ref, other_ref)):
        shared = ref[:, : held * width, :].astype(F32).reshape(pairs * held * width, cols)
        shared_ref[side * pairs * held * width : (side + 1) * pairs * held * width, :] = shared
        aux = ref[:, held * width :, :].astype(F32)
        aux = jnp.where(core == 0, aux[:, :8], aux[:, 8:])
        aux_ref[side * pairs * 8 : (side + 1) * pairs * 8, :] = aux.reshape(pairs * 8, cols)
    lane = lax.broadcasted_iota(jnp.int32, (devices, LANES), 1)
    marks = []
    for row in range(0, 2 * held + 2, 2):
        low = aux_ref[pl.ds(row, devices, stride=8), :]
        high = aux_ref[pl.ds(row + 1, devices, stride=8), :]
        marks.append(jnp.where(lane < LANES // 2, pltpu.roll(low, LANES // 2, 1), high))
    cover = jnp.concatenate(marks[:held], axis=0).astype(BF16)
    flags = marks[held][0:1]
    chosen = lax.broadcasted_iota(jnp.int32, (rows, LANES), 1) == (
        lax.broadcasted_iota(jnp.int32, (rows, LANES), 0) + lax.axis_index("dap") * rows
    )
    cover_rows = dot(chosen.astype(BF16), cover, 1, 1).astype(BF16)
    scale = 1.0 / dot(cover_rows, cover)
    mask_ref[...] = jnp.sum(jnp.where(chosen, flags, 0.0), axis=1, keepdims=True) * flags
    per_tile = LANES // width
    tiles = []
    for tile in range(rows // per_tile):
        sides = [jnp.zeros((devices, LANES), F32) for _ in range(held)]
        for place in range(per_tile):
            values = aux_ref[pl.ds(tile * per_tile + place, devices, stride=8), :]
            here = (lane >= place * width) & (lane < (place + 1) * width)
            for s in range(held):
                turn = ((place - s) * width) % LANES
                moved = pltpu.roll(values, turn, 1) if turn else values
                sides[s] = jnp.where(here, moved, sides[s])
        tiles.append(jnp.concatenate(sides, axis=0))
    own = jnp.transpose(jnp.concatenate(tiles, axis=1)).astype(BF16)
    for e in range(0, width, 2):
        parts = []
        for step in range(2):
            parts.append(
                jnp.concatenate(
                    [
                        shared_ref[pl.ds(s * width + e + step, devices, stride=held * width), :]
                        for s in range(held)
                    ],
                    axis=0,
                )
            )
        result = dot(own, jnp.concatenate(parts, axis=1).astype(BF16)).astype(BF16)
        for step in range(2):
            for i in range(rows):
                outer_ref[(e + step) * width : (e + step + 1) * width, i * cols : (i + 1) * cols] = result[
                    i * width : (i + 1) * width, step * cols : (step + 1) * cols
                ]
    couple = jnp.concatenate([jnp.transpose(couple_ref[row]) for row in range(rows)], axis=1)
    pair = (couple.astype(F32) + dot(exit_ref[...], outer_ref[...]) * flat(scale)).astype(BF16)
    pair_ref[...] = pair
    project(pair.astype(F32), weight_ref[0], mask_ref, out_ref, gate_ref)


def product_kernel(incoming, got_ref, out_ref, sides_ref, products_ref):
    devices, _, cols = got_ref.shape
    part = 8
    total = sides_ref.shape[0] // (2 * part)
    sides_ref[...] = got_ref[...].astype(F32).reshape(total * 2 * part, cols)
    for h in range(part):
        left = sides_ref[pl.ds(h, total, stride=2 * part), :].astype(BF16)
        right = sides_ref[pl.ds(part + h, total, stride=2 * part), :].astype(BF16)
        result = dot(left, right, 0, 0) if incoming else dot(left, right, 1, 1)
        products_ref[pl.ds(h, total, stride=part), :] = result
    out_ref[...] = products_ref[...].astype(BF16).reshape(out_ref.shape)


def updated(got_ref, pair_ref, gate_ref, leave):
    devices, size, cols = got_ref.shape
    part = 8
    products = [
        got_ref[:, at : at + part, :].astype(F32).reshape(devices * part, cols) for at in range(0, size, part)
    ]
    update = dot(jnp.transpose(leave), norm(jnp.concatenate(products, axis=1), 0))
    return pair_ref[...].astype(F32) + gate_ref[...] * update


def middle_kernel(got_ref, pair_ref, gate_ref, leave_ref, weight_ref, mask_ref, out_ref, next_ref, next_gate_ref):
    pair = updated(got_ref, pair_ref, gate_ref, leave_ref[0]).astype(BF16)
    next_ref[...] = pair
    project(pair.astype(F32), weight_ref[1], mask_ref, out_ref, next_gate_ref)


def last_kernel(got_ref, pair_ref, gate_ref, leave_ref, out_hbm, out_ref, sems):
    rows, cols, _ = out_ref.shape
    pair = updated(got_ref, pair_ref, gate_ref, leave_ref[1])
    copies = []
    for row in range(rows):
        out_ref[row] = jnp.transpose(pair[:, row * cols : (row + 1) * cols]).astype(BF16)
        if row % 4 == 3:
            part = pl.ds(row - 3, 4)
            copies.append(pltpu.make_async_copy(out_ref.at[part], out_hbm.at[part], sems.at[row // 4]))
            copies[-1].start()
    for copy in copies:
        copy.wait()


def call(kernel, inputs, outputs, scratch=(), in_specs=None, out_specs=None, limit=40):
    return pl.pallas_call(
        kernel,
        out_shape=outputs,
        in_specs=in_specs or [VMEM] * len(inputs),
        out_specs=out_specs or [VMEM] * len(outputs),
        scratch_shapes=list(scratch),
        compiler_params=pltpu.CompilerParams(vmem_limit_bytes=limit * 1024 * 1024),
    )(*inputs)


def shape(dims, kind=BF16):
    return jax.ShapeDtypeStruct(dims, kind)


def fast(
    devices,
    homolog_embedding,
    coverage_indicator,
    genuine_amino_flag,
    couple_embedding,
    pairing_entry_matrices,
    pairing_exit_matrix,
    trilateral_entry_matrices,
    trilateral_exit_matrices,
):
    rows, cols, channels = couple_embedding.shape
    held = homolog_embedding.shape[0]
    width = pairing_entry_matrices.shape[2]
    part = channels // devices
    (packed,) = call(
        entry_kernel,
        (
            homolog_embedding,
            coverage_indicator,
            genuine_amino_flag.reshape(1, cols),
            jnp.transpose(pairing_entry_matrices, (1, 2, 0)),
        ),
        [shape((devices // 2, held * width + 16, cols))],
        [
            pltpu.VMEM(homolog_embedding.shape, BF16),
            pltpu.VMEM(coverage_indicator.shape, jnp.int32),
            pltpu.VMEM((1, cols), jnp.int32),
            pltpu.VMEM((2, width, homolog_embedding.shape[2]), BF16),
            pltpu.SemaphoreType.DMA((4,)),
        ],
        [HBM] * 4,
        limit=60,
    )
    packed, entry, exit_rows = lax.optimization_barrier((packed, trilateral_entry_matrices, pairing_exit_matrix))
    got = two_level(packed, devices)
    entry, exit_matrix = call(
        weight_kernel,
        (jnp.transpose(entry, (0, 2, 1, 3)), exit_rows),
        [
            shape((2, 5 * channels, channels)),
            shape((channels, width * width)),
        ],
        [pltpu.VMEM((width * width, channels), F32)],
    )
    projected = [
        shape((devices, rows * 2 * part, cols)),
        shape((channels, rows * cols)),
        shape((channels, rows * cols), F32),
    ]
    both, pair, gate, row_mask = call(
        outer_kernel,
        (*got, couple_embedding, exit_matrix, entry),
        projected + [shape((rows, cols), F32)],
        [
            pltpu.VMEM((devices * held * width, cols), F32),
            pltpu.VMEM((devices * 8, cols), F32),
            pltpu.VMEM((width * width, rows * cols), BF16),
        ],
    )

    def multiply(both, incoming):
        (products,) = call(
            functools.partial(product_kernel, incoming),
            (exchange(both),),
            [shape((devices, rows * part, cols))],
            [pltpu.VMEM((devices * rows * 2 * part, cols), F32), pltpu.VMEM((devices * rows * part, cols), F32)],
        )
        return exchange(products)

    got = multiply(both, False)
    both, pair, gate = call(middle_kernel, (got, pair, gate, trilateral_exit_matrices, entry, row_mask), projected)
    got = multiply(both, True)
    (pair_out,) = call(
        last_kernel,
        (got, pair, gate, trilateral_exit_matrices),
        [shape((rows, cols, channels))],
        [pltpu.VMEM((rows, cols, channels), BF16), pltpu.SemaphoreType.DMA((rows // 4,))],
        out_specs=[HBM],
    )
    return pair_out


def fits(devices, homolog_embedding, couple_embedding, pairing_entry_matrices):
    rows, cols, channels = couple_embedding.shape
    return (
        devices % 2 == 0
        and homolog_embedding.shape[0] == 2
        and rows == 8
        and cols == LANES
        and channels == 8 * devices
        and channels == LANES
        and pairing_entry_matrices.shape[2] == 32
    )


def solution(mesh):
    devices = mesh.shape["dap"]

    def one_device(*arrays):
        chosen = fast if fits(devices, arrays[0], arrays[3], arrays[4]) else local
        return chosen(devices, *arrays)

    return jax.shard_map(
        one_device,
        mesh=mesh,
        in_specs=(
            P(("crops", "dap"), None, None),
            P(("crops", "dap"), None),
            P("crops"),
            P(("crops", "dap"), None, None),
            P(),
            P(),
            P(),
            P(),
        ),
        out_specs=P(("crops", "dap"), None, None),
        check_vma=False,
    )
```

```python
import functools

import jax
import jax.numpy as jnp
from jax import lax
from jax.experimental import pallas as pl
from jax.experimental.pallas import tpu as pltpu
from jax.sharding import PartitionSpec as P

F32 = jnp.float32
BF16 = jnp.bfloat16
EPS = 1e-05
LANES = 128
VMEM = pl.BlockSpec(memory_space=pltpu.VMEM)
HBM = pl.BlockSpec(memory_space=pltpu.HBM)


def dot(a, b, left=1, right=0):
    return lax.dot_general(a, b, (((left,), (right,)), ((), ())), preferred_element_type=F32)


def sigmoid(values):
    return 0.5 * jnp.tanh(0.5 * values) + 0.5


def norm(values, axis):
    size = values.shape[axis]
    average = jnp.sum(values, axis=axis, keepdims=True) * (1.0 / size)
    centered = values - average
    variance = jnp.sum(centered * centered, axis=axis, keepdims=True) * (1.0 / size)
    return (centered * lax.rsqrt(variance + EPS)).astype(BF16)


def standardize_features(values, axis):
    average = jnp.mean(values, axis=axis, keepdims=True)
    centered = values - average
    variance = jnp.mean(centered * centered, axis=axis, keepdims=True)
    return centered * lax.rsqrt(variance + 1e-05)


def exchange(blocks):
    return lax.all_to_all(blocks, "dap", split_axis=0, concat_axis=0, tiled=True)


def outer_update(left_local, mask_local, right_cols, mask_cols, couple_embedding, pairing_exit_matrix):
    proj_width = left_local.shape[1]
    local_rows = left_local.shape[2]
    col_total = right_cols.shape[2]
    outer = jnp.einsum("rzp,rej->pjze", left_local, right_cols, preferred_element_type=jnp.float32)
    outer = outer.astype(jnp.bfloat16).reshape(local_rows, col_total, proj_width * proj_width)
    pair_update = jnp.einsum("ijf,fc->ijc", outer, pairing_exit_matrix, preferred_element_type=jnp.float32)
    pair_count = jnp.einsum("si,sj->ij", mask_local, mask_cols, preferred_element_type=jnp.float32)
    return (couple_embedding.astype(jnp.float32) + pair_update / pair_count[:, :, None]).astype(jnp.bfloat16)


def triangle(pair_now, row_mask, weights, out_weight, incoming, devices):
    rows, cols, channels = pair_now.shape
    part = channels // devices
    normalized = standardize_features(pair_now.astype(jnp.float32), -1).astype(jnp.bfloat16)
    projections = jnp.einsum("ijc,ckh->khij", normalized, weights[:, :4], preferred_element_type=jnp.float32)
    left_proj = (jax.nn.sigmoid(projections[0]) * projections[1] * row_mask).astype(jnp.bfloat16)
    right_proj = (jax.nn.sigmoid(projections[2]) * projections[3] * row_mask).astype(jnp.bfloat16)
    gate_val = jax.nn.sigmoid(
        jnp.einsum("ijc,ch->ijh", normalized, weights[:, 4], preferred_element_type=jnp.float32)
    )
    both = jnp.stack(
        [left_proj.reshape(devices, part, rows, cols), right_proj.reshape(devices, part, rows, cols)], axis=1
    )
    both = exchange(both)
    both = jnp.transpose(both, (1, 2, 0, 3, 4)).reshape(2, part, devices * rows, cols)
    einsum_form = "hki,hkj->hij" if incoming else "hik,hjk->hij"
    products = jnp.einsum(einsum_form, both[0], both[1], preferred_element_type=jnp.float32).astype(jnp.bfloat16)
    products = jnp.transpose(products.reshape(part, devices, rows, cols), (1, 0, 2, 3))
    returned = exchange(products).reshape(channels, rows, cols)
    normed_products = standardize_features(returned.astype(jnp.float32), 0).astype(jnp.bfloat16)
    pair_update = jnp.einsum("hij,hc->ijc", normed_products, out_weight, preferred_element_type=jnp.float32)
    return (pair_now.astype(jnp.float32) + gate_val * pair_update).astype(jnp.bfloat16)


def local(
    devices,
    homolog_embedding,
    coverage_indicator,
    genuine_amino_flag,
    couple_embedding,
    pairing_entry_matrices,
    pairing_exit_matrix,
    trilateral_entry_matrices,
    trilateral_exit_matrices,
):
    rows, cols, _ = couple_embedding.shape
    held = homolog_embedding.shape[0]
    width = pairing_entry_matrices.shape[2]
    sequence_mask = coverage_indicator.astype(jnp.float32)
    msa_norm = standardize_features(homolog_embedding.astype(jnp.float32), -1).astype(jnp.bfloat16)
    entries = jnp.einsum("rgl,loe->roeg", msa_norm, pairing_entry_matrices, preferred_element_type=jnp.float32)
    entries = (entries * sequence_mask[:, None, None, :]).astype(jnp.bfloat16)
    own = jnp.transpose(entries[:, 0].reshape(held, width, devices, rows), (2, 0, 1, 3))
    shared = jnp.concatenate([entries[:, 1].reshape(held, width * cols), sequence_mask.astype(jnp.bfloat16)], axis=1)
    packed = jnp.concatenate(
        [jnp.broadcast_to(shared[None], (devices,) + shared.shape), own.reshape(devices, held, width * rows)], axis=2
    )
    packed = exchange(packed).reshape(devices * held, -1)
    right_cols = packed[:, : width * cols].reshape(-1, width, cols)
    mask_cols = packed[:, width * cols : (width + 1) * cols]
    left_local = packed[:, (width + 1) * cols :].reshape(-1, width, rows)
    first_row = lax.axis_index("dap") * rows
    mask_local = lax.dynamic_slice_in_dim(mask_cols, first_row, rows, 1)
    pair_one = outer_update(left_local, mask_local, right_cols, mask_cols, couple_embedding, pairing_exit_matrix)
    residues = genuine_amino_flag.astype(jnp.float32)
    row_mask = lax.dynamic_slice_in_dim(residues, first_row, rows, 0)[:, None] * residues[None, :]
    pair_two = triangle(
        pair_one, row_mask, trilateral_entry_matrices[0], trilateral_exit_matrices[0], False, devices
    )
    return triangle(pair_two, row_mask, trilateral_entry_matrices[1], trilateral_exit_matrices[1], True, devices)


def start_copies(pairs, sems):
    copies = [pltpu.make_async_copy(source, target, sems.at[at]) for at, (source, target) in enumerate(pairs)]
    for copy in copies:
        copy.start()
    return copies


def two_level(blocks, devices):
    groups = [list(range(parity, devices, 2)) for parity in range(2)]
    got = lax.all_to_all(blocks, "dap", split_axis=0, concat_axis=0, tiled=True, axis_index_groups=groups)
    return got, lax.ppermute(got, "dap", [(at, at ^ 1) for at in range(devices)])


def halves(row):
    return [pltpu.roll(row, LANES // 2, 1), row]


def entry_kernel(x_hbm, cover_hbm, flag_hbm, weight_hbm, out_ref, x_ref, cover_ref, flag_ref, weight_ref, sems):
    copies = start_copies(
        [(x_hbm, x_ref), (weight_hbm, weight_ref), (cover_hbm, cover_ref), (flag_hbm, flag_ref)], sems
    )
    for copy in copies:
        copy.wait()
    held, cols, _ = x_ref.shape
    width = weight_ref.shape[1]
    pairs = out_ref.shape[0]
    cover = cover_ref[...].astype(F32)
    columns = jnp.transpose(jnp.concatenate([cover, jnp.zeros((8 - held, cols), F32)], axis=0))
    blank = jnp.zeros_like(weight_ref[0])
    own = jnp.zeros((cols, LANES), F32)
    marks = []
    for s in range(held):
        marks += halves(cover[s : s + 1])
    marks += halves(flag_ref[...].astype(F32))
    marks = jnp.concatenate(marks + [jnp.zeros((8 - len(marks), cols), F32)], axis=0)
    for s in range(held):
        normalized = norm(x_ref[s].astype(F32), -1)
        shared = (dot(weight_ref[1], normalized, 1, 1) * cover[s : s + 1]).astype(BF16)
        for pair in range(pairs):
            out_ref[pair, s * width : (s + 1) * width, :] = shared
        weight = jnp.concatenate([weight_ref[0] if at == s else blank for at in range(LANES // width)], axis=0)
        own = own + dot(normalized, weight, 1, 1) * columns[:, s : s + 1]
    lane = lax.broadcasted_iota(jnp.int32, (16, LANES), 1)
    marks = jnp.concatenate([marks, marks], axis=0)
    for pair in range(pairs):
        block = jnp.where(lane < held * width, own[pair * 16 : pair * 16 + 16], marks)
        out_ref[pair, held * width :, :] = block.astype(BF16)


def flat(rows):
    return jnp.concatenate([rows[row : row + 1] for row in range(rows.shape[0])], axis=1)


def project(pair, weights, mask_ref, out_ref, gate_ref):
    size = pair.shape[0]
    rows, cols = mask_ref.shape
    share = size // out_ref.shape[0]
    entries = dot(weights, norm(pair, 0))
    entries = [entries[k * size : (k + 1) * size] for k in range(5)]
    mask = flat(mask_ref[...])
    left, right = (sigmoid(entries[k]) * entries[k + 1] * mask for k in (0, 2))
    gate_ref[...] = sigmoid(entries[4])
    for peer in range(out_ref.shape[0]):
        for row in range(rows):
            block = [side[peer * share : (peer + 1) * share, row * cols : (row + 1) * cols] for side in (left, right)]
            at = row * 2 * share
            out_ref[peer, at : at + 2 * share, :] = jnp.concatenate(block, axis=0).astype(BF16)


def weight_kernel(entry_ref, exit_ref, out_entry, out_exit, rows_ref):
    for t in range(entry_ref.shape[0]):
        for k in range(entry_ref.shape[1]):
            out_entry[t, k * LANES : (k + 1) * LANES, :] = jnp.transpose(entry_ref[t, k])
    width = 32
    rows_ref[...] = exit_ref[...].astype(F32)
    leave = jnp.concatenate([rows_ref[pl.ds(e, width, stride=width), :] for e in range(width)], axis=0)
    out_exit[...] = jnp.transpose(leave).astype(BF16)


def outer_kernel(
    got_ref, other_ref, couple_ref, exit_ref, weight_ref,
    out_ref, pair_ref, gate_ref, mask_ref,
    shared_ref, aux_ref, outer_ref,
):
    pairs, _, cols = got_ref.shape
    devices = 2 * pairs
    rows = couple_ref.shape[0]
    held, width = 2, 32
    core = lax.rem(lax.axis_index("dap"), 2)
    for side, ref in enumerate((got_ref, other_ref)):
        shared = ref[:, : held * width, :].astype(F32).reshape(pairs * held * width, cols)
        shared_ref[side * pairs * held * width : (side + 1) * pairs * held * width, :] = shared
        aux = ref[:, held * width :, :].astype(F32)
        aux = jnp.where(core == 0, aux[:, :8], aux[:, 8:])
        aux_ref[side * pairs * 8 : (side + 1) * pairs * 8, :] = aux.reshape(pairs * 8, cols)
    lane = lax.broadcasted_iota(jnp.int32, (devices, LANES), 1)
    marks = []
    for row in range(0, 2 * held + 2, 2):
        low = aux_ref[pl.ds(row, devices, stride=8), :]
        high = aux_ref[pl.ds(row + 1, devices, stride=8), :]
        marks.append(jnp.where(lane < LANES // 2, pltpu.roll(low, LANES // 2, 1), high))
    cover = jnp.concatenate(marks[:held], axis=0).astype(BF16)
    flags = marks[held][0:1]
    chosen = lax.broadcasted_iota(jnp.int32, (rows, LANES), 1) == (
        lax.broadcasted_iota(jnp.int32, (rows, LANES), 0) + lax.axis_index("dap") * rows
    )
    cover_rows = dot(chosen.astype(BF16), cover, 1, 1).astype(BF16)
    scale = 1.0 / dot(cover_rows, cover)
    mask_ref[...] = jnp.sum(jnp.where(chosen, flags, 0.0), axis=1, keepdims=True) * flags
    per_tile = LANES // width
    tiles = []
    for tile in range(rows // per_tile):
        sides = [jnp.zeros((devices, LANES), F32) for _ in range(held)]
        for place in range(per_tile):
            values = aux_ref[pl.ds(tile * per_tile + place, devices, stride=8), :]
            here = (lane >= place * width) & (lane < (place + 1) * width)
            for s in range(held):
                turn = ((place - s) * width) % LANES
                moved = pltpu.roll(values, turn, 1) if turn else values
                sides[s] = jnp.where(here, moved, sides[s])
        tiles.append(jnp.concatenate(sides, axis=0))
    own = jnp.transpose(jnp.concatenate(tiles, axis=1)).astype(BF16)
    for e in range(0, width, 2):
        parts = []
        for step in range(2):
            parts.append(
                jnp.concatenate(
                    [
                        shared_ref[pl.ds(s * width + e + step, devices, stride=held * width), :]
                        for s in range(held)
                    ],
                    axis=0,
                )
            )
        result = dot(own, jnp.concatenate(parts, axis=1).astype(BF16)).astype(BF16)
        for step in range(2):
            for i in range(rows):
                outer_ref[(e + step) * width : (e + step + 1) * width, i * cols : (i + 1) * cols] = result[
                    i * width : (i + 1) * width, step * cols : (step + 1) * cols
                ]
    couple = jnp.concatenate([jnp.transpose(couple_ref[row]) for row in range(rows)], axis=1)
    pair = (couple.astype(F32) + dot(exit_ref[...], outer_ref[...]) * flat(scale)).astype(BF16)
    pair_ref[...] = pair
    project(pair.astype(F32), weight_ref[0], mask_ref, out_ref, gate_ref)


def product_kernel(incoming, got_ref, out_ref, sides_ref, products_ref):
    cols = got_ref.shape[-1]
    part = products_ref.shape[0] // cols
    total = sides_ref.shape[0] // (2 * part)
    sides_ref[...] = got_ref[...].astype(F32).reshape(total * 2 * part, cols)
    for h in range(part):
        left = sides_ref[pl.ds(h, total, stride=2 * part), :].astype(BF16)
        right = sides_ref[pl.ds(part + h, total, stride=2 * part), :].astype(BF16)
        result = dot(left, right, 0, 0) if incoming else dot(left, right, 1, 1)
        products_ref[pl.ds(h, cols, stride=part), :] = result
    out_ref[...] = products_ref[...].astype(BF16).reshape(out_ref.shape)


def updated(got_ref, pair_ref, gate_ref, leave, parts):
    devices, size, cols = got_ref.shape
    senders = devices // parts
    share = leave.shape[0] // senders
    products = []
    for at in range(0, size, share):
        got = got_ref[:, at : at + share, :].astype(F32)
        got = sum(got[begin : begin + senders] for begin in range(0, devices, senders))
        products.append(got.reshape(senders * share, cols))
    update = dot(jnp.transpose(leave), norm(jnp.concatenate(products, axis=1), 0))
    return pair_ref[...].astype(F32) + gate_ref[...] * update


def middle_kernel(got_ref, pair_ref, gate_ref, leave_ref, weight_ref, mask_ref, out_ref, next_ref, next_gate_ref):
    pair = updated(got_ref, pair_ref, gate_ref, leave_ref[0], 1).astype(BF16)
    next_ref[...] = pair
    project(pair.astype(F32), weight_ref[1], mask_ref, out_ref, next_gate_ref)


def last_kernel(got_ref, pair_ref, gate_ref, leave_ref, out_hbm, out_ref, sems):
    rows, cols, _ = out_ref.shape
    pair = updated(got_ref, pair_ref, gate_ref, leave_ref[1], 2)
    copies = []
    for row in range(rows):
        out_ref[row] = jnp.transpose(pair[:, row * cols : (row + 1) * cols]).astype(BF16)
        if row % 4 == 3:
            part = pl.ds(row - 3, 4)
            copies.append(pltpu.make_async_copy(out_ref.at[part], out_hbm.at[part], sems.at[row // 4]))
            copies[-1].start()
    for copy in copies:
        copy.wait()


def call(kernel, inputs, outputs, scratch=(), in_specs=None, out_specs=None, limit=40):
    return pl.pallas_call(
        kernel,
        out_shape=outputs,
        in_specs=in_specs or [VMEM] * len(inputs),
        out_specs=out_specs or [VMEM] * len(outputs),
        scratch_shapes=list(scratch),
        compiler_params=pltpu.CompilerParams(vmem_limit_bytes=limit * 1024 * 1024),
    )(*inputs)


def shape(dims, kind=BF16):
    return jax.ShapeDtypeStruct(dims, kind)


def fast(
    devices,
    homolog_embedding,
    coverage_indicator,
    genuine_amino_flag,
    couple_embedding,
    pairing_entry_matrices,
    pairing_exit_matrix,
    trilateral_entry_matrices,
    trilateral_exit_matrices,
):
    rows, cols, channels = couple_embedding.shape
    held = homolog_embedding.shape[0]
    width = pairing_entry_matrices.shape[2]
    part = channels // devices
    (packed,) = call(
        entry_kernel,
        (
            homolog_embedding,
            coverage_indicator,
            genuine_amino_flag.reshape(1, cols),
            jnp.transpose(pairing_entry_matrices, (1, 2, 0)),
        ),
        [shape((devices // 2, held * width + 16, cols))],
        [
            pltpu.VMEM(homolog_embedding.shape, BF16),
            pltpu.VMEM(coverage_indicator.shape, jnp.int32),
            pltpu.VMEM((1, cols), jnp.int32),
            pltpu.VMEM((2, width, homolog_embedding.shape[2]), BF16),
            pltpu.SemaphoreType.DMA((4,)),
        ],
        [HBM] * 4,
        limit=60,
    )
    packed, entry, exit_rows = lax.optimization_barrier((packed, trilateral_entry_matrices, pairing_exit_matrix))
    got = two_level(packed, devices)
    entry, exit_matrix = call(
        weight_kernel,
        (jnp.transpose(entry, (0, 2, 1, 3)), exit_rows),
        [
            shape((2, 5 * channels, channels)),
            shape((channels, width * width)),
        ],
        [pltpu.VMEM((width * width, channels), F32)],
    )
    def projected(peers):
        return [
            shape((peers, devices * rows * 2 * part // peers, cols)),
            shape((channels, rows * cols)),
            shape((channels, rows * cols), F32),
        ]

    both, pair, gate, row_mask = call(
        outer_kernel,
        (*got, couple_embedding, exit_matrix, entry),
        projected(devices) + [shape((rows, cols), F32)],
        [
            pltpu.VMEM((devices * held * width, cols), F32),
            pltpu.VMEM((devices * 8, cols), F32),
            pltpu.VMEM((width * width, rows * cols), BF16),
        ],
    )

    def multiply(both, incoming, part):
        (products,) = call(
            functools.partial(product_kernel, incoming),
            (both,),
            [shape((devices, rows * part, cols))],
            [pltpu.VMEM((both.size // cols, cols), F32), pltpu.VMEM((devices * rows * part, cols), F32)],
        )
        return exchange(products)

    got = multiply(exchange(both), False, part)
    both, pair, gate = call(
        middle_kernel, (got, pair, gate, trilateral_exit_matrices, entry, row_mask), projected(devices // 2)
    )
    halves_of = [list(range(begin, begin + devices // 2)) for begin in (0, devices // 2)]
    both = lax.all_to_all(both, "dap", split_axis=0, concat_axis=0, tiled=True, axis_index_groups=halves_of)
    got = multiply(both, True, 2 * part)
    (pair_out,) = call(
        last_kernel,
        (got, pair, gate, trilateral_exit_matrices),
        [shape((rows, cols, channels))],
        [pltpu.VMEM((rows, cols, channels), BF16), pltpu.SemaphoreType.DMA((rows // 4,))],
        out_specs=[HBM],
    )
    return pair_out


def fits(devices, homolog_embedding, couple_embedding, pairing_entry_matrices):
    rows, cols, channels = couple_embedding.shape
    return (
        devices % 2 == 0
        and homolog_embedding.shape[0] == 2
        and rows == 8
        and cols == LANES
        and channels == 8 * devices
        and channels == LANES
        and pairing_entry_matrices.shape[2] == 32
    )


def solution(mesh):
    devices = mesh.shape["dap"]

    def one_device(*arrays):
        chosen = fast if fits(devices, arrays[0], arrays[3], arrays[4]) else local
        return chosen(devices, *arrays)

    return jax.shard_map(
        one_device,
        mesh=mesh,
        in_specs=(
            P(("crops", "dap"), None, None),
            P(("crops", "dap"), None),
            P("crops"),
            P(("crops", "dap"), None, None),
            P(),
            P(),
            P(),
            P(),
        ),
        out_specs=P(("crops", "dap"), None, None),
        check_vma=False,
    )
```

```python
import jax
import jax.numpy as jnp
from jax import lax
from jax.experimental import pallas as pl
from jax.experimental.pallas import tpu as pltpu
from jax.sharding import PartitionSpec as P

F32 = jnp.float32
BF16 = jnp.bfloat16
EPS = 1e-05
LANES = 128
VMEM = pl.BlockSpec(memory_space=pltpu.VMEM)
HBM = pl.BlockSpec(memory_space=pltpu.HBM)


def dot(a, b, left=1, right=0):
    return lax.dot_general(a, b, (((left,), (right,)), ((), ())), preferred_element_type=F32)


def sigmoid(values):
    return 0.5 * jnp.tanh(0.5 * values) + 0.5


def norm(values, axis):
    size = values.shape[axis]
    average = jnp.sum(values, axis=axis, keepdims=True) * (1.0 / size)
    centered = values - average
    variance = jnp.sum(centered * centered, axis=axis, keepdims=True) * (1.0 / size)
    return (centered * lax.rsqrt(variance + EPS)).astype(BF16)


def standardize_features(values, axis):
    average = jnp.mean(values, axis=axis, keepdims=True)
    centered = values - average
    variance = jnp.mean(centered * centered, axis=axis, keepdims=True)
    return centered * lax.rsqrt(variance + 1e-05)


def exchange(blocks):
    return lax.all_to_all(blocks, "dap", split_axis=0, concat_axis=0, tiled=True)


def outer_update(left_local, mask_local, right_cols, mask_cols, couple_embedding, pairing_exit_matrix):
    proj_width = left_local.shape[1]
    local_rows = left_local.shape[2]
    col_total = right_cols.shape[2]
    outer = jnp.einsum("rzp,rej->pjze", left_local, right_cols, preferred_element_type=jnp.float32)
    outer = outer.astype(jnp.bfloat16).reshape(local_rows, col_total, proj_width * proj_width)
    pair_update = jnp.einsum("ijf,fc->ijc", outer, pairing_exit_matrix, preferred_element_type=jnp.float32)
    pair_count = jnp.einsum("si,sj->ij", mask_local, mask_cols, preferred_element_type=jnp.float32)
    return (couple_embedding.astype(jnp.float32) + pair_update / pair_count[:, :, None]).astype(jnp.bfloat16)


def triangle(pair_now, row_mask, weights, out_weight, incoming, devices):
    rows, cols, channels = pair_now.shape
    part = channels // devices
    normalized = standardize_features(pair_now.astype(jnp.float32), -1).astype(jnp.bfloat16)
    projections = jnp.einsum("ijc,ckh->khij", normalized, weights[:, :4], preferred_element_type=jnp.float32)
    left_proj = (jax.nn.sigmoid(projections[0]) * projections[1] * row_mask).astype(jnp.bfloat16)
    right_proj = (jax.nn.sigmoid(projections[2]) * projections[3] * row_mask).astype(jnp.bfloat16)
    gate_val = jax.nn.sigmoid(
        jnp.einsum("ijc,ch->ijh", normalized, weights[:, 4], preferred_element_type=jnp.float32)
    )
    both = jnp.stack(
        [left_proj.reshape(devices, part, rows, cols), right_proj.reshape(devices, part, rows, cols)], axis=1
    )
    both = exchange(both)
    both = jnp.transpose(both, (1, 2, 0, 3, 4)).reshape(2, part, devices * rows, cols)
    einsum_form = "hki,hkj->hij" if incoming else "hik,hjk->hij"
    products = jnp.einsum(einsum_form, both[0], both[1], preferred_element_type=jnp.float32).astype(jnp.bfloat16)
    products = jnp.transpose(products.reshape(part, devices, rows, cols), (1, 0, 2, 3))
    returned = exchange(products).reshape(channels, rows, cols)
    normed_products = standardize_features(returned.astype(jnp.float32), 0).astype(jnp.bfloat16)
    pair_update = jnp.einsum("hij,hc->ijc", normed_products, out_weight, preferred_element_type=jnp.float32)
    return (pair_now.astype(jnp.float32) + gate_val * pair_update).astype(jnp.bfloat16)


def local(
    devices,
    homolog_embedding,
    coverage_indicator,
    genuine_amino_flag,
    couple_embedding,
    pairing_entry_matrices,
    pairing_exit_matrix,
    trilateral_entry_matrices,
    trilateral_exit_matrices,
):
    rows, cols, _ = couple_embedding.shape
    held = homolog_embedding.shape[0]
    width = pairing_entry_matrices.shape[2]
    sequence_mask = coverage_indicator.astype(jnp.float32)
    msa_norm = standardize_features(homolog_embedding.astype(jnp.float32), -1).astype(jnp.bfloat16)
    entries = jnp.einsum("rgl,loe->roeg", msa_norm, pairing_entry_matrices, preferred_element_type=jnp.float32)
    entries = (entries * sequence_mask[:, None, None, :]).astype(jnp.bfloat16)
    own = jnp.transpose(entries[:, 0].reshape(held, width, devices, rows), (2, 0, 1, 3))
    shared = jnp.concatenate([entries[:, 1].reshape(held, width * cols), sequence_mask.astype(jnp.bfloat16)], axis=1)
    packed = jnp.concatenate(
        [jnp.broadcast_to(shared[None], (devices,) + shared.shape), own.reshape(devices, held, width * rows)], axis=2
    )
    packed = exchange(packed).reshape(devices * held, -1)
    right_cols = packed[:, : width * cols].reshape(-1, width, cols)
    mask_cols = packed[:, width * cols : (width + 1) * cols]
    left_local = packed[:, (width + 1) * cols :].reshape(-1, width, rows)
    first_row = lax.axis_index("dap") * rows
    mask_local = lax.dynamic_slice_in_dim(mask_cols, first_row, rows, 1)
    pair_one = outer_update(left_local, mask_local, right_cols, mask_cols, couple_embedding, pairing_exit_matrix)
    residues = genuine_amino_flag.astype(jnp.float32)
    row_mask = lax.dynamic_slice_in_dim(residues, first_row, rows, 0)[:, None] * residues[None, :]
    pair_two = triangle(
        pair_one, row_mask, trilateral_entry_matrices[0], trilateral_exit_matrices[0], False, devices
    )
    return triangle(pair_two, row_mask, trilateral_entry_matrices[1], trilateral_exit_matrices[1], True, devices)


def start_copies(pairs, sems):
    copies = [pltpu.make_async_copy(source, target, sems.at[at]) for at, (source, target) in enumerate(pairs)]
    for copy in copies:
        copy.start()
    return copies


def two_level(blocks, devices):
    groups = [list(range(parity, devices, 2)) for parity in range(2)]
    got = lax.all_to_all(blocks, "dap", split_axis=0, concat_axis=0, tiled=True, axis_index_groups=groups)
    return got, lax.ppermute(got, "dap", [(at, at ^ 1) for at in range(devices)])


def halves(row):
    return [pltpu.roll(row, LANES // 2, 1), row]


def entry_kernel(x_hbm, cover_hbm, flag_hbm, weight_hbm, out_ref, x_ref, cover_ref, flag_ref, weight_ref, sems):
    copies = start_copies(
        [(x_hbm, x_ref), (weight_hbm, weight_ref), (cover_hbm, cover_ref), (flag_hbm, flag_ref)], sems
    )
    for copy in copies:
        copy.wait()
    held, cols, _ = x_ref.shape
    width = weight_ref.shape[1]
    pairs = out_ref.shape[0]
    cover = cover_ref[...].astype(F32)
    columns = jnp.transpose(jnp.concatenate([cover, jnp.zeros((8 - held, cols), F32)], axis=0))
    blank = jnp.zeros_like(weight_ref[0])
    own = jnp.zeros((cols, LANES), F32)
    marks = []
    for s in range(held):
        marks += halves(cover[s : s + 1])
    marks += halves(flag_ref[...].astype(F32))
    marks = jnp.concatenate(marks + [jnp.zeros((8 - len(marks), cols), F32)], axis=0)
    for s in range(held):
        normalized = norm(x_ref[s].astype(F32), -1)
        shared = (dot(weight_ref[1], normalized, 1, 1) * cover[s : s + 1]).astype(BF16)
        for pair in range(pairs):
            out_ref[pair, s * width : (s + 1) * width, :] = shared
        weight = jnp.concatenate([weight_ref[0] if at == s else blank for at in range(LANES // width)], axis=0)
        own = own + dot(normalized, weight, 1, 1) * columns[:, s : s + 1]
    lane = lax.broadcasted_iota(jnp.int32, (16, LANES), 1)
    marks = jnp.concatenate([marks, marks], axis=0)
    for pair in range(pairs):
        block = jnp.where(lane < held * width, own[pair * 16 : pair * 16 + 16], marks)
        out_ref[pair, held * width :, :] = block.astype(BF16)


def flat(rows):
    return jnp.concatenate([rows[row : row + 1] for row in range(rows.shape[0])], axis=1)


def project(pair, weights, mask_ref, out_ref, gate_ref):
    size = pair.shape[0]
    rows, cols = mask_ref.shape
    share = size // out_ref.shape[0]
    entries = dot(weights, norm(pair, 0))
    entries = [entries[k * size : (k + 1) * size] for k in range(5)]
    mask = flat(mask_ref[...])
    left, right = (sigmoid(entries[k]) * entries[k + 1] * mask for k in (0, 2))
    gate_ref[...] = sigmoid(entries[4])
    for peer in range(out_ref.shape[0]):
        for row in range(rows):
            block = [side[peer * share : (peer + 1) * share, row * cols : (row + 1) * cols] for side in (left, right)]
            at = row * 2 * share
            out_ref[peer, at : at + 2 * share, :] = jnp.concatenate(block, axis=0).astype(BF16)


def weight_kernel(entry_ref, exit_ref, out_entry, out_exit, rows_ref):
    for t in range(entry_ref.shape[0]):
        for k in range(entry_ref.shape[1]):
            out_entry[t, k * LANES : (k + 1) * LANES, :] = jnp.transpose(entry_ref[t, k])
    width = 32
    rows_ref[...] = exit_ref[...].astype(F32)
    leave = jnp.concatenate([rows_ref[pl.ds(e, width, stride=width), :] for e in range(width)], axis=0)
    out_exit[...] = jnp.transpose(leave).astype(BF16)


def outer_kernel(
    got_ref, other_ref, couple_ref, exit_ref, weight_ref,
    out_ref, pair_ref, gate_ref, mask_ref,
    shared_ref, aux_ref, outer_ref,
):
    pairs, _, cols = got_ref.shape
    devices = 2 * pairs
    rows = couple_ref.shape[0]
    held, width = 2, 32
    core = lax.rem(lax.axis_index("dap"), 2)
    for side, ref in enumerate((got_ref, other_ref)):
        shared = ref[:, : held * width, :].astype(F32).reshape(pairs * held * width, cols)
        shared_ref[side * pairs * held * width : (side + 1) * pairs * held * width, :] = shared
        aux = ref[:, held * width :, :].astype(F32)
        aux = jnp.where(core == 0, aux[:, :8], aux[:, 8:])
        aux_ref[side * pairs * 8 : (side + 1) * pairs * 8, :] = aux.reshape(pairs * 8, cols)
    lane = lax.broadcasted_iota(jnp.int32, (devices, LANES), 1)
    marks = []
    for row in range(0, 2 * held + 2, 2):
        low = aux_ref[pl.ds(row, devices, stride=8), :]
        high = aux_ref[pl.ds(row + 1, devices, stride=8), :]
        marks.append(jnp.where(lane < LANES // 2, pltpu.roll(low, LANES // 2, 1), high))
    cover = jnp.concatenate(marks[:held], axis=0).astype(BF16)
    flags = marks[held][0:1]
    chosen = lax.broadcasted_iota(jnp.int32, (rows, LANES), 1) == (
        lax.broadcasted_iota(jnp.int32, (rows, LANES), 0) + lax.axis_index("dap") * rows
    )
    cover_rows = dot(chosen.astype(BF16), cover, 1, 1).astype(BF16)
    scale = 1.0 / dot(cover_rows, cover)
    mask_ref[...] = jnp.sum(jnp.where(chosen, flags, 0.0), axis=1, keepdims=True) * flags
    per_tile = LANES // width
    tiles = []
    for tile in range(rows // per_tile):
        sides = [jnp.zeros((devices, LANES), F32) for _ in range(held)]
        for place in range(per_tile):
            values = aux_ref[pl.ds(tile * per_tile + place, devices, stride=8), :]
            here = (lane >= place * width) & (lane < (place + 1) * width)
            for s in range(held):
                turn = ((place - s) * width) % LANES
                moved = pltpu.roll(values, turn, 1) if turn else values
                sides[s] = jnp.where(here, moved, sides[s])
        tiles.append(jnp.concatenate(sides, axis=0))
    own = jnp.transpose(jnp.concatenate(tiles, axis=1)).astype(BF16)
    for e in range(0, width, 2):
        parts = []
        for step in range(2):
            parts.append(
                jnp.concatenate(
                    [
                        shared_ref[pl.ds(s * width + e + step, devices, stride=held * width), :]
                        for s in range(held)
                    ],
                    axis=0,
                )
            )
        result = dot(own, jnp.concatenate(parts, axis=1).astype(BF16)).astype(BF16)
        for step in range(2):
            for i in range(rows):
                outer_ref[(e + step) * width : (e + step + 1) * width, i * cols : (i + 1) * cols] = result[
                    i * width : (i + 1) * width, step * cols : (step + 1) * cols
                ]
    couple = jnp.concatenate([jnp.transpose(couple_ref[row]) for row in range(rows)], axis=1)
    pair = (couple.astype(F32) + dot(exit_ref[...], outer_ref[...]) * flat(scale)).astype(BF16)
    pair_ref[...] = pair
    project(pair.astype(F32), weight_ref[0], mask_ref, out_ref, gate_ref)


def side_rows(got_ref, sides_ref, part):
    sides_ref[...] = got_ref[...].astype(F32).reshape(sides_ref.shape)
    lines = sides_ref.shape[0] // (2 * part)
    return lambda h: sides_ref[pl.ds(h, lines, stride=2 * part), :].astype(BF16)


def outgoing_kernel(got_ref, out_ref, sides_ref, products_ref):
    cols = got_ref.shape[-1]
    part = products_ref.shape[0] // cols
    side = side_rows(got_ref, sides_ref, part)
    for h in range(part):
        products_ref[pl.ds(h, cols, stride=part), :] = dot(side(h), side(part + h), 1, 1)
    out_ref[...] = products_ref[...].astype(BF16).reshape(out_ref.shape)


def incoming_kernel(got_ref, out_ref, sides_ref):
    peers, size, cols = out_ref.shape
    rows = cols // peers
    part = size // rows
    side = side_rows(got_ref, sides_ref, part)
    for h in range(0, part, 2):
        results = [dot(side(at), side(part + at), 0, 0) for at in (h, h + 1)]
        for peer in range(peers):
            block = [result[peer * rows : (peer + 1) * rows] for result in results]
            out_ref[peer, h * rows : (h + 2) * rows, :] = jnp.concatenate(block, axis=0).astype(BF16)


def updated(products, pair_ref, gate_ref, leave):
    update = dot(jnp.transpose(leave), norm(jnp.concatenate(products, axis=1), 0))
    return pair_ref[...].astype(F32) + gate_ref[...] * update


def middle_kernel(got_ref, pair_ref, gate_ref, leave_ref, weight_ref, mask_ref, out_ref, next_ref, next_gate_ref):
    devices, size, cols = got_ref.shape
    part = size // mask_ref.shape[0]
    products = [
        got_ref[:, at : at + part, :].astype(F32).reshape(devices * part, cols) for at in range(0, size, part)
    ]
    pair = updated(products, pair_ref, gate_ref, leave_ref[0]).astype(BF16)
    next_ref[...] = pair
    project(pair.astype(F32), weight_ref[1], mask_ref, out_ref, next_gate_ref)


def last_kernel(got_ref, pair_ref, gate_ref, leave_ref, out_hbm, out_ref, sums_ref, sems):
    rows, cols, channels = out_ref.shape
    senders = got_ref.shape[0] // 2
    sums = got_ref[:senders].astype(F32) + got_ref[senders:].astype(F32)
    sums_ref[...] = sums.reshape(sums_ref.shape)
    products = [sums_ref[pl.ds(row, channels, stride=rows), :] for row in range(rows)]
    pair = updated(products, pair_ref, gate_ref, leave_ref[1])
    copies = []
    for row in range(rows):
        out_ref[row] = jnp.transpose(pair[:, row * cols : (row + 1) * cols]).astype(BF16)
        if row % 4 == 3:
            part = pl.ds(row - 3, 4)
            copies.append(pltpu.make_async_copy(out_ref.at[part], out_hbm.at[part], sems.at[row // 4]))
            copies[-1].start()
    for copy in copies:
        copy.wait()


def call(kernel, inputs, outputs, scratch=(), in_specs=None, out_specs=None, limit=40):
    return pl.pallas_call(
        kernel,
        out_shape=outputs,
        in_specs=in_specs or [VMEM] * len(inputs),
        out_specs=out_specs or [VMEM] * len(outputs),
        scratch_shapes=list(scratch),
        compiler_params=pltpu.CompilerParams(vmem_limit_bytes=limit * 1024 * 1024),
    )(*inputs)


def shape(dims, kind=BF16):
    return jax.ShapeDtypeStruct(dims, kind)


def fast(
    devices,
    homolog_embedding,
    coverage_indicator,
    genuine_amino_flag,
    couple_embedding,
    pairing_entry_matrices,
    pairing_exit_matrix,
    trilateral_entry_matrices,
    trilateral_exit_matrices,
):
    rows, cols, channels = couple_embedding.shape
    held = homolog_embedding.shape[0]
    width = pairing_entry_matrices.shape[2]
    part = channels // devices
    (packed,) = call(
        entry_kernel,
        (
            homolog_embedding,
            coverage_indicator,
            genuine_amino_flag.reshape(1, cols),
            jnp.transpose(pairing_entry_matrices, (1, 2, 0)),
        ),
        [shape((devices // 2, held * width + 16, cols))],
        [
            pltpu.VMEM(homolog_embedding.shape, BF16),
            pltpu.VMEM(coverage_indicator.shape, jnp.int32),
            pltpu.VMEM((1, cols), jnp.int32),
            pltpu.VMEM((2, width, homolog_embedding.shape[2]), BF16),
            pltpu.SemaphoreType.DMA((4,)),
        ],
        [HBM] * 4,
        limit=60,
    )
    packed, entry, exit_rows = lax.optimization_barrier((packed, trilateral_entry_matrices, pairing_exit_matrix))
    got = two_level(packed, devices)
    entry, exit_matrix = call(
        weight_kernel,
        (jnp.transpose(entry, (0, 2, 1, 3)), exit_rows),
        [
            shape((2, 5 * channels, channels)),
            shape((channels, width * width)),
        ],
        [pltpu.VMEM((width * width, channels), F32)],
    )
    def projected(peers):
        return [
            shape((peers, devices * rows * 2 * part // peers, cols)),
            shape((channels, rows * cols)),
            shape((channels, rows * cols), F32),
        ]

    both, pair, gate, row_mask = call(
        outer_kernel,
        (*got, couple_embedding, exit_matrix, entry),
        projected(devices) + [shape((rows, cols), F32)],
        [
            pltpu.VMEM((devices * held * width, cols), F32),
            pltpu.VMEM((devices * 8, cols), F32),
            pltpu.VMEM((width * width, rows * cols), BF16),
        ],
    )

    sides = pltpu.VMEM((devices * rows * 2 * part, cols), F32)
    (products,) = call(
        outgoing_kernel,
        (exchange(both),),
        [shape((devices, rows * part, cols))],
        [sides, pltpu.VMEM((devices * rows * part, cols), F32)],
    )
    both, pair, gate = call(
        middle_kernel,
        (exchange(products), pair, gate, trilateral_exit_matrices, entry, row_mask),
        projected(devices // 2),
    )
    groups = [list(range(begin, begin + devices // 2)) for begin in (0, devices // 2)]
    both = lax.all_to_all(both, "dap", split_axis=0, concat_axis=0, tiled=True, axis_index_groups=groups)
    (products,) = call(incoming_kernel, (both,), [shape((devices, rows * 2 * part, cols))], [sides])
    (pair_out,) = call(
        last_kernel,
        (exchange(products), pair, gate, trilateral_exit_matrices),
        [shape((rows, cols, channels))],
        [pltpu.VMEM((rows, cols, channels), BF16), pltpu.VMEM((channels * rows, cols), F32), pltpu.SemaphoreType.DMA((rows // 4,))],
        out_specs=[HBM],
    )
    return pair_out


def fits(devices, homolog_embedding, couple_embedding, pairing_entry_matrices):
    rows, cols, channels = couple_embedding.shape
    return (
        devices % 2 == 0
        and homolog_embedding.shape[0] == 2
        and rows == 8
        and cols == LANES
        and channels == 8 * devices
        and channels == LANES
        and pairing_entry_matrices.shape[2] == 32
    )


def solution(mesh):
    devices = mesh.shape["dap"]

    def one_device(*arrays):
        chosen = fast if fits(devices, arrays[0], arrays[3], arrays[4]) else local
        return chosen(devices, *arrays)

    return jax.shard_map(
        one_device,
        mesh=mesh,
        in_specs=(
            P(("crops", "dap"), None, None),
            P(("crops", "dap"), None),
            P("crops"),
            P(("crops", "dap"), None, None),
            P(),
            P(),
            P(),
            P(),
        ),
        out_specs=P(("crops", "dap"), None, None),
        check_vma=False,
    )
```

```python
import jax
import jax.numpy as jnp
from jax import lax
from jax.experimental import pallas as pl
from jax.experimental.pallas import tpu as pltpu
from jax.sharding import PartitionSpec as P

F32 = jnp.float32
BF16 = jnp.bfloat16
EPS = 1e-05
LANES = 128
VMEM = pl.BlockSpec(memory_space=pltpu.VMEM)
HBM = pl.BlockSpec(memory_space=pltpu.HBM)


def dot(a, b, left=1, right=0):
    return lax.dot_general(a, b, (((left,), (right,)), ((), ())), preferred_element_type=F32)


def sigmoid(values):
    return 0.5 * jnp.tanh(0.5 * values) + 0.5


def norm(values, axis):
    size = values.shape[axis]
    average = jnp.sum(values, axis=axis, keepdims=True) * (1.0 / size)
    centered = values - average
    variance = jnp.sum(centered * centered, axis=axis, keepdims=True) * (1.0 / size)
    return (centered * lax.rsqrt(variance + EPS)).astype(BF16)


def standardize_features(values, axis):
    average = jnp.mean(values, axis=axis, keepdims=True)
    centered = values - average
    variance = jnp.mean(centered * centered, axis=axis, keepdims=True)
    return centered * lax.rsqrt(variance + 1e-05)


def exchange(blocks):
    return lax.all_to_all(blocks, "dap", split_axis=0, concat_axis=0, tiled=True)


def outer_update(left_local, mask_local, right_cols, mask_cols, couple_embedding, pairing_exit_matrix):
    proj_width = left_local.shape[1]
    local_rows = left_local.shape[2]
    col_total = right_cols.shape[2]
    outer = jnp.einsum("rzp,rej->pjze", left_local, right_cols, preferred_element_type=jnp.float32)
    outer = outer.astype(jnp.bfloat16).reshape(local_rows, col_total, proj_width * proj_width)
    pair_update = jnp.einsum("ijf,fc->ijc", outer, pairing_exit_matrix, preferred_element_type=jnp.float32)
    pair_count = jnp.einsum("si,sj->ij", mask_local, mask_cols, preferred_element_type=jnp.float32)
    return (couple_embedding.astype(jnp.float32) + pair_update / pair_count[:, :, None]).astype(jnp.bfloat16)


def triangle(pair_now, row_mask, weights, out_weight, incoming, devices):
    rows, cols, channels = pair_now.shape
    part = channels // devices
    normalized = standardize_features(pair_now.astype(jnp.float32), -1).astype(jnp.bfloat16)
    projections = jnp.einsum("ijc,ckh->khij", normalized, weights[:, :4], preferred_element_type=jnp.float32)
    left_proj = (jax.nn.sigmoid(projections[0]) * projections[1] * row_mask).astype(jnp.bfloat16)
    right_proj = (jax.nn.sigmoid(projections[2]) * projections[3] * row_mask).astype(jnp.bfloat16)
    gate_val = jax.nn.sigmoid(
        jnp.einsum("ijc,ch->ijh", normalized, weights[:, 4], preferred_element_type=jnp.float32)
    )
    both = jnp.stack(
        [left_proj.reshape(devices, part, rows, cols), right_proj.reshape(devices, part, rows, cols)], axis=1
    )
    both = exchange(both)
    both = jnp.transpose(both, (1, 2, 0, 3, 4)).reshape(2, part, devices * rows, cols)
    einsum_form = "hki,hkj->hij" if incoming else "hik,hjk->hij"
    products = jnp.einsum(einsum_form, both[0], both[1], preferred_element_type=jnp.float32).astype(jnp.bfloat16)
    products = jnp.transpose(products.reshape(part, devices, rows, cols), (1, 0, 2, 3))
    returned = exchange(products).reshape(channels, rows, cols)
    normed_products = standardize_features(returned.astype(jnp.float32), 0).astype(jnp.bfloat16)
    pair_update = jnp.einsum("hij,hc->ijc", normed_products, out_weight, preferred_element_type=jnp.float32)
    return (pair_now.astype(jnp.float32) + gate_val * pair_update).astype(jnp.bfloat16)


def local(
    devices,
    homolog_embedding,
    coverage_indicator,
    genuine_amino_flag,
    couple_embedding,
    pairing_entry_matrices,
    pairing_exit_matrix,
    trilateral_entry_matrices,
    trilateral_exit_matrices,
):
    rows, cols, _ = couple_embedding.shape
    held = homolog_embedding.shape[0]
    width = pairing_entry_matrices.shape[2]
    sequence_mask = coverage_indicator.astype(jnp.float32)
    msa_norm = standardize_features(homolog_embedding.astype(jnp.float32), -1).astype(jnp.bfloat16)
    entries = jnp.einsum("rgl,loe->roeg", msa_norm, pairing_entry_matrices, preferred_element_type=jnp.float32)
    entries = (entries * sequence_mask[:, None, None, :]).astype(jnp.bfloat16)
    own = jnp.transpose(entries[:, 0].reshape(held, width, devices, rows), (2, 0, 1, 3))
    shared = jnp.concatenate([entries[:, 1].reshape(held, width * cols), sequence_mask.astype(jnp.bfloat16)], axis=1)
    packed = jnp.concatenate(
        [jnp.broadcast_to(shared[None], (devices,) + shared.shape), own.reshape(devices, held, width * rows)], axis=2
    )
    packed = exchange(packed).reshape(devices * held, -1)
    right_cols = packed[:, : width * cols].reshape(-1, width, cols)
    mask_cols = packed[:, width * cols : (width + 1) * cols]
    left_local = packed[:, (width + 1) * cols :].reshape(-1, width, rows)
    first_row = lax.axis_index("dap") * rows
    mask_local = lax.dynamic_slice_in_dim(mask_cols, first_row, rows, 1)
    pair_one = outer_update(left_local, mask_local, right_cols, mask_cols, couple_embedding, pairing_exit_matrix)
    residues = genuine_amino_flag.astype(jnp.float32)
    row_mask = lax.dynamic_slice_in_dim(residues, first_row, rows, 0)[:, None] * residues[None, :]
    pair_two = triangle(
        pair_one, row_mask, trilateral_entry_matrices[0], trilateral_exit_matrices[0], False, devices
    )
    return triangle(pair_two, row_mask, trilateral_entry_matrices[1], trilateral_exit_matrices[1], True, devices)


def two_level(blocks, devices):
    groups = [list(range(parity, devices, 2)) for parity in range(2)]
    got = lax.all_to_all(blocks, "dap", split_axis=0, concat_axis=0, tiled=True, axis_index_groups=groups)
    return got, lax.ppermute(got, "dap", [(at, at ^ 1) for at in range(devices)])


def halves(row):
    return [pltpu.roll(row, LANES // 2, 1), row]


def entry_kernel(all_ref, out_ref):
    pairs, _, cols = out_ref.shape
    held, width = 2, 32
    lines = held * cols
    normalized = norm(all_ref[:lines].astype(F32), -1)
    flags = all_ref[lines + 2 * width :, :cols].astype(F32)
    cover = flags[:held]
    entries = dot(all_ref[lines : lines + 2 * width], normalized, 1, 1) * flat(cover)
    entries = [entries[:, s * cols : (s + 1) * cols] for s in range(held)]
    shared = jnp.concatenate([values[width:] for values in entries], axis=0).astype(BF16)
    blank = jnp.zeros((LANES - held * width, cols), F32)
    own = jnp.transpose(jnp.concatenate([values[:width] for values in entries] + [blank], axis=0))
    marks = []
    for row in range(held + 1):
        marks += halves(flags[row : row + 1])
    marks = jnp.concatenate(marks + [jnp.zeros((8 - len(marks), cols), F32)], axis=0)
    marks = jnp.concatenate([marks, marks], axis=0)
    lane = lax.broadcasted_iota(jnp.int32, (16, LANES), 1)
    for pair in range(pairs):
        out_ref[pair, : held * width, :] = shared
        block = jnp.where(lane < held * width, own[pair * 16 : pair * 16 + 16], marks)
        out_ref[pair, held * width :, :] = block.astype(BF16)


def flat(rows):
    return jnp.concatenate([rows[row : row + 1] for row in range(rows.shape[0])], axis=1)


def project(pair, weights, mask_ref, out_ref, gate_ref):
    size = pair.shape[0]
    rows, cols = mask_ref.shape
    share = size // out_ref.shape[0]
    entries = dot(weights, norm(pair, 0))
    entries = [entries[k * size : (k + 1) * size] for k in range(5)]
    mask = flat(mask_ref[...])
    left, right = (sigmoid(entries[k]) * entries[k + 1] * mask for k in (0, 2))
    gate_ref[...] = sigmoid(entries[4])
    for peer in range(out_ref.shape[0]):
        for row in range(rows):
            block = [side[peer * share : (peer + 1) * share, row * cols : (row + 1) * cols] for side in (left, right)]
            at = row * 2 * share
            out_ref[peer, at : at + 2 * share, :] = jnp.concatenate(block, axis=0).astype(BF16)


def weight_kernel(entry_ref, exit_ref, out_entry, out_exit, rows_ref):
    for t in range(entry_ref.shape[0]):
        for k in range(entry_ref.shape[1]):
            out_entry[t, k * LANES : (k + 1) * LANES, :] = jnp.transpose(entry_ref[t, k])
    width = 32
    rows_ref[...] = exit_ref[...].astype(F32)
    leave = jnp.concatenate([rows_ref[pl.ds(e, width, stride=width), :] for e in range(width)], axis=0)
    out_exit[...] = jnp.transpose(leave).astype(BF16)


def outer_kernel(
    got_ref, other_ref, couple_ref, exit_ref, weight_ref,
    out_ref, pair_ref, gate_ref, mask_ref,
    shared_ref, aux_ref, outer_ref,
):
    pairs, _, cols = got_ref.shape
    devices = 2 * pairs
    rows = couple_ref.shape[0]
    held, width = 2, 32
    core = lax.rem(lax.axis_index("dap"), 2)
    for side, ref in enumerate((got_ref, other_ref)):
        shared = ref[:, : held * width, :].astype(F32).reshape(pairs * held * width, cols)
        shared_ref[side * pairs * held * width : (side + 1) * pairs * held * width, :] = shared
        aux = ref[:, held * width :, :].astype(F32)
        aux = jnp.where(core == 0, aux[:, :8], aux[:, 8:])
        aux_ref[side * pairs * 8 : (side + 1) * pairs * 8, :] = aux.reshape(pairs * 8, cols)
    lane = lax.broadcasted_iota(jnp.int32, (devices, LANES), 1)
    marks = []
    for row in range(0, 2 * held + 2, 2):
        low = aux_ref[pl.ds(row, devices, stride=8), :]
        high = aux_ref[pl.ds(row + 1, devices, stride=8), :]
        marks.append(jnp.where(lane < LANES // 2, pltpu.roll(low, LANES // 2, 1), high))
    cover = jnp.concatenate(marks[:held], axis=0).astype(BF16)
    flags = marks[held][0:1]
    chosen = lax.broadcasted_iota(jnp.int32, (rows, LANES), 1) == (
        lax.broadcasted_iota(jnp.int32, (rows, LANES), 0) + lax.axis_index("dap") * rows
    )
    cover_rows = dot(chosen.astype(BF16), cover, 1, 1).astype(BF16)
    scale = 1.0 / dot(cover_rows, cover)
    mask_ref[...] = jnp.sum(jnp.where(chosen, flags, 0.0), axis=1, keepdims=True) * flags
    per_tile = LANES // width
    tiles = []
    for tile in range(rows // per_tile):
        sides = [jnp.zeros((devices, LANES), F32) for _ in range(held)]
        for place in range(per_tile):
            values = aux_ref[pl.ds(tile * per_tile + place, devices, stride=8), :]
            here = (lane >= place * width) & (lane < (place + 1) * width)
            for s in range(held):
                turn = ((place - s) * width) % LANES
                moved = pltpu.roll(values, turn, 1) if turn else values
                sides[s] = jnp.where(here, moved, sides[s])
        tiles.append(jnp.concatenate(sides, axis=0))
    own = jnp.transpose(jnp.concatenate(tiles, axis=1)).astype(BF16)
    for e in range(0, width, 2):
        parts = []
        for step in range(2):
            parts.append(
                jnp.concatenate(
                    [
                        shared_ref[pl.ds(s * width + e + step, devices, stride=held * width), :]
                        for s in range(held)
                    ],
                    axis=0,
                )
            )
        result = dot(own, jnp.concatenate(parts, axis=1).astype(BF16)).astype(BF16)
        for step in range(2):
            for i in range(rows):
                outer_ref[(e + step) * width : (e + step + 1) * width, i * cols : (i + 1) * cols] = result[
                    i * width : (i + 1) * width, step * cols : (step + 1) * cols
                ]
    couple = jnp.concatenate([jnp.transpose(couple_ref[row]) for row in range(rows)], axis=1)
    pair = (couple.astype(F32) + dot(exit_ref[...], outer_ref[...]) * flat(scale)).astype(BF16)
    pair_ref[...] = pair
    project(pair.astype(F32), weight_ref[0], mask_ref, out_ref, gate_ref)


def side_rows(got_ref, sides_ref, part):
    sides_ref[...] = got_ref[...].astype(F32).reshape(sides_ref.shape)
    lines = sides_ref.shape[0] // (2 * part)
    return lambda h: sides_ref[pl.ds(h, lines, stride=2 * part), :].astype(BF16)


def outgoing_kernel(got_ref, out_ref, sides_ref, products_ref):
    cols = got_ref.shape[-1]
    part = products_ref.shape[0] // cols
    side = side_rows(got_ref, sides_ref, part)
    for h in range(part):
        products_ref[pl.ds(h, cols, stride=part), :] = dot(side(h), side(part + h), 1, 1)
    out_ref[...] = products_ref[...].astype(BF16).reshape(out_ref.shape)


def incoming_kernel(got_ref, out_ref, sides_ref):
    peers, size, cols = out_ref.shape
    rows = cols // peers
    part = size // rows
    side = side_rows(got_ref, sides_ref, part)
    for h in range(0, part, 2):
        results = [dot(side(at), side(part + at), 0, 0) for at in (h, h + 1)]
        for peer in range(peers):
            block = [result[peer * rows : (peer + 1) * rows] for result in results]
            out_ref[peer, h * rows : (h + 2) * rows, :] = jnp.concatenate(block, axis=0).astype(BF16)


def updated(products, pair_ref, gate_ref, leave):
    update = dot(jnp.transpose(leave), norm(jnp.concatenate(products, axis=1), 0))
    return pair_ref[...].astype(F32) + gate_ref[...] * update


def middle_kernel(got_ref, pair_ref, gate_ref, leave_ref, weight_ref, mask_ref, out_ref, next_ref, next_gate_ref):
    devices, size, cols = got_ref.shape
    part = size // mask_ref.shape[0]
    products = []
    for at in range(0, size, 2 * part):
        lines = got_ref[:, at : at + 2 * part, :].astype(F32)
        products += [values.reshape(devices * part, cols) for values in (lines[:, :part], lines[:, part:])]
    pair = updated(products, pair_ref, gate_ref, leave_ref[0]).astype(BF16)
    next_ref[...] = pair
    project(pair.astype(F32), weight_ref[1], mask_ref, out_ref, next_gate_ref)


def last_kernel(got_ref, pair_ref, gate_ref, leave_ref, out_hbm, out_ref, sums_ref, sems):
    rows, cols, channels = out_ref.shape
    senders = got_ref.shape[0] // 2
    sums = got_ref[:senders].astype(F32) + got_ref[senders:].astype(F32)
    sums_ref[...] = sums.reshape(sums_ref.shape)
    products = [sums_ref[pl.ds(row, channels, stride=rows), :] for row in range(rows)]
    pair = updated(products, pair_ref, gate_ref, leave_ref[1])
    copies = []
    for row in range(rows):
        out_ref[row] = jnp.transpose(pair[:, row * cols : (row + 1) * cols]).astype(BF16)
        if row % 4 == 3:
            part = pl.ds(row - 3, 4)
            copies.append(pltpu.make_async_copy(out_ref.at[part], out_hbm.at[part], sems.at[row // 4]))
            copies[-1].start()
    for copy in copies:
        copy.wait()


def call(kernel, inputs, outputs, scratch=(), in_specs=None, out_specs=None):
    return pl.pallas_call(
        kernel,
        out_shape=outputs,
        in_specs=in_specs or [VMEM] * len(inputs),
        out_specs=out_specs or [VMEM] * len(outputs),
        scratch_shapes=list(scratch),
        compiler_params=pltpu.CompilerParams(vmem_limit_bytes=40 * 1024 * 1024),
    )(*inputs)


def shape(dims, kind=BF16):
    return jax.ShapeDtypeStruct(dims, kind)


def fast(
    devices,
    homolog_embedding,
    coverage_indicator,
    genuine_amino_flag,
    couple_embedding,
    pairing_entry_matrices,
    pairing_exit_matrix,
    trilateral_entry_matrices,
    trilateral_exit_matrices,
):
    rows, cols, channels = couple_embedding.shape
    held = homolog_embedding.shape[0]
    width = pairing_entry_matrices.shape[2]
    part = channels // devices
    depth = homolog_embedding.shape[2]
    flags = jnp.concatenate([coverage_indicator, genuine_amino_flag.reshape(1, cols)], axis=0)
    flags = jnp.pad(flags, ((0, 16 - held - 1), (0, depth - cols))).astype(BF16)
    everything = jnp.concatenate(
        [
            homolog_embedding.reshape(held * cols, depth),
            jnp.transpose(pairing_entry_matrices, (1, 2, 0)).reshape(2 * width, depth),
            flags,
        ],
        axis=0,
    )
    (packed,) = call(entry_kernel, (everything,), [shape((devices // 2, held * width + 16, cols))])
    packed, entry, exit_rows = lax.optimization_barrier((packed, trilateral_entry_matrices, pairing_exit_matrix))
    got = two_level(packed, devices)
    entry, exit_matrix = call(
        weight_kernel,
        (jnp.transpose(entry, (0, 2, 1, 3)), exit_rows),
        [
            shape((2, 5 * channels, channels)),
            shape((channels, width * width)),
        ],
        [pltpu.VMEM((width * width, channels), F32)],
    )
    def projected(peers):
        return [
            shape((peers, devices * rows * 2 * part // peers, cols)),
            shape((channels, rows * cols)),
            shape((channels, rows * cols), F32),
        ]

    both, pair, gate, row_mask = call(
        outer_kernel,
        (*got, couple_embedding, exit_matrix, entry),
        projected(devices) + [shape((rows, cols), F32)],
        [
            pltpu.VMEM((devices * held * width, cols), F32),
            pltpu.VMEM((devices * 8, cols), F32),
            pltpu.VMEM((width * width, rows * cols), BF16),
        ],
    )

    sides = pltpu.VMEM((devices * rows * 2 * part, cols), F32)
    (products,) = call(
        outgoing_kernel,
        (exchange(both),),
        [shape((devices, rows * part, cols))],
        [sides, pltpu.VMEM((devices * rows * part, cols), F32)],
    )
    both, pair, gate = call(
        middle_kernel,
        (exchange(products), pair, gate, trilateral_exit_matrices, entry, row_mask),
        projected(devices // 2),
    )
    groups = [list(range(begin, begin + devices // 2)) for begin in (0, devices // 2)]
    both = lax.all_to_all(both, "dap", split_axis=0, concat_axis=0, tiled=True, axis_index_groups=groups)
    (products,) = call(incoming_kernel, (both,), [shape((devices, rows * 2 * part, cols))], [sides])
    (pair_out,) = call(
        last_kernel,
        (exchange(products), pair, gate, trilateral_exit_matrices),
        [shape((rows, cols, channels))],
        [pltpu.VMEM((rows, cols, channels), BF16), pltpu.VMEM((channels * rows, cols), F32), pltpu.SemaphoreType.DMA((rows // 4,))],
        out_specs=[HBM],
    )
    return pair_out


def fits(devices, homolog_embedding, couple_embedding, pairing_entry_matrices):
    rows, cols, channels = couple_embedding.shape
    return (
        devices % 2 == 0
        and homolog_embedding.shape[0] == 2
        and rows == 8
        and cols == LANES
        and channels == 8 * devices
        and channels == LANES
        and pairing_entry_matrices.shape[2] == 32
        and homolog_embedding.shape[2] >= cols
    )


def solution(mesh):
    devices = mesh.shape["dap"]

    def one_device(*arrays):
        chosen = fast if fits(devices, arrays[0], arrays[3], arrays[4]) else local
        return chosen(devices, *arrays)

    return jax.shard_map(
        one_device,
        mesh=mesh,
        in_specs=(
            P(("crops", "dap"), None, None),
            P(("crops", "dap"), None),
            P("crops"),
            P(("crops", "dap"), None, None),
            P(),
            P(),
            P(),
            P(),
        ),
        out_specs=P(("crops", "dap"), None, None),
        check_vma=False,
    )
```

```python
import jax
import jax.numpy as jnp
from jax import lax
from jax.experimental import pallas as pl
from jax.experimental.pallas import tpu as pltpu
from jax.sharding import PartitionSpec as P

F32 = jnp.float32
BF16 = jnp.bfloat16
EPS = 1e-05
LANES = 128
GAP = 8
VMEM = pl.BlockSpec(memory_space=pltpu.VMEM)
HBM = pl.BlockSpec(memory_space=pltpu.HBM)


def dot(a, b, left=1, right=0):
    return lax.dot_general(a, b, (((left,), (right,)), ((), ())), preferred_element_type=F32)


def sigmoid(values):
    return 0.5 * jnp.tanh(0.5 * values) + 0.5


def norm(values, axis):
    size = values.shape[axis]
    average = jnp.sum(values, axis=axis, keepdims=True) * (1.0 / size)
    centered = values - average
    variance = jnp.sum(centered * centered, axis=axis, keepdims=True) * (1.0 / size)
    return (centered * lax.rsqrt(variance + EPS)).astype(BF16)


def standardize_features(values, axis):
    average = jnp.mean(values, axis=axis, keepdims=True)
    centered = values - average
    variance = jnp.mean(centered * centered, axis=axis, keepdims=True)
    return centered * lax.rsqrt(variance + 1e-05)


def exchange(blocks):
    return lax.all_to_all(blocks, "dap", split_axis=0, concat_axis=0, tiled=True)


def outer_update(left_local, mask_local, right_cols, mask_cols, couple_embedding, pairing_exit_matrix):
    proj_width = left_local.shape[1]
    local_rows = left_local.shape[2]
    col_total = right_cols.shape[2]
    outer = jnp.einsum("rzp,rej->pjze", left_local, right_cols, preferred_element_type=jnp.float32)
    outer = outer.astype(jnp.bfloat16).reshape(local_rows, col_total, proj_width * proj_width)
    pair_update = jnp.einsum("ijf,fc->ijc", outer, pairing_exit_matrix, preferred_element_type=jnp.float32)
    pair_count = jnp.einsum("si,sj->ij", mask_local, mask_cols, preferred_element_type=jnp.float32)
    return (couple_embedding.astype(jnp.float32) + pair_update / pair_count[:, :, None]).astype(jnp.bfloat16)


def triangle(pair_now, row_mask, weights, out_weight, incoming, devices):
    rows, cols, channels = pair_now.shape
    part = channels // devices
    normalized = standardize_features(pair_now.astype(jnp.float32), -1).astype(jnp.bfloat16)
    projections = jnp.einsum("ijc,ckh->khij", normalized, weights[:, :4], preferred_element_type=jnp.float32)
    left_proj = (jax.nn.sigmoid(projections[0]) * projections[1] * row_mask).astype(jnp.bfloat16)
    right_proj = (jax.nn.sigmoid(projections[2]) * projections[3] * row_mask).astype(jnp.bfloat16)
    gate_val = jax.nn.sigmoid(
        jnp.einsum("ijc,ch->ijh", normalized, weights[:, 4], preferred_element_type=jnp.float32)
    )
    both = jnp.stack(
        [left_proj.reshape(devices, part, rows, cols), right_proj.reshape(devices, part, rows, cols)], axis=1
    )
    both = exchange(both)
    both = jnp.transpose(both, (1, 2, 0, 3, 4)).reshape(2, part, devices * rows, cols)
    einsum_form = "hki,hkj->hij" if incoming else "hik,hjk->hij"
    products = jnp.einsum(einsum_form, both[0], both[1], preferred_element_type=jnp.float32).astype(jnp.bfloat16)
    products = jnp.transpose(products.reshape(part, devices, rows, cols), (1, 0, 2, 3))
    returned = exchange(products).reshape(channels, rows, cols)
    normed_products = standardize_features(returned.astype(jnp.float32), 0).astype(jnp.bfloat16)
    pair_update = jnp.einsum("hij,hc->ijc", normed_products, out_weight, preferred_element_type=jnp.float32)
    return (pair_now.astype(jnp.float32) + gate_val * pair_update).astype(jnp.bfloat16)


def local(
    devices,
    homolog_embedding,
    coverage_indicator,
    genuine_amino_flag,
    couple_embedding,
    pairing_entry_matrices,
    pairing_exit_matrix,
    trilateral_entry_matrices,
    trilateral_exit_matrices,
):
    rows, cols, _ = couple_embedding.shape
    held = homolog_embedding.shape[0]
    width = pairing_entry_matrices.shape[2]
    sequence_mask = coverage_indicator.astype(jnp.float32)
    msa_norm = standardize_features(homolog_embedding.astype(jnp.float32), -1).astype(jnp.bfloat16)
    entries = jnp.einsum("rgl,loe->roeg", msa_norm, pairing_entry_matrices, preferred_element_type=jnp.float32)
    entries = (entries * sequence_mask[:, None, None, :]).astype(jnp.bfloat16)
    own = jnp.transpose(entries[:, 0].reshape(held, width, devices, rows), (2, 0, 1, 3))
    shared = jnp.concatenate([entries[:, 1].reshape(held, width * cols), sequence_mask.astype(jnp.bfloat16)], axis=1)
    packed = jnp.concatenate(
        [jnp.broadcast_to(shared[None], (devices,) + shared.shape), own.reshape(devices, held, width * rows)], axis=2
    )
    packed = exchange(packed).reshape(devices * held, -1)
    right_cols = packed[:, : width * cols].reshape(-1, width, cols)
    mask_cols = packed[:, width * cols : (width + 1) * cols]
    left_local = packed[:, (width + 1) * cols :].reshape(-1, width, rows)
    first_row = lax.axis_index("dap") * rows
    mask_local = lax.dynamic_slice_in_dim(mask_cols, first_row, rows, 1)
    pair_one = outer_update(left_local, mask_local, right_cols, mask_cols, couple_embedding, pairing_exit_matrix)
    residues = genuine_amino_flag.astype(jnp.float32)
    row_mask = lax.dynamic_slice_in_dim(residues, first_row, rows, 0)[:, None] * residues[None, :]
    pair_two = triangle(
        pair_one, row_mask, trilateral_entry_matrices[0], trilateral_exit_matrices[0], False, devices
    )
    return triangle(pair_two, row_mask, trilateral_entry_matrices[1], trilateral_exit_matrices[1], True, devices)


def two_level(blocks, devices):
    groups = [list(range(parity, devices, 2)) for parity in range(2)]
    got = lax.all_to_all(blocks, "dap", split_axis=0, concat_axis=0, tiled=True, axis_index_groups=groups)
    return got, lax.ppermute(got, "dap", [(at, at ^ 1) for at in range(devices)])


def spread(blocks, target_ref, first=0):
    count, rows, _ = blocks.shape
    for at in range(count):
        begin = (first + at) * (rows + GAP)
        target_ref[begin : begin + rows, :] = blocks[at]
    return rows + GAP


def halves(row):
    return [pltpu.roll(row, LANES // 2, 1), row]


def entry_kernel(all_ref, out_ref):
    pairs, _, cols = out_ref.shape
    held, width = 2, 32
    lines = held * cols
    normalized = norm(all_ref[:lines].astype(F32), -1)
    flags = all_ref[lines + 2 * width :, :cols].astype(F32)
    cover = flags[:held]
    entries = dot(all_ref[lines : lines + 2 * width], normalized, 1, 1) * flat(cover)
    entries = [entries[:, s * cols : (s + 1) * cols] for s in range(held)]
    shared = jnp.concatenate([values[width:] for values in entries], axis=0).astype(BF16)
    blank = jnp.zeros((LANES - held * width, cols), F32)
    own = jnp.transpose(jnp.concatenate([values[:width] for values in entries] + [blank], axis=0))
    marks = []
    for row in range(held + 1):
        marks += halves(flags[row : row + 1])
    marks = jnp.concatenate(marks + [jnp.zeros((8 - len(marks), cols), F32)], axis=0)
    marks = jnp.concatenate([marks, marks], axis=0)
    lane = lax.broadcasted_iota(jnp.int32, (16, LANES), 1)
    for pair in range(pairs):
        out_ref[pair, : held * width, :] = shared
        block = jnp.where(lane < held * width, own[pair * 16 : pair * 16 + 16], marks)
        out_ref[pair, held * width :, :] = block.astype(BF16)


def flat(rows):
    return jnp.concatenate([rows[row : row + 1] for row in range(rows.shape[0])], axis=1)


def project(pair, weights, mask_ref, out_ref, gate_ref):
    size = pair.shape[0]
    rows, cols = mask_ref.shape
    share = size // out_ref.shape[0]
    entries = dot(weights, norm(pair, 0))
    entries = [entries[k * size : (k + 1) * size] for k in range(5)]
    mask = flat(mask_ref[...])
    left, right = (sigmoid(entries[k]) * entries[k + 1] * mask for k in (0, 2))
    gate_ref[...] = sigmoid(entries[4])
    for peer in range(out_ref.shape[0]):
        for row in range(rows):
            block = [side[peer * share : (peer + 1) * share, row * cols : (row + 1) * cols] for side in (left, right)]
            at = row * 2 * share
            out_ref[peer, at : at + 2 * share, :] = jnp.concatenate(block, axis=0).astype(BF16)


def weight_kernel(entry_ref, exit_ref, out_entry, out_exit, rows_ref):
    for t in range(entry_ref.shape[0]):
        for k in range(entry_ref.shape[1]):
            out_entry[t, k * LANES : (k + 1) * LANES, :] = jnp.transpose(entry_ref[t, k])
    width = 32
    step = spread(exit_ref[...].astype(F32).reshape(width, width, LANES), rows_ref)
    leave = jnp.concatenate([rows_ref[pl.ds(e, width, stride=step), :] for e in range(width)], axis=0)
    out_exit[...] = jnp.transpose(leave).astype(BF16)


def outer_kernel(
    got_ref, other_ref, couple_ref, exit_ref, weight_ref,
    out_ref, pair_ref, gate_ref, mask_ref,
    shared_ref, aux_ref, outer_ref,
):
    pairs, _, cols = got_ref.shape
    devices = 2 * pairs
    rows = couple_ref.shape[0]
    held, width = 2, 32
    core = lax.rem(lax.axis_index("dap"), 2)
    for side, ref in enumerate((got_ref, other_ref)):
        step = spread(ref[:, : held * width, :].astype(F32), shared_ref, side * pairs)
        aux = ref[:, held * width :, :].astype(F32)
        aux = jnp.where(core == 0, aux[:, :8], aux[:, 8:])
        aux_ref[side * pairs * 8 : (side + 1) * pairs * 8, :] = aux.reshape(pairs * 8, cols)
    lane = lax.broadcasted_iota(jnp.int32, (devices, LANES), 1)
    marks = []
    for row in range(0, 2 * held + 2, 2):
        low = aux_ref[pl.ds(row, devices, stride=8), :]
        high = aux_ref[pl.ds(row + 1, devices, stride=8), :]
        marks.append(jnp.where(lane < LANES // 2, pltpu.roll(low, LANES // 2, 1), high))
    cover = jnp.concatenate(marks[:held], axis=0).astype(BF16)
    flags = marks[held][0:1]
    chosen = lax.broadcasted_iota(jnp.int32, (rows, LANES), 1) == (
        lax.broadcasted_iota(jnp.int32, (rows, LANES), 0) + lax.axis_index("dap") * rows
    )
    cover_rows = dot(chosen.astype(BF16), cover, 1, 1).astype(BF16)
    scale = 1.0 / dot(cover_rows, cover)
    mask_ref[...] = jnp.sum(jnp.where(chosen, flags, 0.0), axis=1, keepdims=True) * flags
    per_tile = LANES // width
    tiles = []
    for tile in range(rows // per_tile):
        sides = [jnp.zeros((devices, LANES), F32) for _ in range(held)]
        for place in range(per_tile):
            values = aux_ref[pl.ds(tile * per_tile + place, devices, stride=8), :]
            here = (lane >= place * width) & (lane < (place + 1) * width)
            for s in range(held):
                turn = ((place - s) * width) % LANES
                moved = pltpu.roll(values, turn, 1) if turn else values
                sides[s] = jnp.where(here, moved, sides[s])
        tiles.append(jnp.concatenate(sides, axis=0))
    own = jnp.transpose(jnp.concatenate(tiles, axis=1)).astype(BF16)
    for e in range(0, width, 2):
        parts = []
        for more in range(2):
            parts.append(
                jnp.concatenate(
                    [
                        shared_ref[pl.ds(s * width + e + more, devices, stride=step), :]
                        for s in range(held)
                    ],
                    axis=0,
                )
            )
        result = dot(own, jnp.concatenate(parts, axis=1).astype(BF16)).astype(BF16)
        for more in range(2):
            for i in range(rows):
                outer_ref[(e + more) * width : (e + more + 1) * width, i * cols : (i + 1) * cols] = result[
                    i * width : (i + 1) * width, more * cols : (more + 1) * cols
                ]
    couple = jnp.concatenate([jnp.transpose(couple_ref[row]) for row in range(rows)], axis=1)
    pair = (couple.astype(F32) + dot(exit_ref[...], outer_ref[...]) * flat(scale)).astype(BF16)
    pair_ref[...] = pair
    project(pair.astype(F32), weight_ref[0], mask_ref, out_ref, gate_ref)


def side_rows(got_ref, sides_ref, part):
    lines = got_ref.shape[0] * got_ref.shape[1] // (2 * part)
    step = spread(got_ref[...].astype(F32).reshape(lines, 2 * part, got_ref.shape[2]), sides_ref)
    return lambda h: sides_ref[pl.ds(h, lines, stride=step), :].astype(BF16)


def outgoing_kernel(got_ref, out_ref, sides_ref, products_ref):
    cols = got_ref.shape[-1]
    part = products_ref.shape[0] // cols
    side = side_rows(got_ref, sides_ref, part)
    for h in range(part):
        products_ref[pl.ds(h, cols, stride=part), :] = dot(side(h), side(part + h), 1, 1)
    out_ref[...] = products_ref[...].astype(BF16).reshape(out_ref.shape)


def incoming_kernel(got_ref, out_ref, sides_ref):
    peers, size, cols = out_ref.shape
    rows = cols // peers
    part = size // rows
    side = side_rows(got_ref, sides_ref, part)
    for h in range(0, part, 2):
        results = [dot(side(at), side(part + at), 0, 0) for at in (h, h + 1)]
        for peer in range(peers):
            block = [result[peer * rows : (peer + 1) * rows] for result in results]
            out_ref[peer, h * rows : (h + 2) * rows, :] = jnp.concatenate(block, axis=0).astype(BF16)


def updated(products, pair_ref, gate_ref, leave):
    update = dot(jnp.transpose(leave), norm(jnp.concatenate(products, axis=1), 0))
    return pair_ref[...].astype(F32) + gate_ref[...] * update


def middle_kernel(got_ref, pair_ref, gate_ref, leave_ref, weight_ref, mask_ref, out_ref, next_ref, next_gate_ref):
    devices, size, cols = got_ref.shape
    part = size // mask_ref.shape[0]
    products = []
    for at in range(0, size, 2 * part):
        lines = got_ref[:, at : at + 2 * part, :].astype(F32)
        products += [values.reshape(devices * part, cols) for values in (lines[:, :part], lines[:, part:])]
    pair = updated(products, pair_ref, gate_ref, leave_ref[0]).astype(BF16)
    next_ref[...] = pair
    project(pair.astype(F32), weight_ref[1], mask_ref, out_ref, next_gate_ref)


def last_kernel(got_ref, pair_ref, gate_ref, leave_ref, out_hbm, out_ref, sums_ref, sems):
    rows, cols, channels = out_ref.shape
    senders = got_ref.shape[0] // 2
    sums = got_ref[:senders].astype(F32) + got_ref[senders:].astype(F32)
    sums_ref[...] = sums.reshape(sums_ref.shape)
    products = [sums_ref[pl.ds(row, channels, stride=rows), :] for row in range(rows)]
    pair = updated(products, pair_ref, gate_ref, leave_ref[1])
    copies = []
    for row in range(rows):
        out_ref[row] = jnp.transpose(pair[:, row * cols : (row + 1) * cols]).astype(BF16)
        if row % 4 == 3:
            part = pl.ds(row - 3, 4)
            copies.append(pltpu.make_async_copy(out_ref.at[part], out_hbm.at[part], sems.at[row // 4]))
            copies[-1].start()
    for copy in copies:
        copy.wait()


def call(kernel, inputs, outputs, scratch=(), in_specs=None, out_specs=None):
    return pl.pallas_call(
        kernel,
        out_shape=outputs,
        in_specs=in_specs or [VMEM] * len(inputs),
        out_specs=out_specs or [VMEM] * len(outputs),
        scratch_shapes=list(scratch),
        compiler_params=pltpu.CompilerParams(vmem_limit_bytes=40 * 1024 * 1024),
    )(*inputs)


def shape(dims, kind=BF16):
    return jax.ShapeDtypeStruct(dims, kind)


def fast(
    devices,
    homolog_embedding,
    coverage_indicator,
    genuine_amino_flag,
    couple_embedding,
    pairing_entry_matrices,
    pairing_exit_matrix,
    trilateral_entry_matrices,
    trilateral_exit_matrices,
):
    rows, cols, channels = couple_embedding.shape
    held = homolog_embedding.shape[0]
    width = pairing_entry_matrices.shape[2]
    part = channels // devices
    depth = homolog_embedding.shape[2]
    flags = jnp.concatenate([coverage_indicator, genuine_amino_flag.reshape(1, cols)], axis=0)
    flags = jnp.pad(flags, ((0, 16 - held - 1), (0, depth - cols))).astype(BF16)
    everything = jnp.concatenate(
        [
            homolog_embedding.reshape(held * cols, depth),
            jnp.transpose(pairing_entry_matrices, (1, 2, 0)).reshape(2 * width, depth),
            flags,
        ],
        axis=0,
    )
    (packed,) = call(entry_kernel, (everything,), [shape((devices // 2, held * width + 16, cols))])
    packed, entry, exit_rows = lax.optimization_barrier((packed, trilateral_entry_matrices, pairing_exit_matrix))
    got = two_level(packed, devices)
    entry, exit_matrix = call(
        weight_kernel,
        (jnp.transpose(entry, (0, 2, 1, 3)), exit_rows),
        [
            shape((2, 5 * channels, channels)),
            shape((channels, width * width)),
        ],
        [pltpu.VMEM((width * (width + GAP), channels), F32)],
    )
    def projected(peers):
        return [
            shape((peers, devices * rows * 2 * part // peers, cols)),
            shape((channels, rows * cols)),
            shape((channels, rows * cols), F32),
        ]

    both, pair, gate, row_mask = call(
        outer_kernel,
        (*got, couple_embedding, exit_matrix, entry),
        projected(devices) + [shape((rows, cols), F32)],
        [
            pltpu.VMEM((devices * (held * width + GAP), cols), F32),
            pltpu.VMEM((devices * 8, cols), F32),
            pltpu.VMEM((width * width, rows * cols), BF16),
        ],
    )

    sides = pltpu.VMEM((devices * rows * (2 * part + GAP), cols), F32)
    (products,) = call(
        outgoing_kernel,
        (exchange(both),),
        [shape((devices, rows * part, cols))],
        [sides, pltpu.VMEM((devices * rows * part, cols), F32)],
    )
    both, pair, gate = call(
        middle_kernel,
        (exchange(products), pair, gate, trilateral_exit_matrices, entry, row_mask),
        projected(devices // 2),
    )
    groups = [list(range(begin, begin + devices // 2)) for begin in (0, devices // 2)]
    both = lax.all_to_all(both, "dap", split_axis=0, concat_axis=0, tiled=True, axis_index_groups=groups)
    (products,) = call(incoming_kernel, (both,), [shape((devices, rows * 2 * part, cols))], [sides])
    (pair_out,) = call(
        last_kernel,
        (exchange(products), pair, gate, trilateral_exit_matrices),
        [shape((rows, cols, channels))],
        [pltpu.VMEM((rows, cols, channels), BF16), pltpu.VMEM((channels * rows, cols), F32), pltpu.SemaphoreType.DMA((rows // 4,))],
        out_specs=[HBM],
    )
    return pair_out


def fits(devices, homolog_embedding, couple_embedding, pairing_entry_matrices):
    rows, cols, channels = couple_embedding.shape
    return (
        devices % 2 == 0
        and homolog_embedding.shape[0] == 2
        and rows == 8
        and cols == LANES
        and channels == 8 * devices
        and channels == LANES
        and pairing_entry_matrices.shape[2] == 32
        and homolog_embedding.shape[2] >= cols
    )


def solution(mesh):
    devices = mesh.shape["dap"]

    def one_device(*arrays):
        chosen = fast if fits(devices, arrays[0], arrays[3], arrays[4]) else local
        return chosen(devices, *arrays)

    return jax.shard_map(
        one_device,
        mesh=mesh,
        in_specs=(
            P(("crops", "dap"), None, None),
            P(("crops", "dap"), None),
            P("crops"),
            P(("crops", "dap"), None, None),
            P(),
            P(),
            P(),
            P(),
        ),
        out_specs=P(("crops", "dap"), None, None),
        check_vma=False,
    )
```

```python
import jax
import jax.numpy as jnp
from jax import lax
from jax.experimental import pallas as pl
from jax.experimental.pallas import tpu as pltpu
from jax.sharding import PartitionSpec as P

F32 = jnp.float32
BF16 = jnp.bfloat16
EPS = 1e-05
LANES = 128
GAP = 8
VMEM = pl.BlockSpec(memory_space=pltpu.VMEM)
HBM = pl.BlockSpec(memory_space=pltpu.HBM)


def dot(a, b, left=1, right=0):
    return lax.dot_general(a, b, (((left,), (right,)), ((), ())), preferred_element_type=F32)


def sigmoid(values):
    return 0.5 * jnp.tanh(0.5 * values) + 0.5


def norm(values, axis):
    size = values.shape[axis]
    average = jnp.sum(values, axis=axis, keepdims=True) * (1.0 / size)
    centered = values - average
    variance = jnp.sum(centered * centered, axis=axis, keepdims=True) * (1.0 / size)
    return (centered * lax.rsqrt(variance + EPS)).astype(BF16)


def standardize_features(values, axis):
    average = jnp.mean(values, axis=axis, keepdims=True)
    centered = values - average
    variance = jnp.mean(centered * centered, axis=axis, keepdims=True)
    return centered * lax.rsqrt(variance + 1e-05)


def exchange(blocks):
    return lax.all_to_all(blocks, "dap", split_axis=0, concat_axis=0, tiled=True)


def outer_update(left_local, mask_local, right_cols, mask_cols, couple_embedding, pairing_exit_matrix):
    proj_width = left_local.shape[1]
    local_rows = left_local.shape[2]
    col_total = right_cols.shape[2]
    outer = jnp.einsum("rzp,rej->pjze", left_local, right_cols, preferred_element_type=jnp.float32)
    outer = outer.astype(jnp.bfloat16).reshape(local_rows, col_total, proj_width * proj_width)
    pair_update = jnp.einsum("ijf,fc->ijc", outer, pairing_exit_matrix, preferred_element_type=jnp.float32)
    pair_count = jnp.einsum("si,sj->ij", mask_local, mask_cols, preferred_element_type=jnp.float32)
    return (couple_embedding.astype(jnp.float32) + pair_update / pair_count[:, :, None]).astype(jnp.bfloat16)


def triangle(pair_now, row_mask, weights, out_weight, incoming, devices):
    rows, cols, channels = pair_now.shape
    part = channels // devices
    normalized = standardize_features(pair_now.astype(jnp.float32), -1).astype(jnp.bfloat16)
    projections = jnp.einsum("ijc,ckh->khij", normalized, weights[:, :4], preferred_element_type=jnp.float32)
    left_proj = (jax.nn.sigmoid(projections[0]) * projections[1] * row_mask).astype(jnp.bfloat16)
    right_proj = (jax.nn.sigmoid(projections[2]) * projections[3] * row_mask).astype(jnp.bfloat16)
    gate_val = jax.nn.sigmoid(
        jnp.einsum("ijc,ch->ijh", normalized, weights[:, 4], preferred_element_type=jnp.float32)
    )
    both = jnp.stack(
        [left_proj.reshape(devices, part, rows, cols), right_proj.reshape(devices, part, rows, cols)], axis=1
    )
    both = exchange(both)
    both = jnp.transpose(both, (1, 2, 0, 3, 4)).reshape(2, part, devices * rows, cols)
    einsum_form = "hki,hkj->hij" if incoming else "hik,hjk->hij"
    products = jnp.einsum(einsum_form, both[0], both[1], preferred_element_type=jnp.float32).astype(jnp.bfloat16)
    products = jnp.transpose(products.reshape(part, devices, rows, cols), (1, 0, 2, 3))
    returned = exchange(products).reshape(channels, rows, cols)
    normed_products = standardize_features(returned.astype(jnp.float32), 0).astype(jnp.bfloat16)
    pair_update = jnp.einsum("hij,hc->ijc", normed_products, out_weight, preferred_element_type=jnp.float32)
    return (pair_now.astype(jnp.float32) + gate_val * pair_update).astype(jnp.bfloat16)


def local(
    devices,
    homolog_embedding,
    coverage_indicator,
    genuine_amino_flag,
    couple_embedding,
    pairing_entry_matrices,
    pairing_exit_matrix,
    trilateral_entry_matrices,
    trilateral_exit_matrices,
):
    rows, cols, _ = couple_embedding.shape
    held = homolog_embedding.shape[0]
    width = pairing_entry_matrices.shape[2]
    sequence_mask = coverage_indicator.astype(jnp.float32)
    msa_norm = standardize_features(homolog_embedding.astype(jnp.float32), -1).astype(jnp.bfloat16)
    entries = jnp.einsum("rgl,loe->roeg", msa_norm, pairing_entry_matrices, preferred_element_type=jnp.float32)
    entries = (entries * sequence_mask[:, None, None, :]).astype(jnp.bfloat16)
    own = jnp.transpose(entries[:, 0].reshape(held, width, devices, rows), (2, 0, 1, 3))
    shared = jnp.concatenate([entries[:, 1].reshape(held, width * cols), sequence_mask.astype(jnp.bfloat16)], axis=1)
    packed = jnp.concatenate(
        [jnp.broadcast_to(shared[None], (devices,) + shared.shape), own.reshape(devices, held, width * rows)], axis=2
    )
    packed = exchange(packed).reshape(devices * held, -1)
    right_cols = packed[:, : width * cols].reshape(-1, width, cols)
    mask_cols = packed[:, width * cols : (width + 1) * cols]
    left_local = packed[:, (width + 1) * cols :].reshape(-1, width, rows)
    first_row = lax.axis_index("dap") * rows
    mask_local = lax.dynamic_slice_in_dim(mask_cols, first_row, rows, 1)
    pair_one = outer_update(left_local, mask_local, right_cols, mask_cols, couple_embedding, pairing_exit_matrix)
    residues = genuine_amino_flag.astype(jnp.float32)
    row_mask = lax.dynamic_slice_in_dim(residues, first_row, rows, 0)[:, None] * residues[None, :]
    pair_two = triangle(
        pair_one, row_mask, trilateral_entry_matrices[0], trilateral_exit_matrices[0], False, devices
    )
    return triangle(pair_two, row_mask, trilateral_entry_matrices[1], trilateral_exit_matrices[1], True, devices)


def two_level(blocks, devices):
    groups = [list(range(parity, devices, 2)) for parity in range(2)]
    got = lax.all_to_all(blocks, "dap", split_axis=0, concat_axis=0, tiled=True, axis_index_groups=groups)
    return got, lax.ppermute(got, "dap", [(at, at ^ 1) for at in range(devices)])


def spread(blocks, target_ref, first=0):
    count, rows, _ = blocks.shape
    for at in range(count):
        begin = (first + at) * (rows + GAP)
        target_ref[begin : begin + rows, :] = blocks[at]
    return rows + GAP


def halves(row):
    return [pltpu.roll(row, LANES // 2, 1), row]


def entry_kernel(all_ref, out_ref):
    lines = all_ref.shape[0] - out_ref.shape[0]
    out_ref[...] = dot(all_ref[lines:], norm(all_ref[:lines].astype(F32), -1), 1, 1)


def pack_kernel(entries_ref, cover_ref, flag_ref, out_ref):
    pairs, _, cols = out_ref.shape
    held, width = 2, 32
    cover = cover_ref[...].astype(F32)
    flags = jnp.concatenate([cover, flag_ref[...].astype(F32)], axis=0)
    entries = entries_ref[...] * flat(cover)
    entries = [entries[:, s * cols : (s + 1) * cols] for s in range(held)]
    shared = jnp.concatenate([values[width:] for values in entries], axis=0).astype(BF16)
    blank = jnp.zeros((LANES - held * width, cols), F32)
    own = jnp.transpose(jnp.concatenate([values[:width] for values in entries] + [blank], axis=0))
    marks = []
    for row in range(held + 1):
        marks += halves(flags[row : row + 1])
    marks = jnp.concatenate(marks + [jnp.zeros((8 - len(marks), cols), F32)], axis=0)
    marks = jnp.concatenate([marks, marks], axis=0)
    lane = lax.broadcasted_iota(jnp.int32, (16, LANES), 1)
    for pair in range(pairs):
        out_ref[pair, : held * width, :] = shared
        block = jnp.where(lane < held * width, own[pair * 16 : pair * 16 + 16], marks)
        out_ref[pair, held * width :, :] = block.astype(BF16)


def flat(rows):
    return jnp.concatenate([rows[row : row + 1] for row in range(rows.shape[0])], axis=1)


def project(pair, weights, mask_ref, out_ref, gate_ref):
    size = pair.shape[0]
    rows, cols = mask_ref.shape
    share = size // out_ref.shape[0]
    entries = dot(weights, norm(pair, 0))
    entries = [entries[k * size : (k + 1) * size] for k in range(5)]
    mask = flat(mask_ref[...])
    left, right = (sigmoid(entries[k]) * entries[k + 1] * mask for k in (0, 2))
    gate_ref[...] = sigmoid(entries[4])
    for peer in range(out_ref.shape[0]):
        for row in range(rows):
            block = [side[peer * share : (peer + 1) * share, row * cols : (row + 1) * cols] for side in (left, right)]
            at = row * 2 * share
            out_ref[peer, at : at + 2 * share, :] = jnp.concatenate(block, axis=0).astype(BF16)


def weight_kernel(entry_ref, exit_ref, out_entry, out_exit, rows_ref):
    for t in range(entry_ref.shape[0]):
        for k in range(entry_ref.shape[1]):
            out_entry[t, k * LANES : (k + 1) * LANES, :] = jnp.transpose(entry_ref[t, k])
    width = 32
    step = spread(exit_ref[...].astype(F32).reshape(width, width, LANES), rows_ref)
    leave = jnp.concatenate([rows_ref[pl.ds(e, width, stride=step), :] for e in range(width)], axis=0)
    out_exit[...] = jnp.transpose(leave).astype(BF16)


def outer_kernel(
    got_ref, other_ref, couple_ref, exit_ref, weight_ref,
    out_ref, pair_ref, gate_ref, mask_ref,
    shared_ref, aux_ref, outer_ref,
):
    pairs, _, cols = got_ref.shape
    devices = 2 * pairs
    rows = couple_ref.shape[0]
    held, width = 2, 32
    core = lax.rem(lax.axis_index("dap"), 2)
    for side, ref in enumerate((got_ref, other_ref)):
        step = spread(ref[:, : held * width, :].astype(F32), shared_ref, side * pairs)
        aux = ref[:, held * width :, :].astype(F32)
        aux = jnp.where(core == 0, aux[:, :8], aux[:, 8:])
        aux_ref[side * pairs * 8 : (side + 1) * pairs * 8, :] = aux.reshape(pairs * 8, cols)
    lane = lax.broadcasted_iota(jnp.int32, (devices, LANES), 1)
    marks = []
    for row in range(0, 2 * held + 2, 2):
        low = aux_ref[pl.ds(row, devices, stride=8), :]
        high = aux_ref[pl.ds(row + 1, devices, stride=8), :]
        marks.append(jnp.where(lane < LANES // 2, pltpu.roll(low, LANES // 2, 1), high))
    cover = jnp.concatenate(marks[:held], axis=0).astype(BF16)
    flags = marks[held][0:1]
    chosen = lax.broadcasted_iota(jnp.int32, (rows, LANES), 1) == (
        lax.broadcasted_iota(jnp.int32, (rows, LANES), 0) + lax.axis_index("dap") * rows
    )
    cover_rows = dot(chosen.astype(BF16), cover, 1, 1).astype(BF16)
    scale = 1.0 / dot(cover_rows, cover)
    mask_ref[...] = jnp.sum(jnp.where(chosen, flags, 0.0), axis=1, keepdims=True) * flags
    per_tile = LANES // width
    tiles = []
    for tile in range(rows // per_tile):
        sides = [jnp.zeros((devices, LANES), F32) for _ in range(held)]
        for place in range(per_tile):
            values = aux_ref[pl.ds(tile * per_tile + place, devices, stride=8), :]
            here = (lane >= place * width) & (lane < (place + 1) * width)
            for s in range(held):
                turn = ((place - s) * width) % LANES
                moved = pltpu.roll(values, turn, 1) if turn else values
                sides[s] = jnp.where(here, moved, sides[s])
        tiles.append(jnp.concatenate(sides, axis=0))
    own = jnp.transpose(jnp.concatenate(tiles, axis=1)).astype(BF16)
    for e in range(0, width, 2):
        parts = []
        for more in range(2):
            parts.append(
                jnp.concatenate(
                    [
                        shared_ref[pl.ds(s * width + e + more, devices, stride=step), :]
                        for s in range(held)
                    ],
                    axis=0,
                )
            )
        result = dot(own, jnp.concatenate(parts, axis=1).astype(BF16)).astype(BF16)
        for more in range(2):
            for i in range(rows):
                outer_ref[(e + more) * width : (e + more + 1) * width, i * cols : (i + 1) * cols] = result[
                    i * width : (i + 1) * width, more * cols : (more + 1) * cols
                ]
    couple = jnp.concatenate([jnp.transpose(couple_ref[row]) for row in range(rows)], axis=1)
    pair = (couple.astype(F32) + dot(exit_ref[...], outer_ref[...]) * flat(scale)).astype(BF16)
    pair_ref[...] = pair
    project(pair.astype(F32), weight_ref[0], mask_ref, out_ref, gate_ref)


def side_rows(got_ref, sides_ref, part):
    lines = got_ref.shape[0] * got_ref.shape[1] // (2 * part)
    step = spread(got_ref[...].astype(F32).reshape(lines, 2 * part, got_ref.shape[2]), sides_ref)
    return lambda h: sides_ref[pl.ds(h, lines, stride=step), :].astype(BF16)


def outgoing_kernel(got_ref, out_ref, sides_ref, products_ref):
    cols = got_ref.shape[-1]
    part = products_ref.shape[0] // cols
    side = side_rows(got_ref, sides_ref, part)
    for h in range(part):
        products_ref[pl.ds(h, cols, stride=part), :] = dot(side(h), side(part + h), 1, 1)
    out_ref[...] = products_ref[...].astype(BF16).reshape(out_ref.shape)


def incoming_kernel(got_ref, out_ref, sides_ref):
    peers, size, cols = out_ref.shape
    rows = cols // peers
    part = size // rows
    side = side_rows(got_ref, sides_ref, part)
    for h in range(0, part, 2):
        results = [dot(side(at), side(part + at), 0, 0) for at in (h, h + 1)]
        for peer in range(peers):
            block = [result[peer * rows : (peer + 1) * rows] for result in results]
            out_ref[peer, h * rows : (h + 2) * rows, :] = jnp.concatenate(block, axis=0).astype(BF16)


def updated(products, pair_ref, gate_ref, leave):
    update = dot(jnp.transpose(leave), norm(jnp.concatenate(products, axis=1), 0))
    return pair_ref[...].astype(F32) + gate_ref[...] * update


def middle_kernel(got_ref, pair_ref, gate_ref, leave_ref, weight_ref, mask_ref, out_ref, next_ref, next_gate_ref):
    devices, size, cols = got_ref.shape
    part = size // mask_ref.shape[0]
    products = []
    for at in range(0, size, 2 * part):
        lines = got_ref[:, at : at + 2 * part, :].astype(F32)
        products += [values.reshape(devices * part, cols) for values in (lines[:, :part], lines[:, part:])]
    pair = updated(products, pair_ref, gate_ref, leave_ref[0]).astype(BF16)
    next_ref[...] = pair
    project(pair.astype(F32), weight_ref[1], mask_ref, out_ref, next_gate_ref)


def last_kernel(got_ref, pair_ref, gate_ref, leave_ref, out_hbm, out_ref, sums_ref, sems):
    rows, cols, channels = out_ref.shape
    senders = got_ref.shape[0] // 2
    sums = got_ref[:senders].astype(F32) + got_ref[senders:].astype(F32)
    sums_ref[...] = sums.reshape(sums_ref.shape)
    products = [sums_ref[pl.ds(row, channels, stride=rows), :] for row in range(rows)]
    pair = updated(products, pair_ref, gate_ref, leave_ref[1])
    copies = []
    for row in range(rows):
        out_ref[row] = jnp.transpose(pair[:, row * cols : (row + 1) * cols]).astype(BF16)
        if row % 4 == 3:
            part = pl.ds(row - 3, 4)
            copies.append(pltpu.make_async_copy(out_ref.at[part], out_hbm.at[part], sems.at[row // 4]))
            copies[-1].start()
    for copy in copies:
        copy.wait()


def call(kernel, inputs, outputs, scratch=(), in_specs=None, out_specs=None):
    return pl.pallas_call(
        kernel,
        out_shape=outputs,
        in_specs=in_specs or [VMEM] * len(inputs),
        out_specs=out_specs or [VMEM] * len(outputs),
        scratch_shapes=list(scratch),
        compiler_params=pltpu.CompilerParams(vmem_limit_bytes=40 * 1024 * 1024),
    )(*inputs)


def shape(dims, kind=BF16):
    return jax.ShapeDtypeStruct(dims, kind)


def fast(
    devices,
    homolog_embedding,
    coverage_indicator,
    genuine_amino_flag,
    couple_embedding,
    pairing_entry_matrices,
    pairing_exit_matrix,
    trilateral_entry_matrices,
    trilateral_exit_matrices,
):
    rows, cols, channels = couple_embedding.shape
    held = homolog_embedding.shape[0]
    width = pairing_entry_matrices.shape[2]
    part = channels // devices
    depth = homolog_embedding.shape[2]
    everything = jnp.concatenate(
        [
            homolog_embedding.reshape(held * cols, depth),
            jnp.transpose(pairing_entry_matrices, (1, 2, 0)).reshape(2 * width, depth),
        ],
        axis=0,
    )
    (entries,) = call(entry_kernel, (everything,), [shape((2 * width, held * cols), F32)])
    (packed,) = call(
        pack_kernel,
        (entries, coverage_indicator, genuine_amino_flag.reshape(1, cols)),
        [shape((devices // 2, held * width + 16, cols))],
    )
    packed, entry, exit_rows = lax.optimization_barrier((packed, trilateral_entry_matrices, pairing_exit_matrix))
    got = two_level(packed, devices)
    entry, exit_matrix = call(
        weight_kernel,
        (jnp.transpose(entry, (0, 2, 1, 3)), exit_rows),
        [
            shape((2, 5 * channels, channels)),
            shape((channels, width * width)),
        ],
        [pltpu.VMEM((width * (width + GAP), channels), F32)],
    )
    def projected(peers):
        return [
            shape((peers, devices * rows * 2 * part // peers, cols)),
            shape((channels, rows * cols)),
            shape((channels, rows * cols), F32),
        ]

    both, pair, gate, row_mask = call(
        outer_kernel,
        (*got, couple_embedding, exit_matrix, entry),
        projected(devices) + [shape((rows, cols), F32)],
        [
            pltpu.VMEM((devices * (held * width + GAP), cols), F32),
            pltpu.VMEM((devices * 8, cols), F32),
            pltpu.VMEM((width * width, rows * cols), BF16),
        ],
    )

    sides = pltpu.VMEM((devices * rows * (2 * part + GAP), cols), F32)
    (products,) = call(
        outgoing_kernel,
        (exchange(both),),
        [shape((devices, rows * part, cols))],
        [sides, pltpu.VMEM((devices * rows * part, cols), F32)],
    )
    both, pair, gate = call(
        middle_kernel,
        (exchange(products), pair, gate, trilateral_exit_matrices, entry, row_mask),
        projected(devices // 2),
    )
    groups = [list(range(begin, begin + devices // 2)) for begin in (0, devices // 2)]
    both = lax.all_to_all(both, "dap", split_axis=0, concat_axis=0, tiled=True, axis_index_groups=groups)
    (products,) = call(incoming_kernel, (both,), [shape((devices, rows * 2 * part, cols))], [sides])
    (pair_out,) = call(
        last_kernel,
        (exchange(products), pair, gate, trilateral_exit_matrices),
        [shape((rows, cols, channels))],
        [pltpu.VMEM((rows, cols, channels), BF16), pltpu.VMEM((channels * rows, cols), F32), pltpu.SemaphoreType.DMA((rows // 4,))],
        out_specs=[HBM],
    )
    return pair_out


def fits(devices, homolog_embedding, couple_embedding, pairing_entry_matrices):
    rows, cols, channels = couple_embedding.shape
    return (
        devices % 2 == 0
        and homolog_embedding.shape[0] == 2
        and rows == 8
        and cols == LANES
        and channels == 8 * devices
        and channels == LANES
        and pairing_entry_matrices.shape[2] == 32
        and homolog_embedding.shape[2] >= cols
    )


def solution(mesh):
    devices = mesh.shape["dap"]

    def one_device(*arrays):
        chosen = fast if fits(devices, arrays[0], arrays[3], arrays[4]) else local
        return chosen(devices, *arrays)

    return jax.shard_map(
        one_device,
        mesh=mesh,
        in_specs=(
            P(("crops", "dap"), None, None),
            P(("crops", "dap"), None),
            P("crops"),
            P(("crops", "dap"), None, None),
            P(),
            P(),
            P(),
            P(),
        ),
        out_specs=P(("crops", "dap"), None, None),
        check_vma=False,
    )
```

```python
import jax
import jax.numpy as jnp
from jax import lax
from jax.experimental import pallas as pl
from jax.experimental.pallas import tpu as pltpu
from jax.sharding import PartitionSpec as P

F32 = jnp.float32
BF16 = jnp.bfloat16
EPS = 1e-05
LANES = 128
GAP = 8
VMEM = pl.BlockSpec(memory_space=pltpu.VMEM)
HBM = pl.BlockSpec(memory_space=pltpu.HBM)


def dot(a, b, left=1, right=0):
    return lax.dot_general(a, b, (((left,), (right,)), ((), ())), preferred_element_type=F32)


def sigmoid(values, half_scale):
    return 0.5 * jnp.tanh(values * half_scale) + 0.5


def norm(values, axis):
    size = values.shape[axis]
    average = jnp.sum(values, axis=axis, keepdims=True) * (1.0 / size)
    centered = values - average
    variance = jnp.sum(centered * centered, axis=axis, keepdims=True) * (1.0 / size)
    return (centered * lax.rsqrt(variance + EPS)).astype(BF16)


def centre(values):
    size = values.shape[0]
    centered = values - jnp.sum(values, axis=0, keepdims=True) * (1.0 / size)
    variance = jnp.sum(centered * centered, axis=0, keepdims=True) * (1.0 / size)
    return centered.astype(BF16), lax.rsqrt(variance + EPS)


def standardize_features(values, axis):
    average = jnp.mean(values, axis=axis, keepdims=True)
    centered = values - average
    variance = jnp.mean(centered * centered, axis=axis, keepdims=True)
    return centered * lax.rsqrt(variance + 1e-05)


def exchange(blocks):
    return lax.all_to_all(blocks, "dap", split_axis=0, concat_axis=0, tiled=True)


def outer_update(left_local, mask_local, right_cols, mask_cols, couple_embedding, pairing_exit_matrix):
    proj_width = left_local.shape[1]
    local_rows = left_local.shape[2]
    col_total = right_cols.shape[2]
    outer = jnp.einsum("rzp,rej->pjze", left_local, right_cols, preferred_element_type=jnp.float32)
    outer = outer.astype(jnp.bfloat16).reshape(local_rows, col_total, proj_width * proj_width)
    pair_update = jnp.einsum("ijf,fc->ijc", outer, pairing_exit_matrix, preferred_element_type=jnp.float32)
    pair_count = jnp.einsum("si,sj->ij", mask_local, mask_cols, preferred_element_type=jnp.float32)
    return (couple_embedding.astype(jnp.float32) + pair_update / pair_count[:, :, None]).astype(jnp.bfloat16)


def triangle(pair_now, row_mask, weights, out_weight, incoming, devices):
    rows, cols, channels = pair_now.shape
    part = channels // devices
    normalized = standardize_features(pair_now.astype(jnp.float32), -1).astype(jnp.bfloat16)
    projections = jnp.einsum("ijc,ckh->khij", normalized, weights[:, :4], preferred_element_type=jnp.float32)
    left_proj = (jax.nn.sigmoid(projections[0]) * projections[1] * row_mask).astype(jnp.bfloat16)
    right_proj = (jax.nn.sigmoid(projections[2]) * projections[3] * row_mask).astype(jnp.bfloat16)
    gate_val = jax.nn.sigmoid(
        jnp.einsum("ijc,ch->ijh", normalized, weights[:, 4], preferred_element_type=jnp.float32)
    )
    both = jnp.stack(
        [left_proj.reshape(devices, part, rows, cols), right_proj.reshape(devices, part, rows, cols)], axis=1
    )
    both = exchange(both)
    both = jnp.transpose(both, (1, 2, 0, 3, 4)).reshape(2, part, devices * rows, cols)
    einsum_form = "hki,hkj->hij" if incoming else "hik,hjk->hij"
    products = jnp.einsum(einsum_form, both[0], both[1], preferred_element_type=jnp.float32).astype(jnp.bfloat16)
    products = jnp.transpose(products.reshape(part, devices, rows, cols), (1, 0, 2, 3))
    returned = exchange(products).reshape(channels, rows, cols)
    normed_products = standardize_features(returned.astype(jnp.float32), 0).astype(jnp.bfloat16)
    pair_update = jnp.einsum("hij,hc->ijc", normed_products, out_weight, preferred_element_type=jnp.float32)
    return (pair_now.astype(jnp.float32) + gate_val * pair_update).astype(jnp.bfloat16)


def local(
    devices,
    homolog_embedding,
    coverage_indicator,
    genuine_amino_flag,
    couple_embedding,
    pairing_entry_matrices,
    pairing_exit_matrix,
    trilateral_entry_matrices,
    trilateral_exit_matrices,
):
    rows, cols, _ = couple_embedding.shape
    held = homolog_embedding.shape[0]
    width = pairing_entry_matrices.shape[2]
    sequence_mask = coverage_indicator.astype(jnp.float32)
    msa_norm = standardize_features(homolog_embedding.astype(jnp.float32), -1).astype(jnp.bfloat16)
    entries = jnp.einsum("rgl,loe->roeg", msa_norm, pairing_entry_matrices, preferred_element_type=jnp.float32)
    entries = (entries * sequence_mask[:, None, None, :]).astype(jnp.bfloat16)
    own = jnp.transpose(entries[:, 0].reshape(held, width, devices, rows), (2, 0, 1, 3))
    shared = jnp.concatenate([entries[:, 1].reshape(held, width * cols), sequence_mask.astype(jnp.bfloat16)], axis=1)
    packed = jnp.concatenate(
        [jnp.broadcast_to(shared[None], (devices,) + shared.shape), own.reshape(devices, held, width * rows)], axis=2
    )
    packed = exchange(packed).reshape(devices * held, -1)
    right_cols = packed[:, : width * cols].reshape(-1, width, cols)
    mask_cols = packed[:, width * cols : (width + 1) * cols]
    left_local = packed[:, (width + 1) * cols :].reshape(-1, width, rows)
    first_row = lax.axis_index("dap") * rows
    mask_local = lax.dynamic_slice_in_dim(mask_cols, first_row, rows, 1)
    pair_one = outer_update(left_local, mask_local, right_cols, mask_cols, couple_embedding, pairing_exit_matrix)
    residues = genuine_amino_flag.astype(jnp.float32)
    row_mask = lax.dynamic_slice_in_dim(residues, first_row, rows, 0)[:, None] * residues[None, :]
    pair_two = triangle(
        pair_one, row_mask, trilateral_entry_matrices[0], trilateral_exit_matrices[0], False, devices
    )
    return triangle(pair_two, row_mask, trilateral_entry_matrices[1], trilateral_exit_matrices[1], True, devices)


def two_level(blocks, devices):
    groups = [list(range(parity, devices, 2)) for parity in range(2)]
    got = lax.all_to_all(blocks, "dap", split_axis=0, concat_axis=0, tiled=True, axis_index_groups=groups)
    return got, lax.ppermute(got, "dap", [(at, at ^ 1) for at in range(devices)])


def spread(blocks, target_ref, first=0):
    count, rows, _ = blocks.shape
    for at in range(count):
        begin = (first + at) * (rows + GAP)
        target_ref[begin : begin + rows, :] = blocks[at]
    return rows + GAP


def halves(row):
    return [pltpu.roll(row, LANES // 2, 1), row]


def entry_kernel(all_ref, out_ref):
    lines = all_ref.shape[0] - out_ref.shape[0]
    out_ref[...] = dot(all_ref[lines:], norm(all_ref[:lines].astype(F32), -1), 1, 1)


def pack_kernel(entries_ref, cover_ref, flag_ref, out_ref):
    pairs, _, cols = out_ref.shape
    held, width = 2, 32
    cover = cover_ref[...].astype(F32)
    flags = jnp.concatenate([cover, flag_ref[...].astype(F32)], axis=0)
    entries = entries_ref[...] * flat(cover)
    entries = [entries[:, s * cols : (s + 1) * cols] for s in range(held)]
    shared = jnp.concatenate([values[width:] for values in entries], axis=0).astype(BF16)
    blank = jnp.zeros((LANES - held * width, cols), F32)
    own = jnp.transpose(jnp.concatenate([values[:width] for values in entries] + [blank], axis=0))
    marks = []
    for row in range(held + 1):
        marks += halves(flags[row : row + 1])
    marks = jnp.concatenate(marks + [jnp.zeros((8 - len(marks), cols), F32)], axis=0)
    marks = jnp.concatenate([marks, marks], axis=0)
    lane = lax.broadcasted_iota(jnp.int32, (16, LANES), 1)
    for pair in range(pairs):
        out_ref[pair, : held * width, :] = shared
        block = jnp.where(lane < held * width, own[pair * 16 : pair * 16 + 16], marks)
        out_ref[pair, held * width :, :] = block.astype(BF16)


def flat(rows):
    return jnp.concatenate([rows[row : row + 1] for row in range(rows.shape[0])], axis=1)


def project(pair, weights, mask_ref, out_ref, gate_ref):
    size = pair.shape[0]
    rows, cols = mask_ref.shape
    share = size // out_ref.shape[0]
    centered, scale = centre(pair)
    entries = dot(weights, centered)
    entries = [entries[k * size : (k + 1) * size] for k in range(5)]
    half = 0.5 * scale
    mask = flat(mask_ref[...]) * scale
    left, right = (sigmoid(entries[k], half) * entries[k + 1] * mask for k in (0, 2))
    gate_ref[...] = sigmoid(entries[4], half)
    for peer in range(out_ref.shape[0]):
        for row in range(rows):
            block = [side[peer * share : (peer + 1) * share, row * cols : (row + 1) * cols] for side in (left, right)]
            at = row * 2 * share
            out_ref[peer, at : at + 2 * share, :] = jnp.concatenate(block, axis=0).astype(BF16)


def weight_kernel(entry_ref, exit_ref, out_entry, out_exit, rows_ref):
    for t in range(entry_ref.shape[0]):
        for k in range(entry_ref.shape[1]):
            out_entry[t, k * LANES : (k + 1) * LANES, :] = jnp.transpose(entry_ref[t, k])
    width = 32
    step = spread(exit_ref[...].astype(F32).reshape(width, width, LANES), rows_ref)
    leave = jnp.concatenate([rows_ref[pl.ds(e, width, stride=step), :] for e in range(width)], axis=0)
    out_exit[...] = jnp.transpose(leave).astype(BF16)


def outer_kernel(
    got_ref, other_ref, couple_ref, exit_ref, weight_ref,
    out_ref, pair_ref, gate_ref, mask_ref,
    shared_ref, aux_ref, outer_ref,
):
    pairs, _, cols = got_ref.shape
    devices = 2 * pairs
    rows = couple_ref.shape[0]
    held, width = 2, 32
    core = lax.rem(lax.axis_index("dap"), 2)
    for side, ref in enumerate((got_ref, other_ref)):
        step = spread(ref[:, : held * width, :].astype(F32), shared_ref, side * pairs)
        aux = ref[:, held * width :, :].astype(F32)
        aux = jnp.where(core == 0, aux[:, :8], aux[:, 8:])
        aux_ref[side * pairs * 8 : (side + 1) * pairs * 8, :] = aux.reshape(pairs * 8, cols)
    lane = lax.broadcasted_iota(jnp.int32, (devices, LANES), 1)
    marks = []
    for row in range(0, 2 * held + 2, 2):
        low = aux_ref[pl.ds(row, devices, stride=8), :]
        high = aux_ref[pl.ds(row + 1, devices, stride=8), :]
        marks.append(jnp.where(lane < LANES // 2, pltpu.roll(low, LANES // 2, 1), high))
    cover = jnp.concatenate(marks[:held], axis=0).astype(BF16)
    flags = marks[held][0:1]
    chosen = lax.broadcasted_iota(jnp.int32, (rows, LANES), 1) == (
        lax.broadcasted_iota(jnp.int32, (rows, LANES), 0) + lax.axis_index("dap") * rows
    )
    cover_rows = dot(chosen.astype(BF16), cover, 1, 1).astype(BF16)
    scale = 1.0 / dot(cover_rows, cover)
    mask_ref[...] = jnp.sum(jnp.where(chosen, flags, 0.0), axis=1, keepdims=True) * flags
    per_tile = LANES // width
    tiles = []
    for tile in range(rows // per_tile):
        sides = [jnp.zeros((devices, LANES), F32) for _ in range(held)]
        for place in range(per_tile):
            values = aux_ref[pl.ds(tile * per_tile + place, devices, stride=8), :]
            here = (lane >= place * width) & (lane < (place + 1) * width)
            for s in range(held):
                turn = ((place - s) * width) % LANES
                moved = pltpu.roll(values, turn, 1) if turn else values
                sides[s] = jnp.where(here, moved, sides[s])
        tiles.append(jnp.concatenate(sides, axis=0))
    own = jnp.transpose(jnp.concatenate(tiles, axis=1)).astype(BF16)
    for e in range(0, width, 2):
        parts = []
        for more in range(2):
            parts.append(
                jnp.concatenate(
                    [
                        shared_ref[pl.ds(s * width + e + more, devices, stride=step), :]
                        for s in range(held)
                    ],
                    axis=0,
                )
            )
        result = dot(own, jnp.concatenate(parts, axis=1).astype(BF16)).astype(BF16)
        for more in range(2):
            for i in range(rows):
                outer_ref[(e + more) * width : (e + more + 1) * width, i * cols : (i + 1) * cols] = result[
                    i * width : (i + 1) * width, more * cols : (more + 1) * cols
                ]
    couple = jnp.concatenate([jnp.transpose(couple_ref[row]) for row in range(rows)], axis=1)
    pair = (couple.astype(F32) + dot(exit_ref[...], outer_ref[...]) * flat(scale)).astype(BF16)
    pair_ref[...] = pair
    project(pair.astype(F32), weight_ref[0], mask_ref, out_ref, gate_ref)


def side_rows(got_ref, sides_ref, part):
    lines = got_ref.shape[0] * got_ref.shape[1] // (2 * part)
    step = spread(got_ref[...].astype(F32).reshape(lines, 2 * part, got_ref.shape[2]), sides_ref)
    return lambda h: sides_ref[pl.ds(h, lines, stride=step), :].astype(BF16)


def outgoing_kernel(got_ref, out_ref, sides_ref, products_ref):
    cols = got_ref.shape[-1]
    part = products_ref.shape[0] // cols
    side = side_rows(got_ref, sides_ref, part)
    for h in range(part):
        products_ref[pl.ds(h, cols, stride=part), :] = dot(side(h), side(part + h), 1, 1)
    out_ref[...] = products_ref[...].astype(BF16).reshape(out_ref.shape)


def incoming_kernel(got_ref, out_ref, sides_ref):
    peers, size, cols = out_ref.shape
    rows = cols // peers
    part = size // rows
    side = side_rows(got_ref, sides_ref, part)
    for h in range(0, part, 2):
        results = [dot(side(at), side(part + at), 0, 0) for at in (h, h + 1)]
        for peer in range(peers):
            block = [result[peer * rows : (peer + 1) * rows] for result in results]
            out_ref[peer, h * rows : (h + 2) * rows, :] = jnp.concatenate(block, axis=0).astype(BF16)


def updated(products, pair_ref, gate_ref, leave):
    centered, scale = centre(jnp.concatenate(products, axis=1))
    return pair_ref[...].astype(F32) + gate_ref[...] * scale * dot(jnp.transpose(leave), centered)


def middle_kernel(got_ref, pair_ref, gate_ref, leave_ref, weight_ref, mask_ref, out_ref, next_ref, next_gate_ref):
    devices, size, cols = got_ref.shape
    part = size // mask_ref.shape[0]
    products = []
    for at in range(0, size, 2 * part):
        lines = got_ref[:, at : at + 2 * part, :].astype(F32)
        products += [values.reshape(devices * part, cols) for values in (lines[:, :part], lines[:, part:])]
    pair = updated(products, pair_ref, gate_ref, leave_ref[0]).astype(BF16)
    next_ref[...] = pair
    project(pair.astype(F32), weight_ref[1], mask_ref, out_ref, next_gate_ref)


def last_kernel(got_ref, pair_ref, gate_ref, leave_ref, out_hbm, out_ref, sums_ref, sems):
    rows, cols, channels = out_ref.shape
    senders = got_ref.shape[0] // 2
    sums = got_ref[:senders].astype(F32) + got_ref[senders:].astype(F32)
    sums_ref[...] = sums.reshape(sums_ref.shape)
    products = [sums_ref[pl.ds(row, channels, stride=rows), :] for row in range(rows)]
    pair = updated(products, pair_ref, gate_ref, leave_ref[1])
    copies = []
    for row in range(rows):
        out_ref[row] = jnp.transpose(pair[:, row * cols : (row + 1) * cols]).astype(BF16)
        if row % 4 == 3:
            part = pl.ds(row - 3, 4)
            copies.append(pltpu.make_async_copy(out_ref.at[part], out_hbm.at[part], sems.at[row // 4]))
            copies[-1].start()
    for copy in copies:
        copy.wait()


def call(kernel, inputs, outputs, scratch=(), in_specs=None, out_specs=None):
    return pl.pallas_call(
        kernel,
        out_shape=outputs,
        in_specs=in_specs or [VMEM] * len(inputs),
        out_specs=out_specs or [VMEM] * len(outputs),
        scratch_shapes=list(scratch),
        compiler_params=pltpu.CompilerParams(vmem_limit_bytes=40 * 1024 * 1024),
    )(*inputs)


def shape(dims, kind=BF16):
    return jax.ShapeDtypeStruct(dims, kind)


def fast(
    devices,
    homolog_embedding,
    coverage_indicator,
    genuine_amino_flag,
    couple_embedding,
    pairing_entry_matrices,
    pairing_exit_matrix,
    trilateral_entry_matrices,
    trilateral_exit_matrices,
):
    rows, cols, channels = couple_embedding.shape
    held = homolog_embedding.shape[0]
    width = pairing_entry_matrices.shape[2]
    part = channels // devices
    depth = homolog_embedding.shape[2]
    everything = jnp.concatenate(
        [
            homolog_embedding.reshape(held * cols, depth),
            jnp.transpose(pairing_entry_matrices, (1, 2, 0)).reshape(2 * width, depth),
        ],
        axis=0,
    )
    (entries,) = call(entry_kernel, (everything,), [shape((2 * width, held * cols), F32)])
    (packed,) = call(
        pack_kernel,
        (entries, coverage_indicator, genuine_amino_flag.reshape(1, cols)),
        [shape((devices // 2, held * width + 16, cols))],
    )
    packed, entry, exit_rows = lax.optimization_barrier((packed, trilateral_entry_matrices, pairing_exit_matrix))
    got = two_level(packed, devices)
    entry, exit_matrix = call(
        weight_kernel,
        (jnp.transpose(entry, (0, 2, 1, 3)), exit_rows),
        [
            shape((2, 5 * channels, channels)),
            shape((channels, width * width)),
        ],
        [pltpu.VMEM((width * (width + GAP), channels), F32)],
    )
    def projected(peers):
        return [
            shape((peers, devices * rows * 2 * part // peers, cols)),
            shape((channels, rows * cols)),
            shape((channels, rows * cols), F32),
        ]

    both, pair, gate, row_mask = call(
        outer_kernel,
        (*got, couple_embedding, exit_matrix, entry),
        projected(devices) + [shape((rows, cols), F32)],
        [
            pltpu.VMEM((devices * (held * width + GAP), cols), F32),
            pltpu.VMEM((devices * 8, cols), F32),
            pltpu.VMEM((width * width, rows * cols), BF16),
        ],
    )

    sides = pltpu.VMEM((devices * rows * (2 * part + GAP), cols), F32)
    (products,) = call(
        outgoing_kernel,
        (exchange(both),),
        [shape((devices, rows * part, cols))],
        [sides, pltpu.VMEM((devices * rows * part, cols), F32)],
    )
    both, pair, gate = call(
        middle_kernel,
        (exchange(products), pair, gate, trilateral_exit_matrices, entry, row_mask),
        projected(devices // 2),
    )
    groups = [list(range(begin, begin + devices // 2)) for begin in (0, devices // 2)]
    both = lax.all_to_all(both, "dap", split_axis=0, concat_axis=0, tiled=True, axis_index_groups=groups)
    (products,) = call(incoming_kernel, (both,), [shape((devices, rows * 2 * part, cols))], [sides])
    (pair_out,) = call(
        last_kernel,
        (exchange(products), pair, gate, trilateral_exit_matrices),
        [shape((rows, cols, channels))],
        [pltpu.VMEM((rows, cols, channels), BF16), pltpu.VMEM((channels * rows, cols), F32), pltpu.SemaphoreType.DMA((rows // 4,))],
        out_specs=[HBM],
    )
    return pair_out


def fits(devices, homolog_embedding, couple_embedding, pairing_entry_matrices):
    rows, cols, channels = couple_embedding.shape
    return (
        devices % 2 == 0
        and homolog_embedding.shape[0] == 2
        and rows == 8
        and cols == LANES
        and channels == 8 * devices
        and channels == LANES
        and pairing_entry_matrices.shape[2] == 32
        and homolog_embedding.shape[2] >= cols
    )


def solution(mesh):
    devices = mesh.shape["dap"]

    def one_device(*arrays):
        chosen = fast if fits(devices, arrays[0], arrays[3], arrays[4]) else local
        return chosen(devices, *arrays)

    return jax.shard_map(
        one_device,
        mesh=mesh,
        in_specs=(
            P(("crops", "dap"), None, None),
            P(("crops", "dap"), None),
            P("crops"),
            P(("crops", "dap"), None, None),
            P(),
            P(),
            P(),
            P(),
        ),
        out_specs=P(("crops", "dap"), None, None),
        check_vma=False,
    )
```

```python
import jax
import jax.numpy as jnp
from jax import lax
from jax.experimental import pallas as pl
from jax.experimental.pallas import tpu as pltpu
from jax.sharding import PartitionSpec as P

F32 = jnp.float32
BF16 = jnp.bfloat16
EPS = 1e-05
LANES = 128
GAP = 8
VMEM = pl.BlockSpec(memory_space=pltpu.VMEM)
HBM = pl.BlockSpec(memory_space=pltpu.HBM)


def dot(a, b, left=1, right=0):
    return lax.dot_general(a, b, (((left,), (right,)), ((), ())), preferred_element_type=F32)


def sigmoid(values, half_scale):
    return 0.5 * jnp.tanh(values * half_scale) + 0.5


def norm(values, axis):
    size = values.shape[axis]
    average = jnp.sum(values, axis=axis, keepdims=True) * (1.0 / size)
    centered = values - average
    variance = jnp.sum(centered * centered, axis=axis, keepdims=True) * (1.0 / size)
    return (centered * lax.rsqrt(variance + EPS)).astype(BF16)


def centre(values):
    size = values.shape[0]
    centered = values - jnp.sum(values, axis=0, keepdims=True) * (1.0 / size)
    variance = jnp.sum(centered * centered, axis=0, keepdims=True) * (1.0 / size)
    return centered.astype(BF16), lax.rsqrt(variance + EPS)


def standardize_features(values, axis):
    average = jnp.mean(values, axis=axis, keepdims=True)
    centered = values - average
    variance = jnp.mean(centered * centered, axis=axis, keepdims=True)
    return centered * lax.rsqrt(variance + 1e-05)


def exchange(blocks):
    return lax.all_to_all(blocks, "dap", split_axis=0, concat_axis=0, tiled=True)


def outer_update(left_local, mask_local, right_cols, mask_cols, couple_embedding, pairing_exit_matrix):
    proj_width = left_local.shape[1]
    local_rows = left_local.shape[2]
    col_total = right_cols.shape[2]
    outer = jnp.einsum("rzp,rej->pjze", left_local, right_cols, preferred_element_type=jnp.float32)
    outer = outer.astype(jnp.bfloat16).reshape(local_rows, col_total, proj_width * proj_width)
    pair_update = jnp.einsum("ijf,fc->ijc", outer, pairing_exit_matrix, preferred_element_type=jnp.float32)
    pair_count = jnp.einsum("si,sj->ij", mask_local, mask_cols, preferred_element_type=jnp.float32)
    return (couple_embedding.astype(jnp.float32) + pair_update / pair_count[:, :, None]).astype(jnp.bfloat16)


def triangle(pair_now, row_mask, weights, out_weight, incoming, devices):
    rows, cols, channels = pair_now.shape
    part = channels // devices
    normalized = standardize_features(pair_now.astype(jnp.float32), -1).astype(jnp.bfloat16)
    projections = jnp.einsum("ijc,ckh->khij", normalized, weights[:, :4], preferred_element_type=jnp.float32)
    left_proj = (jax.nn.sigmoid(projections[0]) * projections[1] * row_mask).astype(jnp.bfloat16)
    right_proj = (jax.nn.sigmoid(projections[2]) * projections[3] * row_mask).astype(jnp.bfloat16)
    gate_val = jax.nn.sigmoid(
        jnp.einsum("ijc,ch->ijh", normalized, weights[:, 4], preferred_element_type=jnp.float32)
    )
    both = jnp.stack(
        [left_proj.reshape(devices, part, rows, cols), right_proj.reshape(devices, part, rows, cols)], axis=1
    )
    both = exchange(both)
    both = jnp.transpose(both, (1, 2, 0, 3, 4)).reshape(2, part, devices * rows, cols)
    einsum_form = "hki,hkj->hij" if incoming else "hik,hjk->hij"
    products = jnp.einsum(einsum_form, both[0], both[1], preferred_element_type=jnp.float32).astype(jnp.bfloat16)
    products = jnp.transpose(products.reshape(part, devices, rows, cols), (1, 0, 2, 3))
    returned = exchange(products).reshape(channels, rows, cols)
    normed_products = standardize_features(returned.astype(jnp.float32), 0).astype(jnp.bfloat16)
    pair_update = jnp.einsum("hij,hc->ijc", normed_products, out_weight, preferred_element_type=jnp.float32)
    return (pair_now.astype(jnp.float32) + gate_val * pair_update).astype(jnp.bfloat16)


def local(
    devices,
    homolog_embedding,
    coverage_indicator,
    genuine_amino_flag,
    couple_embedding,
    pairing_entry_matrices,
    pairing_exit_matrix,
    trilateral_entry_matrices,
    trilateral_exit_matrices,
):
    rows, cols, _ = couple_embedding.shape
    held = homolog_embedding.shape[0]
    width = pairing_entry_matrices.shape[2]
    sequence_mask = coverage_indicator.astype(jnp.float32)
    msa_norm = standardize_features(homolog_embedding.astype(jnp.float32), -1).astype(jnp.bfloat16)
    entries = jnp.einsum("rgl,loe->roeg", msa_norm, pairing_entry_matrices, preferred_element_type=jnp.float32)
    entries = (entries * sequence_mask[:, None, None, :]).astype(jnp.bfloat16)
    own = jnp.transpose(entries[:, 0].reshape(held, width, devices, rows), (2, 0, 1, 3))
    shared = jnp.concatenate([entries[:, 1].reshape(held, width * cols), sequence_mask.astype(jnp.bfloat16)], axis=1)
    packed = jnp.concatenate(
        [jnp.broadcast_to(shared[None], (devices,) + shared.shape), own.reshape(devices, held, width * rows)], axis=2
    )
    packed = exchange(packed).reshape(devices * held, -1)
    right_cols = packed[:, : width * cols].reshape(-1, width, cols)
    mask_cols = packed[:, width * cols : (width + 1) * cols]
    left_local = packed[:, (width + 1) * cols :].reshape(-1, width, rows)
    first_row = lax.axis_index("dap") * rows
    mask_local = lax.dynamic_slice_in_dim(mask_cols, first_row, rows, 1)
    pair_one = outer_update(left_local, mask_local, right_cols, mask_cols, couple_embedding, pairing_exit_matrix)
    residues = genuine_amino_flag.astype(jnp.float32)
    row_mask = lax.dynamic_slice_in_dim(residues, first_row, rows, 0)[:, None] * residues[None, :]
    pair_two = triangle(
        pair_one, row_mask, trilateral_entry_matrices[0], trilateral_exit_matrices[0], False, devices
    )
    return triangle(pair_two, row_mask, trilateral_entry_matrices[1], trilateral_exit_matrices[1], True, devices)


def two_level(blocks, devices):
    groups = [list(range(parity, devices, 2)) for parity in range(2)]
    got = lax.all_to_all(blocks, "dap", split_axis=0, concat_axis=0, tiled=True, axis_index_groups=groups)
    return got, lax.ppermute(got, "dap", [(at, at ^ 1) for at in range(devices)])


def spread(blocks, target_ref, first=0):
    count, rows, _ = blocks.shape
    for at in range(count):
        begin = (first + at) * (rows + GAP)
        target_ref[begin : begin + rows, :] = blocks[at]
    return rows + GAP


def halves(row):
    return [pltpu.roll(row, LANES // 2, 1), row]


def entry_kernel(all_ref, out_ref):
    lines = all_ref.shape[0] - out_ref.shape[0]
    out_ref[...] = dot(all_ref[lines:], norm(all_ref[:lines].astype(F32), -1), 1, 1)


def pack_kernel(entries_ref, cover_ref, flag_ref, out_ref):
    pairs, _, cols = out_ref.shape
    held, width = 2, 32
    cover = cover_ref[...].astype(F32)
    flags = jnp.concatenate([cover, flag_ref[...].astype(F32)], axis=0)
    entries = entries_ref[...] * flat(cover)
    entries = [entries[:, s * cols : (s + 1) * cols] for s in range(held)]
    shared = jnp.concatenate([values[width:] for values in entries], axis=0).astype(BF16)
    blank = jnp.zeros((LANES - held * width, cols), F32)
    own = jnp.transpose(jnp.concatenate([values[:width] for values in entries] + [blank], axis=0))
    marks = []
    for row in range(held + 1):
        marks += halves(flags[row : row + 1])
    marks = jnp.concatenate(marks + [jnp.zeros((8 - len(marks), cols), F32)], axis=0)
    marks = jnp.concatenate([marks, marks], axis=0)
    lane = lax.broadcasted_iota(jnp.int32, (16, LANES), 1)
    for pair in range(pairs):
        out_ref[pair, : held * width, :] = shared
        block = jnp.where(lane < held * width, own[pair * 16 : pair * 16 + 16], marks)
        out_ref[pair, held * width :, :] = block.astype(BF16)


def flat(rows):
    return jnp.concatenate([rows[row : row + 1] for row in range(rows.shape[0])], axis=1)


def project(pair, weights, mask_ref, out_ref, gate_ref):
    size = pair.shape[0]
    rows, cols = mask_ref.shape
    share = size // out_ref.shape[0]
    centered, scale = centre(pair)
    entries = dot(weights, centered)
    entries = [entries[k * size : (k + 1) * size] for k in range(5)]
    half = 0.5 * scale
    mask = flat(mask_ref[...]) * scale
    left, right = (sigmoid(entries[k], half) * entries[k + 1] * mask for k in (0, 2))
    gate_ref[...] = sigmoid(entries[4], half)
    for peer in range(out_ref.shape[0]):
        for row in range(rows):
            block = [side[peer * share : (peer + 1) * share, row * cols : (row + 1) * cols] for side in (left, right)]
            at = row * 2 * share
            out_ref[peer, at : at + 2 * share, :] = jnp.concatenate(block, axis=0).astype(BF16)


def weight_kernel(entry_ref, exit_ref, couple_ref, out_entry, out_exit, out_couple, rows_ref):
    for t in range(entry_ref.shape[0]):
        for k in range(entry_ref.shape[1]):
            out_entry[t, k * LANES : (k + 1) * LANES, :] = jnp.transpose(entry_ref[t, k])
    width = 32
    step = spread(exit_ref[...].astype(F32).reshape(width, width, LANES), rows_ref)
    leave = jnp.concatenate([rows_ref[pl.ds(e, width, stride=step), :] for e in range(width)], axis=0)
    out_exit[...] = jnp.transpose(leave).astype(BF16)
    for row in range(couple_ref.shape[0]):
        out_couple[:, row * LANES : (row + 1) * LANES] = jnp.transpose(couple_ref[row])


def outer_kernel(
    got_ref, other_ref, couple_ref, exit_ref, weight_ref,
    out_ref, pair_ref, gate_ref, mask_ref,
    shared_ref, aux_ref, outer_ref,
):
    pairs, _, cols = got_ref.shape
    devices = 2 * pairs
    rows = couple_ref.shape[1] // cols
    held, width = 2, 32
    core = lax.rem(lax.axis_index("dap"), 2)
    for side, ref in enumerate((got_ref, other_ref)):
        step = spread(ref[:, : held * width, :].astype(F32), shared_ref, side * pairs)
        aux = ref[:, held * width :, :].astype(F32)
        aux = jnp.where(core == 0, aux[:, :8], aux[:, 8:])
        aux_ref[side * pairs * 8 : (side + 1) * pairs * 8, :] = aux.reshape(pairs * 8, cols)
    lane = lax.broadcasted_iota(jnp.int32, (devices, LANES), 1)
    marks = []
    for row in range(0, 2 * held + 2, 2):
        low = aux_ref[pl.ds(row, devices, stride=8), :]
        high = aux_ref[pl.ds(row + 1, devices, stride=8), :]
        marks.append(jnp.where(lane < LANES // 2, pltpu.roll(low, LANES // 2, 1), high))
    cover = jnp.concatenate(marks[:held], axis=0).astype(BF16)
    flags = marks[held][0:1]
    chosen = lax.broadcasted_iota(jnp.int32, (rows, LANES), 1) == (
        lax.broadcasted_iota(jnp.int32, (rows, LANES), 0) + lax.axis_index("dap") * rows
    )
    cover_rows = dot(chosen.astype(BF16), cover, 1, 1).astype(BF16)
    scale = 1.0 / dot(cover_rows, cover)
    mask_ref[...] = jnp.sum(jnp.where(chosen, flags, 0.0), axis=1, keepdims=True) * flags
    per_tile = LANES // width
    tiles = []
    for tile in range(rows // per_tile):
        sides = [jnp.zeros((devices, LANES), F32) for _ in range(held)]
        for place in range(per_tile):
            values = aux_ref[pl.ds(tile * per_tile + place, devices, stride=8), :]
            here = (lane >= place * width) & (lane < (place + 1) * width)
            for s in range(held):
                turn = ((place - s) * width) % LANES
                moved = pltpu.roll(values, turn, 1) if turn else values
                sides[s] = jnp.where(here, moved, sides[s])
        tiles.append(jnp.concatenate(sides, axis=0))
    own = jnp.transpose(jnp.concatenate(tiles, axis=1)).astype(BF16)
    for e in range(0, width, 2):
        parts = []
        for more in range(2):
            parts.append(
                jnp.concatenate(
                    [
                        shared_ref[pl.ds(s * width + e + more, devices, stride=step), :]
                        for s in range(held)
                    ],
                    axis=0,
                )
            )
        result = dot(own, jnp.concatenate(parts, axis=1).astype(BF16)).astype(BF16)
        for more in range(2):
            for i in range(rows):
                outer_ref[(e + more) * width : (e + more + 1) * width, i * cols : (i + 1) * cols] = result[
                    i * width : (i + 1) * width, more * cols : (more + 1) * cols
                ]
    pair = (couple_ref[...].astype(F32) + dot(exit_ref[...], outer_ref[...]) * flat(scale)).astype(BF16)
    pair_ref[...] = pair
    project(pair.astype(F32), weight_ref[0], mask_ref, out_ref, gate_ref)


def side_rows(got_ref, sides_ref, part):
    lines = got_ref.shape[0] * got_ref.shape[1] // (2 * part)
    step = spread(got_ref[...].astype(F32).reshape(lines, 2 * part, got_ref.shape[2]), sides_ref)
    return lambda h: sides_ref[pl.ds(h, lines, stride=step), :].astype(BF16)


def outgoing_kernel(got_ref, out_ref, sides_ref, products_ref):
    cols = got_ref.shape[-1]
    part = products_ref.shape[0] // cols
    side = side_rows(got_ref, sides_ref, part)
    for h in range(part):
        products_ref[pl.ds(h, cols, stride=part), :] = dot(side(h), side(part + h), 1, 1)
    out_ref[...] = products_ref[...].astype(BF16).reshape(out_ref.shape)


def incoming_kernel(got_ref, out_ref, sides_ref):
    peers, size, cols = out_ref.shape
    rows = cols // peers
    part = size // rows
    side = side_rows(got_ref, sides_ref, part)
    for h in range(0, part, 2):
        results = [dot(side(at), side(part + at), 0, 0) for at in (h, h + 1)]
        for peer in range(peers):
            block = [result[peer * rows : (peer + 1) * rows] for result in results]
            out_ref[peer, h * rows : (h + 2) * rows, :] = jnp.concatenate(block, axis=0).astype(BF16)


def updated(products, pair_ref, gate_ref, leave):
    centered, scale = centre(jnp.concatenate(products, axis=1))
    return pair_ref[...].astype(F32) + gate_ref[...] * scale * dot(jnp.transpose(leave), centered)


def middle_kernel(got_ref, pair_ref, gate_ref, leave_ref, weight_ref, mask_ref, out_ref, next_ref, next_gate_ref):
    devices, size, cols = got_ref.shape
    part = size // mask_ref.shape[0]
    products = []
    for at in range(0, size, 2 * part):
        lines = got_ref[:, at : at + 2 * part, :].astype(F32)
        products += [values.reshape(devices * part, cols) for values in (lines[:, :part], lines[:, part:])]
    pair = updated(products, pair_ref, gate_ref, leave_ref[0]).astype(BF16)
    next_ref[...] = pair
    project(pair.astype(F32), weight_ref[1], mask_ref, out_ref, next_gate_ref)


def last_kernel(got_ref, pair_ref, gate_ref, leave_ref, out_hbm, out_ref, sums_ref, sems):
    rows, cols, channels = out_ref.shape
    senders = got_ref.shape[0] // 2
    sums = got_ref[:senders].astype(F32) + got_ref[senders:].astype(F32)
    sums_ref[...] = sums.reshape(sums_ref.shape)
    products = [sums_ref[pl.ds(row, channels, stride=rows), :] for row in range(rows)]
    pair = updated(products, pair_ref, gate_ref, leave_ref[1])
    copies = []
    for row in range(rows):
        out_ref[row] = jnp.transpose(pair[:, row * cols : (row + 1) * cols]).astype(BF16)
        if row % 4 == 3:
            part = pl.ds(row - 3, 4)
            copies.append(pltpu.make_async_copy(out_ref.at[part], out_hbm.at[part], sems.at[row // 4]))
            copies[-1].start()
    for copy in copies:
        copy.wait()


def call(kernel, inputs, outputs, scratch=(), in_specs=None, out_specs=None):
    return pl.pallas_call(
        kernel,
        out_shape=outputs,
        in_specs=in_specs or [VMEM] * len(inputs),
        out_specs=out_specs or [VMEM] * len(outputs),
        scratch_shapes=list(scratch),
        compiler_params=pltpu.CompilerParams(vmem_limit_bytes=40 * 1024 * 1024),
    )(*inputs)


def shape(dims, kind=BF16):
    return jax.ShapeDtypeStruct(dims, kind)


def fast(
    devices,
    homolog_embedding,
    coverage_indicator,
    genuine_amino_flag,
    couple_embedding,
    pairing_entry_matrices,
    pairing_exit_matrix,
    trilateral_entry_matrices,
    trilateral_exit_matrices,
):
    rows, cols, channels = couple_embedding.shape
    held = homolog_embedding.shape[0]
    width = pairing_entry_matrices.shape[2]
    part = channels // devices
    depth = homolog_embedding.shape[2]
    everything = jnp.concatenate(
        [
            homolog_embedding.reshape(held * cols, depth),
            jnp.transpose(pairing_entry_matrices, (1, 2, 0)).reshape(2 * width, depth),
        ],
        axis=0,
    )
    (entries,) = call(entry_kernel, (everything,), [shape((2 * width, held * cols), F32)])
    (packed,) = call(
        pack_kernel,
        (entries, coverage_indicator, genuine_amino_flag.reshape(1, cols)),
        [shape((devices // 2, held * width + 16, cols))],
    )
    packed, entry, exit_rows, couple_rows = lax.optimization_barrier(
        (packed, trilateral_entry_matrices, pairing_exit_matrix, couple_embedding)
    )
    got = two_level(packed, devices)
    entry, exit_matrix, couple = call(
        weight_kernel,
        (jnp.transpose(entry, (0, 2, 1, 3)), exit_rows, couple_rows),
        [
            shape((2, 5 * channels, channels)),
            shape((channels, width * width)),
            shape((channels, rows * cols)),
        ],
        [pltpu.VMEM((width * (width + GAP), channels), F32)],
    )
    def projected(peers):
        return [
            shape((peers, devices * rows * 2 * part // peers, cols)),
            shape((channels, rows * cols)),
            shape((channels, rows * cols), F32),
        ]

    both, pair, gate, row_mask = call(
        outer_kernel,
        (*got, couple, exit_matrix, entry),
        projected(devices) + [shape((rows, cols), F32)],
        [
            pltpu.VMEM((devices * (held * width + GAP), cols), F32),
            pltpu.VMEM((devices * 8, cols), F32),
            pltpu.VMEM((width * width, rows * cols), BF16),
        ],
    )

    sides = pltpu.VMEM((devices * rows * (2 * part + GAP), cols), F32)
    (products,) = call(
        outgoing_kernel,
        (exchange(both),),
        [shape((devices, rows * part, cols))],
        [sides, pltpu.VMEM((devices * rows * part, cols), F32)],
    )
    both, pair, gate = call(
        middle_kernel,
        (exchange(products), pair, gate, trilateral_exit_matrices, entry, row_mask),
        projected(devices // 2),
    )
    groups = [list(range(begin, begin + devices // 2)) for begin in (0, devices // 2)]
    both = lax.all_to_all(both, "dap", split_axis=0, concat_axis=0, tiled=True, axis_index_groups=groups)
    (products,) = call(incoming_kernel, (both,), [shape((devices, rows * 2 * part, cols))], [sides])
    (pair_out,) = call(
        last_kernel,
        (exchange(products), pair, gate, trilateral_exit_matrices),
        [shape((rows, cols, channels))],
        [pltpu.VMEM((rows, cols, channels), BF16), pltpu.VMEM((channels * rows, cols), F32), pltpu.SemaphoreType.DMA((rows // 4,))],
        out_specs=[HBM],
    )
    return pair_out


def fits(devices, homolog_embedding, couple_embedding, pairing_entry_matrices):
    rows, cols, channels = couple_embedding.shape
    return (
        devices % 2 == 0
        and homolog_embedding.shape[0] == 2
        and rows == 8
        and cols == LANES
        and channels == 8 * devices
        and channels == LANES
        and pairing_entry_matrices.shape[2] == 32
        and homolog_embedding.shape[2] >= cols
    )


def solution(mesh):
    devices = mesh.shape["dap"]

    def one_device(*arrays):
        chosen = fast if fits(devices, arrays[0], arrays[3], arrays[4]) else local
        return chosen(devices, *arrays)

    return jax.shard_map(
        one_device,
        mesh=mesh,
        in_specs=(
            P(("crops", "dap"), None, None),
            P(("crops", "dap"), None),
            P("crops"),
            P(("crops", "dap"), None, None),
            P(),
            P(),
            P(),
            P(),
        ),
        out_specs=P(("crops", "dap"), None, None),
        check_vma=False,
    )
```
